128 devices in a mesh: focus: 2 (over x_lo), gx: 4 (over x_hi, core), gy: 16 (over y, z).
Axes of the slice: x: 4 (x_hi: 2, x_lo: 2; x = x_hi * 2 + x_lo), y: 4, z: 4, core: 2. Of those that a mesh axis runs over, the one named last changes fastest.
Arguments:
- level_set: float32 [4096, 8192], P('gx', 'gy'), may hold values from -12 to 12
- focus_grads: float32 [4, 4096, 8192], P('focus', 'gx', 'gy'), may hold values from -6 to 6
- focus_weight: float32 [4], P('focus'), may hold values from 0.3 to 3
Outputs:
- level_out: float32 [4096, 8192], P('gx', 'gy')
- velocity: float32 [4096, 8192], P('gx', 'gy')
The draws below stay inside these ranges and needn't reach their ends.
All inputs are finite; a program needn't handle non-finite values. Where the reference program divides by a largest or mean magnitude, that divisor is 1e-20 or more.
Results may differ from the reference program's by a relative error of at most 0.00002.
Values sent between devices are 32-bit elements; how exact they have to be, the bound alone decides.
No kernel may reach another device: no remote copies, remote signals or barrier semaphores. Data moves between devices by JAX's collectives and lax.ppermute only.
A program may use at most 128 MiB of HBM per device.

```python
import math
import jax
import jax.numpy as jnp
from jax import lax

EXT_SWEEPS = 8
REINIT_ITERS = 10
FOCUS = 4
NX = 4096
NY = 8192


def level_of(stream_key, dims, pieces, least, high):
    gain, own = 1.0, jax.random.fold_in(stream_key, 6)
    for position, parts in pieces:
        steps = jnp.exp(jax.random.uniform(jax.random.fold_in(own, position), (parts,), jnp.float32, least / len(pieces), high / len(pieces)))
        gain = gain * jnp.repeat(steps, dims[position] // parts).reshape([-1 if axis == position else 1 for axis in range(len(dims))])
    return gain


def centred(own_key, extent, deviation, bound, pieces=(), held_as=jnp.bfloat16):
    array = jax.random.normal(own_key, extent, jnp.float32) * deviation
    if len(pieces) > 0:
        array = level_of(own_key, extent, pieces, -0.22, 0.18) * array
    return jnp.clip(array, min=-bound, max=bound).astype(held_as)


def setup_inputs(seed: int = 0) -> dict:
    arg_keys = jax.random.split(jax.random.key(seed), 4)
    level_set = centred(arg_keys[0], (NX, NY), 2.0, 12.0, ((0, 4), (1, 16)), jnp.float32)
    focus_grads = centred(arg_keys[1], (FOCUS, NX, NY), 1.0, 6.0, ((0, 2), (1, 4), (2, 16)), jnp.float32)
    focus_weight = jnp.clip(jnp.exp(math.log(3.0) - 2.3025851 * jax.random.uniform(arg_keys[2], (FOCUS,), jnp.float32) ** level_of(arg_keys[2], (FOCUS,), ((0, 2),), -0.2, 0.2)), 0.3, 3.0)
    return {"level_set": level_set, "focus_grads": focus_grads, "focus_weight": focus_weight}


band_cells = 3.0
cfl_number = 0.5
pseudo_step = 0.5

def wrap_pad(field, width):
    return jnp.pad(field, width, mode='wrap')

def jacobi(padded, source, band):
    beside = padded[2:, 1:-1] + padded[:-2, 1:-1] + padded[1:-1, 2:] + padded[1:-1, :-2]
    return (band * source + beside) / (band + 4.0)

def hamiltonian(padded, speed):
    center = padded[1:-1, 1:-1]
    dxm = center - padded[:-2, 1:-1]
    dxp = padded[2:, 1:-1] - center
    dym = center - padded[1:-1, :-2]
    dyp = padded[1:-1, 2:] - center
    gplus = jnp.sqrt(jnp.maximum(dxm, 0.0) ** 2 + jnp.minimum(dxp, 0.0) ** 2 + jnp.maximum(dym, 0.0) ** 2 + jnp.minimum(dyp, 0.0) ** 2)
    gminus = jnp.sqrt(jnp.minimum(dxm, 0.0) ** 2 + jnp.maximum(dxp, 0.0) ** 2 + jnp.minimum(dym, 0.0) ** 2 + jnp.maximum(dyp, 0.0) ** 2)
    return jnp.maximum(speed, 0.0) * gplus + jnp.minimum(speed, 0.0) * gminus

def reference(level_set, focus_grads, focus_weight):
    source = lax.optimization_barrier(jnp.sum(focus_weight[:, None, None] * focus_grads, axis=0))
    band = 1.0 / (1.0 + (level_set / band_cells) ** 2)
    velocity = source
    for sweep in range(EXT_SWEEPS):
        velocity = jacobi(wrap_pad(velocity, 1), source, band)
    top = jnp.max(jnp.abs(velocity))
    step = cfl_number / (top + 1e-06)
    advanced = level_set - step * hamiltonian(wrap_pad(level_set, 1), velocity)
    sign = advanced / jnp.sqrt(advanced * advanced + 1.0)
    level_out = advanced
    for sweep in range(REINIT_ITERS):
        level_out = level_out - pseudo_step * (hamiltonian(wrap_pad(level_out, 1), sign) - sign)
    return (level_out, velocity)
```

```python
import functools

import jax
import jax.numpy as jnp
from jax import lax
from jax.experimental import pallas as pl
from jax.experimental.pallas import tpu as pltpu
from jax.sharding import PartitionSpec as P

EXT_SWEEPS = 8
REINIT_ITERS = 10
band_cells = 3.0
cfl_number = 0.5
pseudo_step = 0.5

HALO = 24
LANES = 128
TINY = 1e-18

VMEM = pl.BlockSpec(memory_space=pltpu.VMEM)
SMEM = pl.BlockSpec(memory_space=pltpu.SMEM)
ANY = pl.BlockSpec(memory_space=pl.ANY)


def call(body, out_shapes, in_specs, scratch=(), name=None, flops=0, out_specs=None, aliases=None):
    outs = [jax.ShapeDtypeStruct(s, jnp.float32) for s in out_shapes]
    return pl.pallas_call(
        body,
        out_shape=outs,
        in_specs=in_specs,
        out_specs=out_specs or [VMEM] * len(outs),
        scratch_shapes=list(scratch),
        name=name,
        input_output_aliases=aliases or {},
        compiler_params=pltpu.CompilerParams(vmem_limit_bytes=50 << 20),
        cost_estimate=pl.CostEstimate(flops=flops, bytes_accessed=1 << 20, transcendentals=0),
    )


def aligned(x, n=8):
    return pl.multiple_of(x, n)


def send_part(f_ref, w_ref, g_ref, send_ref, buf, sems):
    rows = send_ref.shape[0]
    start = aligned((1 - f_ref[0]) * (g_ref.shape[1] - rows))
    chunks = sems.shape[0]
    step = rows // 8 // chunks * 8
    spans = [(i * step, step if i < chunks - 1 else rows - i * step) for i in range(chunks)]
    copies = [
        pltpu.make_async_copy(
            g_ref.at[:, pl.ds(aligned(start + at), n), :], buf.at[:, pl.ds(at, n), :], sems.at[i]
        )
        for i, (at, n) in enumerate(spans)
    ]
    for copy in copies:
        copy.start()
    for copy, (at, n) in zip(copies, spans):
        copy.wait()
        send_ref[at : at + n, :] = w_ref[0] * buf[0, at : at + n, :] + w_ref[1] * buf[1, at : at + n, :]


def strips(w_ref, g_ref, ls_ref, p_ref, left_ref, right_ref):
    rows, cols = ls_ref.shape

    def chunk(i, _):
        at = pl.ds(aligned(i * LANES, LANES), LANES)
        p_ref[at, :] = w_ref[0] * g_ref[0, at, :] + w_ref[1] * g_ref[1, at, :]
        for n, ref in enumerate((p_ref, ls_ref)):
            to = slice(n * HALO, (n + 1) * HALO)
            left_ref[to, at] = ref[at, 0:LANES].T[0:HALO, :]
            right_ref[to, at] = ref[at, cols - LANES : cols].T[LANES - HALO :, :]
        return 0

    lax.fori_loop(0, rows // LANES, chunk, 0)


def turned(right, left):
    gap = jnp.zeros((LANES - 2 * HALO, right.shape[1]), jnp.float32)
    return jnp.concatenate([right, gap, left], axis=0).T


def row_messages(f_ref, right_ref, left_ref, p_ref, ls_ref, pcol_ref, lscol_ref, fs_ref, m1_ref, m2_ref):
    rows, cols = ls_ref.shape
    f = f_ref[0]

    def chunk(i, _):
        at = pl.ds(aligned(i * LANES, LANES), LANES)
        for n, ref in enumerate((pcol_ref, lscol_ref)):
            of = slice(n * HALO, (n + 1) * HALO)
            ref[at, :] = turned(right_ref[of, at], left_ref[of, at])
        return 0

    lax.fori_loop(0, rows // LANES, chunk, 0)
    width = fs_ref.shape[1]
    theirs = pl.ds(aligned((1 - f) * (rows - width), LANES), width)
    fs_ref[0:HALO, :] = right_ref[0:HALO, theirs]
    fs_ref[HALO:, :] = left_ref[0:HALO, theirs]
    outer = pl.ds(aligned((1 - f) * (rows - HALO)), HALO)
    inner = pl.ds(aligned(f * (rows - HALO)), HALO)
    m1_ref[0:HALO, 0:cols] = p_ref[outer, :]
    m1_ref[0:HALO, cols:] = pcol_ref[outer, :]
    m1_ref[HALO:, 0:cols] = ls_ref[outer, :]
    m1_ref[HALO:, cols:] = lscol_ref[outer, :]
    m2_ref[:, 0:cols] = p_ref[inner, :]
    m2_ref[:, cols:] = pcol_ref[inner, :]


def spread(nat, r, lo, width):
    return jnp.concatenate(
        [nat[c, pl.ds(lo, 8, stride=r), :] for c in range(width // LANES)], axis=1
    )


def unspread(nat, r, lo, value):
    for c in range(value.shape[1] // LANES):
        nat[c, pl.ds(lo, 8, stride=r), :] = value[:, c * LANES : (c + 1) * LANES]


def put(nat, rows, value, first=0):
    for c in range(value.shape[1] // LANES):
        nat[first + c, rows, :] = value[:, c * LANES : (c + 1) * LANES]


def half_setup(
    f_ref, p_ref, ls_ref, pcol_ref, lscol_ref, m1_ref, m2_ref, fs_ref, t_ref, lsx_ref, q_ref, rec_ref
):
    rows, cols = ls_ref.shape
    f = f_ref[0]
    ext = t_ref.shape[1]
    main = ext - HALO
    first = aligned((1 - f) * HALO)
    beside = pl.ds(aligned(f * main), HALO)
    put(t_ref, beside, m1_ref[0:HALO, :] + m2_ref[...])
    put(lsx_ref, beside, m1_ref[HALO:, :])
    width = fs_ref.shape[1]
    skip = aligned(f * (width - main))
    start = aligned(f * (rows - main))
    for i in range(main // 8):
        to = pl.ds(aligned(first + i * 8), 8)
        of = pl.ds(aligned(start + i * 8), 8)
        put(t_ref, to, p_ref[of, :])
        put(lsx_ref, to, ls_ref[of, :])
        put(t_ref, to, pcol_ref[of, :], cols // LANES)
        put(lsx_ref, to, lscol_ref[of, :], cols // LANES)
    theirs = turned(fs_ref[0:HALO, :], fs_ref[HALO:, :])
    last = cols // LANES

    @pl.when(f == 0)
    def _():
        t_ref[last, HALO : HALO + main, :] = t_ref[last, HALO : HALO + main, :] + theirs[0:main, :]

    @pl.when(f == 1)
    def _():
        t_ref[last, 0:main, :] = t_ref[last, 0:main, :] + theirs[width - main :, :]

    r = ext // 8

    def chunk(k, _):
        x = spread(lsx_ref, r, k, cols + LANES) * (1.0 / band_cells)
        u = x * x
        q = 1.0 / (5.0 + 4.0 * u)
        q_ref[k] = q
        rec_ref[k] = (1.0 + u) * q
        return 0

    lax.fori_loop(0, r, chunk, 0, unroll=2)


def wrap(ref, r):
    ref[0] = pltpu.roll(ref[r], 1, 0)
    ref[r + 1] = pltpu.roll(ref[1], 7, 0)


def sweep(src, r, body, unroll):
    def steps(i, carry):
        up, centre = carry
        for j in range(unroll):
            k = i * unroll + j
            down = src[k + 2]
            body(k, up, centre, down)
            up, centre = centre, down
        return up, centre

    lax.fori_loop(0, r // unroll, steps, (src[0], src[1]))


def divisor(r, most):
    return max(d for d in range(1, most + 1) if r % d == 0)


def half_velocity(f_ref, t_ref, rp_ref, q_ref, rec_ref, vx_ref, msg_ref, top_ref, sum_ref, a_ref, v0, v1):
    cols = rp_ref.shape[1]
    ext = t_ref.shape[1]
    r = ext // 8
    first = (1 - f_ref[0]) * HALO
    main = rp_ref.shape[0]

    def add(i, _):
        to = pl.ds(aligned(first + i * 8), 8)
        of = pl.ds(aligned(i * 8), 8)
        for c in range(cols // LANES):
            sum_ref[c, to, :] = t_ref[c, to, :] + rp_ref[of, c * LANES : (c + 1) * LANES]
        return 0

    lax.fori_loop(0, main // 8, add, 0, unroll=True)
    width = cols + LANES
    beside = pl.ds(aligned(f_ref[0] * main), HALO)
    for c in range(cols // LANES):
        sum_ref[c, beside, :] = t_ref[c, beside, :]

    def load(k, _):
        source = jnp.concatenate(
            [spread(sum_ref, r, k, cols), t_ref[cols // LANES, pl.ds(k, 8, stride=r), :]], axis=1
        )
        v0[k + 1] = source
        a_ref[k] = source * q_ref[k]
        return 0

    lax.fori_loop(0, r, load, 0, unroll=divisor(r, 10))
    wrap(v0, r)
    src, dst = v0, v1
    for s in range(EXT_SWEEPS):
        last = s == EXT_SWEEPS - 1

        def body(k, up, centre, down):
            beside = (up + down) + (pltpu.roll(centre, 1, 1) + pltpu.roll(centre, width - 1, 1))
            value = a_ref[k] + rec_ref[k] * beside
            if last:
                unspread(vx_ref, r, k, value)
            else:
                dst[k + 1] = value

        sweep(src, r, body, divisor(r, 10))
        if not last:
            wrap(dst, r)
        src, dst = dst, src
    half = msg_ref.shape[0] - 2 * HALO
    top = jnp.zeros((8, LANES), jnp.float32)
    for i in range(half // 8):
        for c in range(cols // LANES):
            value = vx_ref[c, HALO + i * 8 : HALO + i * 8 + 8, :]
            top = jnp.maximum(top, jnp.abs(value))
            msg_ref[i * 8 : i * 8 + 8, c * LANES : (c + 1) * LANES] = value
    for i in range(half // LANES):
        side = vx_ref[cols // LANES, HALO + i * LANES : HALO + (i + 1) * LANES, :].T
        msg_ref[half : half + HALO, i * LANES : (i + 1) * LANES] = side[0:HALO, :]
        msg_ref[half + HALO :, i * LANES : (i + 1) * LANES] = side[LANES - HALO :, :]
    top_ref[...] = jnp.full(top_ref.shape, jnp.max(top), jnp.float32)


def speeds(sigma, centre, up, down, left, right):
    a = jnp.maximum(sigma * (centre - up), TINY)
    b = jnp.maximum(sigma * (centre - down), 0.0)
    c = jnp.maximum(sigma * (centre - left), 0.0)
    d = jnp.maximum(sigma * (centre - right), 0.0)
    return (a * a + b * b) + (c * c + d * d)


def reinit(top_ref, ls_nat, v_nat, base, r, out_nat, p0, p1, h_ref, s_ref, width):
    step = cfl_number / (jnp.max(top_ref[...]) + 1e-06)
    unroll = divisor(r, 10)

    def load(k, _):
        p0[k + 1] = spread(ls_nat, r, base + k, width)
        return 0

    lax.fori_loop(0, r, load, 0, unroll=unroll)
    wrap(p0, r)

    def advance(k, up, centre, down):
        speed = spread(v_nat, r, base + k, width)
        sigma = jnp.where(speed >= 0.0, 1.0, -1.0)
        total = speeds(sigma, centre, up, down, pltpu.roll(centre, 1, 1), pltpu.roll(centre, width - 1, 1))
        advanced = centre - step * (speed * (total * lax.rsqrt(total)))
        p1[k + 1] = advanced
        h_ref[k] = pseudo_step * (advanced * lax.rsqrt(advanced * advanced + 1.0))
        s_ref[k] = jnp.where(advanced >= 0.0, 1.0, -1.0)

    sweep(p0, r, advance, unroll)
    wrap(p1, r)
    src, dst = p1, p0
    for it in range(REINIT_ITERS):
        last = it == REINIT_ITERS - 1

        def body(k, up, centre, down):
            total = speeds(
                s_ref[k], centre, up, down, pltpu.roll(centre, 1, 1), pltpu.roll(centre, width - 1, 1)
            )
            h = h_ref[k]
            value = (centre + h) - h * (total * lax.rsqrt(total))
            if last:
                unspread(out_nat, r, k, value[:, 0 : width - LANES])
            else:
                dst[k + 1] = value

        sweep(src, r, body, unroll)
        if not last:
            wrap(dst, r)
        src, dst = dst, src


def outer_part(f_ref, top_ref, lsx_ref, vx_ref, out_ref, nat, p0, p1, h_ref, s_ref):
    n, cols = out_ref.shape
    r = (n + 2 * HALO) // 8
    base = f_ref[0] * (lsx_ref.shape[1] - 8 * r)
    reinit(top_ref, lsx_ref, vx_ref, base, r, nat, p0, p1, h_ref, s_ref, cols + LANES)
    for c in range(cols // LANES):
        out_ref[:, c * LANES : (c + 1) * LANES] = nat[c, HALO : HALO + n, :]


def middle_part(
    f_ref, top_ref, vx_ref, msg_ref, got_ref, ls_ref, lscol_ref, mine_ref, level_ref, vel_ref,
    nat, lsn, vn, p0, p1, h_ref, s_ref,
):
    rows, cols = ls_ref.shape
    f = f_ref[0]
    ext = lsn.shape[1]
    r = ext // 8
    low = (rows - ext) // 2
    last = cols // LANES
    half = rows // 2
    side = turned(got_ref[half : half + HALO, :], got_ref[half + HALO :, :])
    for c in range(last + 1):
        for i in range(ext // 8):
            at = low + i * 8
            lanes = slice(c * LANES, (c + 1) * LANES)
            lsn[c, i * 8 : i * 8 + 8, :] = lscol_ref[at : at + 8, :] if c == last else ls_ref[at : at + 8, lanes]

    @pl.when(f == 0)
    def _():
        cut = half - low
        for c in range(last + 1):
            lanes = slice(c * LANES, (c + 1) * LANES)
            vn[c, 0:cut, :] = vx_ref[c, HALO + low : HALO + half, :]
            vn[c, cut:, :] = side[0 : ext - cut, :] if c == last else got_ref[0 : ext - cut, lanes]
        vel_ref[0:half, :] = msg_ref[0:half, :]
        vel_ref[half:, :] = got_ref[0:half, :]

    @pl.when(f == 1)
    def _():
        cut = half - low
        for c in range(last + 1):
            lanes = slice(c * LANES, (c + 1) * LANES)
            vn[c, 0:cut, :] = side[low:half, :] if c == last else got_ref[low:half, lanes]
            vn[c, cut:, :] = vx_ref[c, HALO : HALO + ext - cut, :]
        vel_ref[0:half, :] = got_ref[0:half, :]
        vel_ref[half:, :] = msg_ref[0:half, :]

    reinit(top_ref, lsn, vn, 0, r, nat, p0, p1, h_ref, s_ref, cols + LANES)
    n = mine_ref.shape[0]
    for c in range(last):
        level_ref[low + HALO : low + ext - HALO, c * LANES : (c + 1) * LANES] = nat[c, HALO : ext - HALO, :]
    level_ref[pl.ds(aligned(f * (rows - n)), n), :] = mine_ref[...]


def insert(f_ref, got_ref, _, level_ref, sem):
    n = got_ref.shape[0]
    to = pl.ds(aligned((1 - f_ref[0]) * (level_ref.shape[0] - n)), n)
    copy = pltpu.make_async_copy(got_ref, level_ref.at[to, :], sem)
    copy.start()
    copy.wait()


def shifted(n, by):
    return [(i, (i + by) % n) for i in range(n)]


def per_device(level_set, focus_grads, focus_weight):
    rows, cols = level_set.shape
    half = rows // 2
    gx, gy = lax.axis_size("gx"), lax.axis_size("gy")
    f = lax.axis_index("focus").reshape(1).astype(jnp.int32)
    planes = focus_grads.shape[0]
    assert planes == 2 and lax.axis_size("focus") == 2
    swap = [(0, 1), (1, 0)]
    main, ext, wide = half + HALO, half + 2 * HALO, cols + LANES
    slabs = wide // LANES

    (to_partner,) = call(
        send_part,
        [(main, cols)],
        [SMEM, SMEM, ANY],
        [pltpu.VMEM((planes, main, cols), jnp.float32), pltpu.SemaphoreType.DMA((4,))],
        "send_part",
    )(f, focus_weight, focus_grads)
    from_partner = lax.ppermute(to_partner, "focus", swap)

    p, left, right = call(
        strips, [(rows, cols), (2 * HALO, rows), (2 * HALO, rows)], [SMEM, VMEM, VMEM], (), "strips"
    )(focus_weight, focus_grads, level_set)
    from_right = lax.ppermute(left, "gy", shifted(gy, -1))
    from_left = lax.ppermute(right, "gy", shifted(gy, 1))
    side = -(-main // LANES) * LANES
    pcol, lscol, fs, m1, m2 = call(
        row_messages,
        [(rows, LANES), (rows, LANES), (2 * HALO, side), (2 * HALO, wide), (HALO, wide)],
        [SMEM, VMEM, VMEM, VMEM, VMEM],
        (),
        "row_messages",
    )(f, from_right, from_left, p, level_set)

    def place(f, x):
        return f * gx + x % gx

    same = [(place(0, x), place(0, x + 1)) for x in range(gx)] + [(place(1, x), place(1, x - 1)) for x in range(gx)]
    cross = [(place(0, x), place(1, x - 1)) for x in range(gx)] + [(place(1, x), place(0, x + 1)) for x in range(gx)]
    got1 = lax.ppermute(m1, ("focus", "gx"), same)
    got2 = lax.ppermute(m2, ("focus", "gx"), cross)
    got_fs = lax.ppermute(fs, "focus", swap)
    r = ext // 8
    t, lsx, q, rec = call(
        half_setup,
        [(slabs, ext, LANES), (slabs, ext, LANES), (r, 8, wide), (r, 8, wide)],
        [SMEM] + [VMEM] * 7,
        (),
        "half_setup",
    )(f, p, level_set, pcol, lscol, got1, got2, got_fs)
    devices = 2 * gx * gy
    vx, msg, top = call(
        half_velocity,
        [(slabs, ext, LANES), (half + 2 * HALO, cols), (devices, 8, LANES)],
        [SMEM] + [VMEM] * 4,
        [pltpu.VMEM((cols // LANES, ext, LANES), jnp.float32), pltpu.VMEM((r, 8, wide), jnp.float32)]
        + [pltpu.VMEM((r + 2, 8, wide), jnp.float32)] * 2,
        "half_velocity",
    )(f, t, from_partner, q, rec)
    got_msg = lax.ppermute(msg, "focus", swap)
    tops = lax.all_to_all(top, ("focus", "gx", "gy"), 0, 0)

    own = rows // 4
    r1 = (own + 2 * HALO) // 8
    (mine,) = call(
        outer_part,
        [(own, cols)],
        [SMEM] + [VMEM] * 3,
        [pltpu.VMEM((cols // LANES, 8 * r1, LANES), jnp.float32)]
        + [pltpu.VMEM((r1 + 2, 8, wide), jnp.float32)] * 2
        + [pltpu.VMEM((r1, 8, wide), jnp.float32)] * 2,
        "outer_part",
    )(f, tops, lsx, vx)
    theirs = lax.ppermute(mine, "focus", swap)
    mid = rows - 2 * own + 2 * HALO
    r2 = mid // 8
    level, velocity = call(
        middle_part,
        [(rows, cols), (rows, cols)],
        [SMEM] + [VMEM] * 7,
        [pltpu.VMEM((cols // LANES, mid, LANES), jnp.float32)]
        + [pltpu.VMEM((slabs, mid, LANES), jnp.float32)] * 2
        + [pltpu.VMEM((r2 + 2, 8, wide), jnp.float32)] * 2
        + [pltpu.VMEM((r2, 8, wide), jnp.float32)] * 2,
        "middle_part",
    )(f, tops, vx, msg, got_msg, level_set, lscol, mine)
    (level,) = call(
        insert,
        [(rows, cols)],
        [SMEM, VMEM, ANY],
        [pltpu.SemaphoreType.DMA(())],
        "insert",
        out_specs=[ANY],
        aliases={2: 0},
    )(f, theirs, level)
    return level, velocity


def solution(mesh):
    in_specs = (P("gx", "gy"), P("focus", "gx", "gy"), P("focus"))
    out_specs = (P("gx", "gy"), P("gx", "gy"))
    return jax.shard_map(
        per_device, mesh=mesh, in_specs=in_specs, out_specs=out_specs, check_vma=False
    )
```

```python
import jax
import jax.numpy as jnp
from jax import lax
from jax.experimental import pallas as pl
from jax.experimental.pallas import tpu as pltpu
from jax.sharding import PartitionSpec as P

EXT_SWEEPS = 8
REINIT_ITERS = 10
band_cells = 3.0
cfl_number = 0.5
pseudo_step = 0.5

HALO = 24
EDGE = 12
STAGED = 16
OWN_PARTS = (3, 16)
LANES = 128
TINY = 1e-18

VMEM = pl.BlockSpec(memory_space=pltpu.VMEM)
SMEM = pl.BlockSpec(memory_space=pltpu.SMEM)
ANY = pl.BlockSpec(memory_space=pl.ANY)
DMA = pltpu.SemaphoreType.DMA


def vmem(*shape):
    return pltpu.VMEM(shape, jnp.float32)


def call(body, out_shapes, in_specs, scratch=(), name=None, flops=0, out_specs=None, aliases=None, mib=24):
    outs = [jax.ShapeDtypeStruct(s, jnp.float32) for s in out_shapes]
    return pl.pallas_call(
        body,
        out_shape=outs,
        in_specs=in_specs,
        out_specs=out_specs or [VMEM] * len(outs),
        scratch_shapes=list(scratch),
        name=name,
        input_output_aliases=aliases or {},
        compiler_params=pltpu.CompilerParams(vmem_limit_bytes=mib << 20),
        cost_estimate=pl.CostEstimate(flops=flops, bytes_accessed=1 << 20, transcendentals=0),
    )


def aligned(x, n=8):
    return pl.multiple_of(x, n)


def lanes_of(c):
    return slice(c * LANES, (c + 1) * LANES)


def partner_rows(f, rows, main):
    return aligned((1 - f) * (rows - main))


def send_part(main, f_ref, w_ref, g_ref, send_ref, buf, sems):
    n = send_ref.shape[0]
    start = partner_rows(f_ref[0], g_ref.shape[1], main)
    chunks = sems.shape[0]
    step = n // 8 // chunks * 8
    spans = [(i * step, step if i < chunks - 1 else n - i * step) for i in range(chunks)]
    copies = [
        pltpu.make_async_copy(
            g_ref.at[:, pl.ds(aligned(start + at), n), :], buf.at[:, pl.ds(at, n), :], sems.at[i]
        )
        for i, (at, n) in enumerate(spans)
    ]
    for copy in copies:
        copy.start()
    for copy, (at, n) in zip(copies, spans):
        copy.wait()
        send_ref[at : at + n, :] = w_ref[0] * buf[0, at : at + n, :] + w_ref[1] * buf[1, at : at + n, :]


def strips(w_ref, g_ref, ls_ref, p_ref, left_ref, right_ref, buf, sems):
    rows, cols = ls_ref.shape
    n = rows // sems.shape[0]
    copies = [
        pltpu.make_async_copy(g_ref.at[:, pl.ds(i * n, n), :], buf.at[:, pl.ds(i * n, n), :], sems.at[i])
        for i in range(sems.shape[0])
    ]
    for copy in copies:
        copy.start()
    lane = lax.broadcasted_iota(jnp.int32, (LANES, LANES), 1)
    for i in range(rows // LANES):
        at = lanes_of(i)
        if i * LANES % n == 0:
            copies[i * LANES // n].wait()
        p_ref[at, :] = w_ref[0] * buf[0, at, :] + w_ref[1] * buf[1, at, :]
        first, last = slice(0, LANES), slice(cols - LANES, cols)
        packed = p_ref[at, first]
        for j, (ref, of) in enumerate(((ls_ref, first), (p_ref, last), (ls_ref, last)), 1):
            held = 0 if of.start == 0 else LANES - HALO
            moved = pltpu.roll(ref[at, of], (j * HALO - held) % LANES, 1)
            packed = jnp.where(lane < j * HALO, packed, moved)
        turned_ = packed.T
        left_ref[:, at] = turned_[0 : 2 * HALO, :]
        right_ref[:, at] = turned_[2 * HALO : 4 * HALO, :]


def turned(right, left):
    gap = jnp.zeros((LANES - 2 * HALO, right.shape[1]), jnp.float32)
    return jnp.concatenate([right, gap, left], axis=0).T


def row_messages(main, f_ref, right_ref, left_ref, p_ref, ls_ref, fs_ref, m1_ref, m2_ref, rest_ref):
    rows, cols = ls_ref.shape
    f = f_ref[0]
    width = fs_ref.shape[1]
    theirs = pl.ds(aligned((1 - f) * (rows - width), LANES), width)
    fs_ref[0:HALO, :] = right_ref[0:HALO, theirs]
    fs_ref[HALO:, :] = left_ref[0:HALO, theirs]

    def corner(of, bottom):
        at = pl.ds(aligned(bottom * (rows - LANES), LANES), LANES)
        return turned(right_ref[of, at], left_ref[of, at])

    def ends(block, bottom):
        return jnp.where(bottom == 1, block[LANES - HALO :, :], block[0:HALO, :])

    outer, inner = 1 - f, f
    p_part, ls_part = slice(0, HALO), slice(HALO, 2 * HALO)
    at_outer = pl.ds(aligned(outer * (rows - HALO)), HALO)
    at_inner = pl.ds(aligned(inner * (rows - HALO)), HALO)
    m1_ref[p_part, 0:cols] = p_ref[at_outer, :]
    m1_ref[p_part, cols:] = ends(corner(p_part, outer), outer)
    m1_ref[ls_part, 0:cols] = ls_ref[at_outer, :]
    m1_ref[ls_part, cols:] = ends(corner(ls_part, outer), outer)
    m2_ref[:, 0:cols] = p_ref[at_inner, :]
    m2_ref[:, cols:] = ends(corner(p_part, inner), inner)
    n = rest_ref.shape[0]
    rest_ref[...] = p_ref[pl.ds(aligned(partner_rows(f, rows, main) + main - n), n), :]


def spread(nat, r, lo, width):
    return jnp.concatenate(
        [nat[c, pl.ds(lo, 8, stride=r), :] for c in range(width // LANES)], axis=1
    )


def unspread(nat, r, lo, value):
    for c in range(value.shape[1] // LANES):
        nat[c, pl.ds(lo, 8, stride=r), :] = value[:, lanes_of(c)]


def put(nat, rows, value, first=0):
    for c in range(value.shape[1] // LANES):
        nat[first + c, rows, :] = value[:, lanes_of(c)]


def half_setup(
    f_ref, p_ref, ls_ref, right_ref, left_ref, m1_ref, m2_ref, fs_ref,
    t_ref, lsx_ref, q_ref, rec_ref, nat, pcol, lscol,
):
    rows, cols = ls_ref.shape
    f = f_ref[0]
    ext = lsx_ref.shape[1]
    main = ext - HALO
    first = aligned((1 - f) * HALO)
    beside = pl.ds(aligned(f * main), HALO)
    put(nat, beside, m1_ref[0:HALO, :] + m2_ref[...])
    put(lsx_ref, beside, m1_ref[HALO:, :])
    width = fs_ref.shape[1]
    skip = f * (width - main)
    lane0 = f * (rows - width)
    for i in range(width // LANES):
        at = pl.ds(aligned(lane0 + i * LANES, LANES), LANES)
        to = lanes_of(i)
        pcol[to, :] = turned(
            right_ref[0:HALO, at] + fs_ref[0:HALO, to], left_ref[0:HALO, at] + fs_ref[HALO:, to]
        )
        lscol[to, :] = turned(right_ref[HALO:, at], left_ref[HALO:, at])
    start = f * (rows - main)
    last = cols // LANES
    for i in range(main // 8):
        to = pl.ds(aligned(first + i * 8), 8)
        of = pl.ds(aligned(start + i * 8), 8)
        side = pl.ds(aligned(skip + i * 8), 8)
        put(nat, to, p_ref[of, :])
        put(lsx_ref, to, ls_ref[of, :])
        nat[last, to, :] = pcol[side, :]
        lsx_ref[last, to, :] = lscol[side, :]

    r = ext // 8
    for k in range(r):
        x = spread(lsx_ref, r, k, cols + LANES) * (1.0 / band_cells)
        u = x * x
        q = 1.0 / (5.0 + 4.0 * u)
        q_ref[k] = q
        rec_ref[k] = (1.0 + u) * q
        t_ref[k] = spread(nat, r, k, cols + LANES)


def wrap(ref, r):
    ref[0] = pltpu.roll(ref[r], 1, 0)
    ref[r + 1] = pltpu.roll(ref[1], 7, 0)


def sweep(src, r, body):
    up, centre = src[0], src[1]
    for k in range(r):
        down = src[k + 2]
        body(k, up, centre, down)
        up, centre = centre, down


def half_velocity(f_ref, t_ref, rp1_ref, rp2_ref, q_ref, rec_ref, vs_ref, top_ref, nat, a_ref, v0, v1):
    cols = rp1_ref.shape[1]
    r, _, width = t_ref.shape
    ext = 8 * r
    f = f_ref[0]
    at = aligned((1 - f) * HALO)
    main = ext - HALO
    for c in range(cols // LANES):
        nat[c, pl.ds(aligned(f * main), HALO), :] = jnp.zeros((HALO, LANES), jnp.float32)
    n1, n2 = rp1_ref.shape[0], rp2_ref.shape[0]
    put(nat, pl.ds(at, n1), rp1_ref[...])
    put(nat, pl.ds(aligned(at + n1), n2), rp2_ref[...])
    for k in range(r):
        t = t_ref[k]
        source = jnp.concatenate([t[:, 0:cols] + spread(nat, r, k, cols), t[:, cols:]], axis=1)
        v0[k + 1] = source
        a_ref[k] = source * q_ref[k]
    wrap(v0, r)

    def relax(k, up, centre, down):
        beside = (up + down) + (pltpu.roll(centre, 1, 1) + pltpu.roll(centre, width - 1, 1))
        return a_ref[k] + rec_ref[k] * beside

    def one(src, dst):
        def body(k, *cells):
            dst[k + 1] = relax(k, *cells)

        sweep(src, r, body)
        wrap(dst, r)

    def pair(i, _):
        one(v0, v1)
        one(v1, v0)
        return 0

    assert EXT_SWEEPS % 2 == 0
    lax.fori_loop(0, EXT_SWEEPS // 2 - 1, pair, 0)
    one(v0, v1)
    sub = lax.broadcasted_iota(jnp.int32, (8, cols), 0)
    tops = [jnp.zeros((8, cols), jnp.float32)] * 2

    def final(k, *cells):
        value = relax(k, *cells)
        vs_ref[k] = value
        size = jnp.abs(value[:, 0:cols])
        row = sub * r + k
        if k < HALO or 7 * r + k >= ext - HALO:
            size = jnp.where((row >= HALO) & (row < ext - HALO), size, 0.0)
        tops[k % 2] = jnp.maximum(tops[k % 2], size)

    sweep(v1, r, final)
    top_ref[...] = jnp.full(top_ref.shape, jnp.max(jnp.maximum(*tops)), jnp.float32)


def velocity_messages(f_ref, vs_ref, vx_ref, near_ref, far_ref):
    slabs, ext, _ = vx_ref.shape
    r = ext // 8
    for k in range(r):
        unspread(vx_ref, r, k, vs_ref[k])
    far = far_ref.shape[0]
    near = near_ref.shape[0] - 2 * HALO
    half = far + near
    f = f_ref[0]
    at_near = pl.ds(aligned(HALO + (1 - f) * far), near)
    at_far = pl.ds(aligned(HALO + f * near), far)
    for c in range(slabs - 1):
        near_ref[0:near, lanes_of(c)] = vx_ref[c, at_near, :]
        far_ref[:, lanes_of(c)] = vx_ref[c, at_far, :]
    for i in range(half // LANES):
        side = vx_ref[slabs - 1, HALO + i * LANES : HALO + (i + 1) * LANES, :].T
        near_ref[near : near + HALO, lanes_of(i)] = side[0:HALO, :]
        near_ref[near + HALO :, lanes_of(i)] = side[LANES - HALO :, :]


def speeds(sigma, centre, up, down, left, right):
    a = jnp.maximum(sigma * (centre - up), TINY)
    b = jnp.maximum(sigma * (centre - down), 0.0)
    c = jnp.maximum(sigma * (centre - left), 0.0)
    d = jnp.maximum(sigma * (centre - right), 0.0)
    return (a * a + b * b) + (c * c + d * d)


def reinit(top_ref, ls_nat, v_nat, base, r, out_nat, shift, p0, p1, h_ref, s_ref, width):
    step = cfl_number / (jnp.max(top_ref[...]) + 1e-06)
    for k in range(r):
        p0[k + 1] = spread(ls_nat, r, base + k, width)
    wrap(p0, r)

    def beside(centre):
        return pltpu.roll(centre, 1, 1), pltpu.roll(centre, width - 1, 1)

    def advance(k, up, centre, down):
        speed = spread(v_nat, r, base + k, width)
        sigma = jnp.where(speed >= 0.0, 1.0, -1.0)
        total = speeds(sigma, centre, up, down, *beside(centre))
        advanced = centre - step * (speed * (total * lax.rsqrt(total)))
        p1[k + 1] = advanced
        h_ref[k] = pseudo_step * (advanced * lax.rsqrt(advanced * advanced + 1.0))
        s_ref[k] = jnp.where(advanced >= 0.0, 1.0, -1.0)

    sweep(p0, r, advance)
    wrap(p1, r)

    def one(src, dst):
        def body(k, up, centre, down):
            total = speeds(s_ref[k], centre, up, down, *beside(centre))
            h = h_ref[k]
            dst[k + 1] = (centre + h) - h * (total * lax.rsqrt(total))

        sweep(src, r, body)
        wrap(dst, r)

    def pair(i, _):
        one(p1, p0)
        one(p0, p1)
        return 0

    assert REINIT_ITERS % 2 == 0
    lax.fori_loop(0, REINIT_ITERS // 2 - 1, pair, 0)
    one(p1, p0)
    cols = width - LANES

    def final(k, up, centre, down):
        left, right = beside(centre)
        c = centre[:, 0:cols]
        total = speeds(s_ref[k][:, 0:cols], c, up[:, 0:cols], down[:, 0:cols], left[:, 0:cols], right[:, 0:cols])
        h = h_ref[k][:, 0:cols]
        unspread(out_nat, r, k + shift, (c + h) - h * (total * lax.rsqrt(total)))

    sweep(p0, r, final)


def outer_part(f_ref, top_ref, lsx_ref, vx_ref, out_ref, nat, p0, p1, h_ref, s_ref):
    n, cols = out_ref.shape
    r = (n + 2 * EDGE) // 8
    base = HALO - EDGE + f_ref[0] * (lsx_ref.shape[1] - 2 * HALO - n)
    reinit(top_ref, lsx_ref, vx_ref, base, r, nat, STAGED - EDGE, p0, p1, h_ref, s_ref, cols + LANES)
    for c in range(cols // LANES):
        out_ref[:, lanes_of(c)] = nat[c, STAGED : STAGED + n, :]


def middle_part(
    f_ref, top_ref, vx_ref, near_ref, ls_ref, right_ref, left_ref, mine_ref, level_ref, vel_ref,
    nat, lsn, vn, p0, p1, h_ref, s_ref, sems,
):
    rows, cols = ls_ref.shape
    f = f_ref[0]
    staged = lsn.shape[1]
    n = staged - 2 * STAGED
    r = (n + 2 * EDGE) // 8
    low = (rows - staged) // 2
    last = cols // LANES
    half = rows // 2
    near = near_ref.shape[0] - 2 * HALO
    own = mine_ref.shape[0]
    ready = [
        pltpu.make_async_copy(
            vx_ref.at[c, pl.ds(HALO, half), :],
            vel_ref.at[pl.ds(aligned(f * half), half), pl.ds(c * LANES, LANES)],
            sems.at[c],
        )
        for c in range(last)
    ]
    ready.append(
        pltpu.make_async_copy(
            near_ref.at[pl.ds(0, near), :],
            vel_ref.at[pl.ds(aligned((1 - f) * half + f * (half - near)), near), :],
            sems.at[last],
        )
    )
    ready.append(
        pltpu.make_async_copy(
            mine_ref, level_ref.at[pl.ds(aligned(f * (rows - own)), own), :], sems.at[last + 1]
        )
    )
    for copy in ready:
        copy.start()
    for c in range(last):
        lsn[c] = ls_ref[low : low + staged, lanes_of(c)]
    cut = half - low
    for i in range(rows // LANES):
        at = i * LANES
        begin, end = max(at, low), min(at + LANES, low + staged)
        if begin < end:
            block = turned(right_ref[HALO:, at : at + LANES], left_ref[HALO:, at : at + LANES])
            lsn[last, begin - low : end - low, :] = block[begin - at : end - at, :]
        if at < half:
            block = turned(near_ref[near : near + HALO, at : at + LANES], near_ref[near + HALO :, at : at + LANES])

            @pl.when(f == 0)
            def _():
                end = min(at + LANES, staged - cut)
                if at < end:
                    vn[last, cut + at : cut + end, :] = block[0 : end - at, :]

            @pl.when(f == 1)
            def _():
                begin = max(at, low)
                if begin < at + LANES:
                    vn[last, begin - low : at + LANES - low, :] = block[begin - at :, :]

    @pl.when(f == 0)
    def _():
        vn[:, 0:cut, :] = vx_ref[:, HALO + low : HALO + half, :]
        put(vn, slice(cut, staged), near_ref[0 : staged - cut, :])

    @pl.when(f == 1)
    def _():
        put(vn, slice(0, cut), near_ref[near - cut : near, :])
        vn[:, cut:, :] = vx_ref[:, HALO : HALO + staged - cut, :]

    reinit(top_ref, lsn, vn, STAGED - EDGE, r, nat, STAGED - EDGE, p0, p1, h_ref, s_ref, cols + LANES)
    results = [
        pltpu.make_async_copy(
            nat.at[c, pl.ds(STAGED, n), :],
            level_ref.at[pl.ds(low + STAGED, n), pl.ds(c * LANES, LANES)],
            sems.at[last + 2 + c],
        )
        for c in range(last)
    ]
    for copy in results:
        copy.start()
    for copy in ready + results:
        copy.wait()


def insert(f_ref, theirs_ref, far_ref, _, __, level_ref, vel_ref, sems):
    rows = level_ref.shape[0]
    n, far = theirs_ref.shape[0], far_ref.shape[0]
    f = f_ref[0]
    copies = [
        pltpu.make_async_copy(
            theirs_ref, level_ref.at[pl.ds(aligned((1 - f) * (rows - n)), n), :], sems.at[0]
        ),
        pltpu.make_async_copy(
            far_ref, vel_ref.at[pl.ds(aligned((1 - f) * (rows - far)), far), :], sems.at[1]
        ),
    ]
    for copy in copies:
        copy.start()
    for copy in copies:
        copy.wait()


def shifted(n, by):
    return [(i, (i + by) % n) for i in range(n)]


def per_device(level_set, focus_grads, focus_weight):
    rows, cols = level_set.shape
    half = rows // 2
    gx, gy = lax.axis_size("gx"), lax.axis_size("gy")
    f = lax.axis_index("focus").reshape(1).astype(jnp.int32)
    planes = focus_grads.shape[0]
    assert planes == 2 and lax.axis_size("focus") == 2
    swap = [(0, 1), (1, 0)]
    main, ext, wide = half + HALO, half + 2 * HALO, cols + LANES
    slabs = wide // LANES
    part = main * 3 // 4 // 16 * 16

    (to_partner,) = call(
        lambda *refs: send_part(main, *refs),
        [(part, cols)],
        [SMEM, SMEM, ANY],
        [vmem(planes, part, cols), DMA((4,))],
        "send_part",
    )(f, focus_weight, focus_grads)
    from_partner = lax.ppermute(to_partner, "focus", swap)

    p, left, right = call(
        strips,
        [(rows, cols), (2 * HALO, rows), (2 * HALO, rows)],
        [SMEM, ANY, VMEM],
        [vmem(planes, rows, cols), DMA((4,))],
        "strips",
    )(focus_weight, focus_grads, level_set)
    from_right = lax.ppermute(left, "gy", shifted(gy, -1))
    from_left = lax.ppermute(right, "gy", shifted(gy, 1))
    side = -(-main // LANES) * LANES
    fs, m1, m2, to_partner2 = call(
        lambda *refs: row_messages(main, *refs),
        [(2 * HALO, side), (2 * HALO, wide), (HALO, wide), (main - part, cols)],
        [SMEM, VMEM, VMEM, VMEM, VMEM],
        (),
        "row_messages",
    )(f, from_right, from_left, p, level_set)

    def place(f, x):
        return f * gx + x % gx

    same = [(place(0, x), place(0, x + 1)) for x in range(gx)] + [(place(1, x), place(1, x - 1)) for x in range(gx)]
    cross = [(place(0, x), place(1, x - 1)) for x in range(gx)] + [(place(1, x), place(0, x + 1)) for x in range(gx)]
    got1 = lax.ppermute(m1, ("focus", "gx"), same)
    got2 = lax.ppermute(m2, ("focus", "gx"), cross)
    got_fs = lax.ppermute(fs, "focus", swap)
    from_partner2 = lax.ppermute(to_partner2, "focus", swap)
    r = ext // 8
    t, lsx, q, rec = call(
        half_setup,
        [(r, 8, wide), (slabs, ext, LANES), (r, 8, wide), (r, 8, wide)],
        [SMEM] + [VMEM] * 7,
        [vmem(slabs, ext, LANES), vmem(side, LANES), vmem(side, LANES)],
        "half_setup",
    )(f, p, level_set, from_right, from_left, got1, got2, got_fs)
    devices = 2 * gx * gy
    vs, top = call(
        half_velocity,
        [(r, 8, wide), (devices, LANES)],
        [SMEM] + [VMEM] * 5,
        [vmem(slabs - 1, ext, LANES), vmem(r, 8, wide), vmem(r + 2, 8, wide), vmem(r + 2, 8, wide)],
        "half_velocity",
    )(f, t, from_partner, from_partner2, q, rec)
    tops = lax.all_to_all(top, ("focus", "gx", "gy"), 0, 0)

    own = rows * OWN_PARTS[0] // OWN_PARTS[1]
    near = half - own + STAGED
    vx, to_near, to_far = call(
        velocity_messages,
        [(slabs, ext, LANES), (near + 2 * HALO, cols), (half - near, cols)],
        [SMEM, VMEM],
        (),
        "velocity_messages",
    )(f, vs)
    got_near = lax.ppermute(to_near, "focus", swap)
    got_far = lax.ppermute(to_far, "focus", swap)

    def work(n):
        r = (n + 2 * EDGE) // 8
        return [vmem(r + 2, 8, wide)] * 2 + [vmem(r, 8, wide)] * 2

    (mine,) = call(
        outer_part,
        [(own, cols)],
        [SMEM] + [VMEM] * 3,
        [vmem(slabs - 1, own + 2 * STAGED, LANES)] + work(own),
        "outer_part",
    )(f, tops, lsx, vx)
    theirs = lax.ppermute(mine, "focus", swap)
    mid = rows - 2 * own
    staged = mid + 2 * STAGED
    level, velocity = call(
        middle_part,
        [(rows, cols), (rows, cols)],
        [SMEM] + [VMEM] * 7,
        [vmem(slabs - 1, staged, LANES), vmem(slabs, staged, LANES), vmem(slabs, staged, LANES)]
        + work(mid)
        + [DMA((2 * slabs,))],
        "middle_part",
        out_specs=[ANY, ANY],
        mib=32,
    )(f, tops, vx, got_near, level_set, from_right, from_left, mine)
    level, velocity = call(
        insert,
        [(rows, cols), (rows, cols)],
        [SMEM, VMEM, VMEM, ANY, ANY],
        [DMA((2,))],
        "insert",
        out_specs=[ANY, ANY],
        aliases={3: 0, 4: 1},
    )(f, theirs, got_far, level, velocity)
    return level, velocity


def solution(mesh):
    in_specs = (P("gx", "gy"), P("focus", "gx", "gy"), P("focus"))
    out_specs = (P("gx", "gy"), P("gx", "gy"))
    return jax.shard_map(
        per_device, mesh=mesh, in_specs=in_specs, out_specs=out_specs, check_vma=False
    )
```

```python
import jax
import jax.numpy as jnp
from jax import lax
from jax.experimental import pallas as pl
from jax.experimental.pallas import tpu as pltpu
from jax.sharding import PartitionSpec as P

EXT_SWEEPS = 8
REINIT_ITERS = 10
band_cells = 3.0
cfl_number = 0.5
pseudo_step = 0.5

HALO = 24
SIDE = 20
EDGE = 12
STAGED = 16
OWN_PARTS = (1, 4)
FIRST_PARTS = (26, 35)
EARLY = 128
LANES = 128
TINY = 1e-18

VMEM = pl.BlockSpec(memory_space=pltpu.VMEM)
SMEM = pl.BlockSpec(memory_space=pltpu.SMEM)
HBM = pl.BlockSpec(memory_space=pl.ANY)
DMA = pltpu.SemaphoreType.DMA


def vmem(*shape):
    return pltpu.VMEM(shape, jnp.float32)


def call(body, out_shapes, in_specs, scratch=(), name=None, out_specs=None, aliases=None, mib=16, us=1):
    out_specs = out_specs or [VMEM] * len(out_shapes)
    outs = [
        pltpu.HBM(s, jnp.float32) if spec is HBM else jax.ShapeDtypeStruct(s, jnp.float32)
        for s, spec in zip(out_shapes, out_specs)
    ]
    kernel = pl.pallas_call(
        body,
        out_shape=outs,
        in_specs=in_specs,
        out_specs=out_specs,
        scratch_shapes=list(scratch),
        name=name,
        input_output_aliases=aliases or {},
        compiler_params=pltpu.CompilerParams(vmem_limit_bytes=mib << 20),
        cost_estimate=pl.CostEstimate(flops=int(us * 1e9), bytes_accessed=0, transcendentals=0),
    )

    def run(*args):
        return kernel(
            *(pltpu.with_memory_space_constraint(x, pltpu.HBM) if spec is HBM else x for x, spec in zip(args, in_specs))
        )

    return run


def aligned(x, n=8):
    return pl.multiple_of(x, n)


def lanes_of(c):
    return slice(c * LANES, (c + 1) * LANES)


def blank(nat, f, main):
    for c in range(nat.shape[0]):
        nat[c, pl.ds(aligned(f * main), HALO), :] = jnp.zeros((HALO, LANES), jnp.float32)


def send_part(f_ref, w_hbm, g_ref, send_ref, buf, nat, w_ref, sems):
    n, main, cols = send_ref.shape[0], buf.shape[1], buf.shape[2]
    f = f_ref[0]
    start = (1 - f) * (g_ref.shape[1] - main)
    chunks = sems.shape[0] - 1
    weights = pltpu.make_async_copy(w_hbm, w_ref, sems.at[chunks])
    weights.start()
    step = main // 8 // chunks * 8
    spans = [(i * step, step if i < chunks - 1 else main - i * step) for i in range(chunks)]
    copies = [
        pltpu.make_async_copy(
            g_ref.at[:, pl.ds(aligned(start + at), n), :], buf.at[:, pl.ds(at, n), :], sems.at[i]
        )
        for i, (at, n) in enumerate(spans)
    ]
    for copy in copies:
        copy.start()
    blank(nat, 1 - f, main)
    weights.wait()
    for copy, (at, rows) in zip(copies, spans):
        copy.wait()
        part = w_ref[0] * buf[0, at : at + rows, :] + w_ref[1] * buf[1, at : at + rows, :]
        put(nat, pl.ds(aligned(f * HALO + at), rows), part)
    for k in range(n):
        send_ref[k] = spread(nat, nat.shape[1] // 8, k, cols)


def send_rest(main, f_ref, p_ref, _, send_ref, nat):
    rows, cols = p_ref.shape
    f = f_ref[0]
    r = nat.shape[1] // 8
    blank(nat, 1 - f, main)
    put(nat, pl.ds(aligned(f * HALO), main), p_ref[pl.ds(aligned((1 - f) * (rows - main)), main), :])
    for k in range(send_ref.shape[0]):
        send_ref[k] = spread(nat, r, r - send_ref.shape[0] + k, cols)


def strips(w_hbm, g_ref, ls_ref, p_ref, left_ref, right_ref, buf, w_ref, sems):
    rows, cols = ls_ref.shape
    chunks = sems.shape[0] - 1
    n = rows // chunks
    weights = pltpu.make_async_copy(w_hbm, w_ref, sems.at[chunks])
    weights.start()
    copies = [
        pltpu.make_async_copy(g_ref.at[:, pl.ds(i * n, n), :], buf.at[:, pl.ds(i * n, n), :], sems.at[i])
        for i in range(chunks)
    ]
    for copy in copies:
        copy.start()
    weights.wait()
    lane = lax.broadcasted_iota(jnp.int32, (LANES, LANES), 1)
    for i in range(rows // LANES):
        at = lanes_of(i)
        if i * LANES % n == 0:
            copies[i * LANES // n].wait()
        p_ref[at, :] = w_ref[0] * buf[0, at, :] + w_ref[1] * buf[1, at, :]
        first, last = slice(0, LANES), slice(cols - LANES, cols)
        packed = p_ref[at, first]
        for j, (ref, of) in enumerate(((ls_ref, first), (p_ref, last), (ls_ref, last)), 1):
            held = 0 if of.start == 0 else LANES - SIDE
            moved = pltpu.roll(ref[at, of], (j * SIDE - held) % LANES, 1)
            packed = jnp.where(lane < j * SIDE, packed, moved)
        turned_ = packed.T
        left_ref[:, at] = turned_[0 : 2 * SIDE, :]
        right_ref[:, at] = turned_[2 * SIDE : 4 * SIDE, :]


def turned(right, left):
    gap = jnp.zeros((LANES - 2 * SIDE, right.shape[1]), jnp.float32)
    return jnp.concatenate([right, gap, left], axis=0).T


def row_messages(f_ref, right_ref, left_ref, p_ref, ls_ref, fs_ref, m1_ref, m2_ref):
    rows, cols = ls_ref.shape
    f = f_ref[0]
    width = fs_ref.shape[1]
    theirs = pl.ds(aligned((1 - f) * (rows - width), LANES), width)
    fs_ref[0:SIDE, :] = right_ref[0:SIDE, theirs]
    fs_ref[SIDE:, :] = left_ref[0:SIDE, theirs]

    def corner(of, bottom):
        at = pl.ds(aligned(bottom * (rows - LANES), LANES), LANES)
        return turned(right_ref[of, at], left_ref[of, at])

    def ends(block, bottom):
        return jnp.where(bottom == 1, block[LANES - HALO :, :], block[0:HALO, :])

    outer, inner = 1 - f, f
    p_cols, ls_cols = slice(0, SIDE), slice(SIDE, 2 * SIDE)
    p_part, ls_part = slice(0, HALO), slice(HALO, 2 * HALO)
    at_outer = pl.ds(aligned(outer * (rows - HALO)), HALO)
    at_inner = pl.ds(aligned(inner * (rows - HALO)), HALO)
    m1_ref[p_part, 0:cols] = p_ref[at_outer, :]
    m1_ref[p_part, cols:] = ends(corner(p_cols, outer), outer)
    m1_ref[ls_part, 0:cols] = ls_ref[at_outer, :]
    m1_ref[ls_part, cols:] = ends(corner(ls_cols, outer), outer)
    m2_ref[:, 0:cols] = p_ref[at_inner, :]
    m2_ref[:, cols:] = ends(corner(p_cols, inner), inner)


def spread(nat, r, lo, width):
    return jnp.concatenate(
        [nat[c, pl.ds(lo, 8, stride=r), :] for c in range(width // LANES)], axis=1
    )


def unspread(nat, r, lo, value):
    for c in range(value.shape[1] // LANES):
        nat[c, pl.ds(lo, 8, stride=r), :] = value[:, lanes_of(c)]


def put(nat, rows, value, first=0):
    for c in range(value.shape[1] // LANES):
        nat[first + c, rows, :] = value[:, lanes_of(c)]


def half_setup(
    f_ref, p_ref, ls_ref, right_ref, left_ref, m1_ref, m2_ref, fs_ref,
    t_ref, q_ref, rec_ref, nat, lsx, pcol, lscol,
):
    rows, cols = ls_ref.shape
    f = f_ref[0]
    ext = lsx.shape[1]
    main = ext - HALO
    first = aligned((1 - f) * HALO)
    beside = pl.ds(aligned(f * main), HALO)
    put(nat, beside, m1_ref[0:HALO, :] + m2_ref[...])
    put(lsx, beside, m1_ref[HALO:, :])
    width = fs_ref.shape[1]
    skip = f * (width - main)
    lane0 = f * (rows - width)
    for i in range(width // LANES):
        at = pl.ds(aligned(lane0 + i * LANES, LANES), LANES)
        to = lanes_of(i)
        pcol[to, :] = turned(
            right_ref[0:SIDE, at] + fs_ref[0:SIDE, to], left_ref[0:SIDE, at] + fs_ref[SIDE:, to]
        )
        lscol[to, :] = turned(right_ref[SIDE:, at], left_ref[SIDE:, at])
    start = f * (rows - main)
    last = cols // LANES
    for i in range(main // 8):
        to = pl.ds(aligned(first + i * 8), 8)
        of = pl.ds(aligned(start + i * 8), 8)
        side = pl.ds(aligned(skip + i * 8), 8)
        put(nat, to, p_ref[of, :])
        put(lsx, to, ls_ref[of, :])
        nat[last, to, :] = pcol[side, :]
        lsx[last, to, :] = lscol[side, :]

    r = ext // 8
    for k in range(r):
        x = spread(lsx, r, k, cols + LANES) * (1.0 / band_cells)
        u = x * x
        q = 1.0 / (5.0 + 4.0 * u)
        q_ref[k] = q
        rec_ref[k] = (1.0 + u) * q
        t_ref[k] = spread(nat, r, k, cols + LANES)


def wrap(ref, r):
    ref[0] = pltpu.roll(ref[r], 1, 0)
    ref[r + 1] = pltpu.roll(ref[1], 7, 0)


def sweep(src, r, body, first=0):
    up, centre = src[first], src[first + 1]
    for k in range(first, r):
        down = src[k + 2]
        body(k, up, centre, down)
        up, centre = centre, down


def relaxed(a_ref, rec_ref, width):
    def relax(k, up, centre, down):
        beside = (up + down) + (pltpu.roll(centre, 1, 1) + pltpu.roll(centre, width - 1, 1))
        return a_ref[k] + rec_ref[k] * beside

    return relax


def add_part(t, part):
    cols = part.shape[1]
    return jnp.concatenate([t[:, 0:cols] + part, t[:, cols:]], axis=1)


def velocity_begun(t_ref, rp1_ref, q_ref, rec_ref, v0, v1, a_ref):
    n = rp1_ref.shape[0]
    for k in range(n):
        source = add_part(t_ref[k], rp1_ref[k])
        v0[k + 1] = source
        a_ref[k] = source * q_ref[k]
    relax = relaxed(a_ref, rec_ref, t_ref.shape[2])
    for level in range(1, EXT_SWEEPS + 1):
        src, dst = (v0, v1) if level % 2 else (v1, v0)

        def body(k, *cells):
            dst[k + 1] = relax(k, *cells)

        sweep(src, n - level, body, level)


def velocity_ended(
    f_ref, t_ref, rp1_ref, rp2_ref, q_ref, rec_ref, b0_ref, b1_ref, vs_hbm, early_ref, near_ref, top_ref,
    nat, a_ref, v0, v1, vs_ref, sems,
):
    n, _, cols = rp1_ref.shape
    r, _, width = t_ref.shape
    ext = 8 * r
    f = f_ref[0]
    group = r // sems.shape[0]
    copies = [
        pltpu.make_async_copy(vs_ref.at[pl.ds(i * group, group)], vs_hbm.at[pl.ds(i * group, group)], sems.at[i])
        for i in range(sems.shape[0])
    ]
    sub = lax.broadcasted_iota(jnp.int32, (8, cols), 0)
    tops = [jnp.zeros((8, cols), jnp.float32)] * 2
    done = set()

    def final(k, value):
        vs_ref[k] = value
        unspread(nat, r, k, value)
        done.add(k)
        i = k // group
        if all(i * group + j in done for j in range(group)):
            copies[i].start()
        size = jnp.abs(value[:, 0:cols])
        row = sub * r + k
        if k < HALO or 7 * r + k >= ext - HALO:
            size = jnp.where((row >= HALO) & (row < ext - HALO), size, 0.0)
        tops[k % 2] = jnp.maximum(tops[k % 2], size)

    edge = EXT_SWEEPS + 1
    for k in (*range(edge), *range(n - edge, n)):
        v0[k + 1] = b0_ref[k + 1]
        v1[k + 1] = b1_ref[k + 1]
    for k in (*range(EXT_SWEEPS), *range(n - EXT_SWEEPS, r)):
        source = add_part(t_ref[k], rp1_ref[k] if k < n else rp2_ref[k - n])
        a_ref[k] = source * q_ref[k]
        if k >= n:
            v0[k + 1] = source
    assert EXT_SWEEPS % 2 == 0
    for k in range(EXT_SWEEPS, n - EXT_SWEEPS):
        final(k, b0_ref[k + 1])
    wrap(v0, r)
    relax = relaxed(a_ref, rec_ref, width)
    for level in range(1, EXT_SWEEPS + 1):
        src, dst = (v0, v1) if level % 2 else (v1, v0)

        def body(k, *cells):
            value = relax(k, *cells)
            if level == EXT_SWEEPS:
                final(k, value)
            else:
                dst[k + 1] = value

        sweep(src, r, body, n - level)
        sweep(src, level, body)
        if level < EXT_SWEEPS:
            wrap(dst, r)
    near = near_ref.shape[0] - 2 * SIDE
    half = ext - 2 * HALO
    early = early_ref.shape[0]
    at_early = pl.ds(aligned(HALO + (1 - f) * (half - early)), early)
    at_near = pl.ds(aligned(HALO + (1 - f) * (half - early - near) + f * early), near)
    for c in range(cols // LANES):
        early_ref[:, lanes_of(c)] = nat[c, at_early, :]
        near_ref[0:near, lanes_of(c)] = nat[c, at_near, :]
    for i in range(half // LANES):
        side = nat[cols // LANES, HALO + i * LANES : HALO + (i + 1) * LANES, :].T
        near_ref[near : near + SIDE, lanes_of(i)] = side[0:SIDE, :]
        near_ref[near + SIDE :, lanes_of(i)] = side[LANES - SIDE :, :]
    for copy in copies:
        copy.wait()
    top_ref[...] = jnp.full(top_ref.shape, jnp.max(jnp.maximum(*tops)), jnp.float32)


def velocity_rows(f_ref, vs_hbm, early_ref, vx_hbm, far_hbm, vel_hbm, vs_ref, nat, sems):
    slabs, ext, _ = nat.shape
    last = slabs - 1
    r = ext // 8
    parts = 2
    group = r // parts
    used = iter(range(sems.shape[0]))

    def begin(src, dst):
        copy = pltpu.make_async_copy(src, dst, sems.at[next(used)])
        copy.start()
        return copy

    loads = [
        begin(vs_hbm.at[pl.ds(i * group, group)], vs_ref.at[pl.ds(i * group, group)]) for i in range(parts)
    ]
    for k in range(r):
        if k % group == 0:
            loads[k // group].wait()
        unspread(nat, r, k, vs_ref[k])
    far = far_hbm.shape[0]
    half = ext - 2 * HALO
    f = f_ref[0]
    at_far = pl.ds(aligned(HALO + f * (half - far)), far)
    lanes = [pl.ds(c * LANES, LANES) for c in range(last)]
    copies = [begin(nat.at[c, at_far, :], far_hbm.at[:, lanes[c]]) for c in range(last)]
    copies.append(begin(nat, vx_hbm))
    early = early_ref.shape[0]
    theirs = vel_hbm.at[pl.ds(aligned((1 - f) * half + f * (half - early)), early), :]
    copies.append(begin(early_ref, theirs))
    for c in range(last):
        mine = vel_hbm.at[pl.ds(aligned(f * half), half), lanes[c]]
        copies.append(begin(nat.at[c, pl.ds(HALO, half), :], mine))
    for copy in copies:
        copy.wait()


def speeds(sigma, centre, up, down, left, right):
    a = jnp.maximum(sigma * (centre - up), TINY)
    b = jnp.maximum(sigma * (centre - down), 0.0)
    c = jnp.maximum(sigma * (centre - left), 0.0)
    d = jnp.maximum(sigma * (centre - right), 0.0)
    return (a * a + b * b) + (c * c + d * d)


def reinit(top_ref, ls_nat, v_nat, base, r, out_nat, shift, p0, p1, h_ref, s_ref, width):
    step = cfl_number / (jnp.max(top_ref[...]) + 1e-06)
    for k in range(r):
        p0[k + 1] = spread(ls_nat, r, base + k, width)
    wrap(p0, r)

    def beside(centre):
        return pltpu.roll(centre, 1, 1), pltpu.roll(centre, width - 1, 1)

    def advance(k, up, centre, down):
        speed = spread(v_nat, r, base + k, width)
        sigma = jnp.where(speed >= 0.0, 1.0, -1.0)
        total = speeds(sigma, centre, up, down, *beside(centre))
        advanced = centre - step * (speed * (total * lax.rsqrt(total)))
        p1[k + 1] = advanced
        h_ref[k] = pseudo_step * (advanced * lax.rsqrt(advanced * advanced + 1.0))
        s_ref[k] = jnp.where(advanced >= 0.0, 1.0, -1.0)

    sweep(p0, r, advance)
    wrap(p1, r)

    def one(src, dst):
        def body(k, up, centre, down):
            total = speeds(s_ref[k], centre, up, down, *beside(centre))
            h = h_ref[k]
            dst[k + 1] = (centre + h) - h * (total * lax.rsqrt(total))

        sweep(src, r, body)
        wrap(dst, r)

    def pair(i, _):
        one(p1, p0)
        one(p0, p1)
        return 0

    assert REINIT_ITERS % 2 == 0
    lax.fori_loop(0, REINIT_ITERS // 2 - 1, pair, 0)
    one(p1, p0)
    cols = width - LANES

    def final(k, up, centre, down):
        left, right = beside(centre)
        c = centre[:, 0:cols]
        total = speeds(s_ref[k][:, 0:cols], c, up[:, 0:cols], down[:, 0:cols], left[:, 0:cols], right[:, 0:cols])
        h = h_ref[k][:, 0:cols]
        unspread(out_nat, r, k + shift, (c + h) - h * (total * lax.rsqrt(total)))

    sweep(p0, r, final)


def outer_part(
    f_ref, top_ref, ls_hbm, right_ref, left_ref, m1_ref, vx_hbm, out_ref,
    nat, lsn, vn, lscol, p0, p1, h_ref, s_ref, sems,
):
    n, cols = out_ref.shape
    rows = ls_hbm.shape[0]
    f = f_ref[0]
    staged = lsn.shape[1]
    last = cols // LANES
    inside = n + HALO
    first = aligned((1 - f) * HALO)
    start = aligned(f * (rows - inside))
    copies = [
        pltpu.make_async_copy(
            ls_hbm.at[pl.ds(start, inside), pl.ds(c * LANES, LANES)], lsn.at[c, pl.ds(first, inside), :], sems.at[c]
        )
        for c in range(last)
    ]
    from_ext = aligned(f * (vx_hbm.shape[1] - staged))
    copies.append(pltpu.make_async_copy(vx_hbm.at[:, pl.ds(from_ext, staged), :], vn, sems.at[last]))
    for copy in copies:
        copy.start()
    put(lsn, pl.ds(aligned(f * inside), HALO), m1_ref[HALO:, :])
    width = lscol.shape[0]
    for i in range(width // LANES):
        at = pl.ds(aligned(f * (rows - width) + i * LANES, LANES), LANES)
        lscol[lanes_of(i), :] = turned(right_ref[SIDE:, at], left_ref[SIDE:, at])
    lsn[last, pl.ds(first, inside), :] = lscol[pl.ds(aligned(f * (width - inside)), inside), :]
    for copy in copies:
        copy.wait()
    r = (n + 2 * EDGE) // 8
    reinit(top_ref, lsn, vn, HALO - EDGE, r, nat, STAGED - EDGE, p0, p1, h_ref, s_ref, cols + LANES)
    for c in range(last):
        out_ref[:, lanes_of(c)] = nat[c, STAGED : STAGED + n, :]


def middle_part(
    f_ref, top_ref, vx_hbm, early_ref, near_ref, ls_hbm, right_ref, left_ref, mine_ref, _, level_ref, vel_ref,
    nat, lsn, vn, p0, p1, h_ref, s_ref, sems,
):
    rows, cols = ls_hbm.shape
    f = f_ref[0]
    staged = lsn.shape[1]
    n = staged - 2 * STAGED
    r = (n + 2 * EDGE) // 8
    low = (rows - staged) // 2
    last = cols // LANES
    half = rows // 2
    cut = half - low
    near = near_ref.shape[0] - 2 * SIDE
    early = early_ref.shape[0]
    own = mine_ref.shape[0]
    used = iter(range(sems.shape[0]))

    def begin(src, dst):
        copy = pltpu.make_async_copy(src, dst, sems.at[next(used)])
        copy.start()
        return copy

    needed = [
        begin(
            vx_hbm.at[:, pl.ds(aligned(HALO + (1 - f) * low), cut), :],
            vn.at[:, pl.ds(aligned(f * cut), cut), :],
        )
    ]
    for c in range(last):
        needed.append(begin(ls_hbm.at[pl.ds(low, staged), pl.ds(c * LANES, LANES)], lsn.at[c]))
    ready = [
        begin(near_ref.at[pl.ds(0, near), :], vel_ref.at[pl.ds(aligned((1 - f) * (half + early) + f * low), near), :]),
        begin(mine_ref, level_ref.at[pl.ds(aligned(f * (rows - own)), own), :]),
    ]
    put(vn, pl.ds(aligned((1 - f) * cut + f * near), early), early_ref[...])
    put(vn, pl.ds(aligned((1 - f) * (cut + early)), near), near_ref[0:near, :])
    for i in range(rows // LANES):
        at = i * LANES
        first, end = max(at, low), min(at + LANES, low + staged)
        if first < end:
            block = turned(right_ref[SIDE:, at : at + LANES], left_ref[SIDE:, at : at + LANES])
            lsn[last, first - low : end - low, :] = block[first - at : end - at, :]
    for i in range(half // LANES):
        at = i * LANES
        block = turned(near_ref[near : near + SIDE, at : at + LANES], near_ref[near + SIDE :, at : at + LANES])

        @pl.when(f == 0)
        def _():
            end = min(at + LANES, staged - cut)
            if at < end:
                vn[last, cut + at : cut + end, :] = block[0 : end - at, :]

        @pl.when(f == 1)
        def _():
            first = max(at, low)
            if first < at + LANES:
                vn[last, first - low : at + LANES - low, :] = block[first - at :, :]

    for copy in needed:
        copy.wait()
    reinit(top_ref, lsn, vn, STAGED - EDGE, r, nat, STAGED - EDGE, p0, p1, h_ref, s_ref, cols + LANES)
    for c in range(last):
        ready.append(
            begin(nat.at[c, pl.ds(STAGED, n), :], level_ref.at[pl.ds(low + STAGED, n), pl.ds(c * LANES, LANES)])
        )
    for copy in ready:
        copy.wait()


def insert(f_ref, theirs_ref, far_ref, _, __, level_ref, vel_ref, sems):
    rows = level_ref.shape[0]
    n, far = theirs_ref.shape[0], far_ref.shape[0]
    f = f_ref[0]
    copies = [
        pltpu.make_async_copy(
            theirs_ref, level_ref.at[pl.ds(aligned((1 - f) * (rows - n)), n), :], sems.at[0]
        ),
        pltpu.make_async_copy(
            far_ref, vel_ref.at[pl.ds(aligned((1 - f) * (rows - far)), far), :], sems.at[1]
        ),
    ]
    for copy in copies:
        copy.start()
    for copy in copies:
        copy.wait()


def shifted(n, by):
    return [(i, (i + by) % n) for i in range(n)]


def per_device(level_set, focus_grads, focus_weight):
    rows, cols = level_set.shape
    half = rows // 2
    gx, gy = lax.axis_size("gx"), lax.axis_size("gy")
    f = lax.axis_index("focus").reshape(1).astype(jnp.int32)
    planes = focus_grads.shape[0]
    assert planes == 2 and lax.axis_size("focus") == 2
    swap = [(0, 1), (1, 0)]
    main, ext, wide = half + HALO, half + 2 * HALO, cols + LANES
    slabs = wide // LANES
    r = ext // 8
    part = r * FIRST_PARTS[0] // FIRST_PARTS[1]
    weights = pltpu.SMEM(focus_weight.shape, jnp.float32)

    (to_partner,) = call(
        send_part,
        [(part, 8, cols)],
        [SMEM, HBM, HBM],
        [vmem(planes, main, cols), vmem(slabs - 1, ext, LANES), weights, DMA((5,))],
        "send_part",
    )(f, focus_weight, focus_grads)
    from_partner = lax.ppermute(to_partner, "focus", swap)

    p, left, right = call(
        strips,
        [(rows, cols), (2 * SIDE, rows), (2 * SIDE, rows)],
        [HBM, HBM, VMEM],
        [vmem(planes, rows, cols), weights, DMA((5,))],
        "strips",
        mib=16,
        us=2,
    )(focus_weight, focus_grads, level_set)
    from_right = lax.ppermute(left, "gy", shifted(gy, -1))
    from_left = lax.ppermute(right, "gy", shifted(gy, 1))
    side = -(-main // LANES) * LANES
    fs, m1, m2 = call(
        row_messages,
        [(2 * SIDE, side), (2 * HALO, wide), (HALO, wide)],
        [SMEM, VMEM, VMEM, VMEM, VMEM],
        (),
        "row_messages",
    )(f, from_right, from_left, p, level_set)

    def place(f, x):
        return f * gx + x % gx

    same = [(place(0, x), place(0, x + 1)) for x in range(gx)] + [(place(1, x), place(1, x - 1)) for x in range(gx)]
    cross = [(place(0, x), place(1, x - 1)) for x in range(gx)] + [(place(1, x), place(0, x + 1)) for x in range(gx)]
    got1 = lax.ppermute(m1, ("focus", "gx"), same)
    got2 = lax.ppermute(m2, ("focus", "gx"), cross)
    got_fs = lax.ppermute(fs, "focus", swap)
    (to_partner2,) = call(
        lambda *refs: send_rest(main, *refs),
        [(r - part, 8, cols)],
        [SMEM, VMEM, VMEM],
        [vmem(slabs - 1, ext, LANES)],
        "send_rest",
    )(f, p, got2)
    from_partner2 = lax.ppermute(to_partner2, "focus", swap)
    t, q, rec = call(
        half_setup,
        [(r, 8, wide)] * 3,
        [SMEM] + [VMEM] * 7,
        [vmem(slabs, ext, LANES), vmem(slabs, ext, LANES), vmem(side, LANES), vmem(side, LANES)],
        "half_setup",
        us=2,
        mib=20,
    )(f, p, level_set, from_right, from_left, got1, got2, got_fs)
    devices = 2 * gx * gy
    own = rows * OWN_PARTS[0] // OWN_PARTS[1]
    far = own - STAGED
    near = half - far - EARLY
    b0, b1 = call(
        velocity_begun,
        [(r + 2, 8, wide)] * 2,
        [VMEM] * 4,
        [vmem(part, 8, wide)],
        "velocity_begun",
        us=4,
    )(t, from_partner, q, rec)
    vs, to_early, to_near, top = call(
        velocity_ended,
        [(r, 8, wide), (EARLY, cols), (near + 2 * SIDE, cols), (devices, LANES)],
        [SMEM] + [VMEM] * 7,
        [
            vmem(slabs, ext, LANES), vmem(r, 8, wide), vmem(r + 2, 8, wide), vmem(r + 2, 8, wide),
            vmem(r, 8, wide), DMA((7,)),
        ],
        "velocity_ended",
        us=5,
        out_specs=[HBM, VMEM, VMEM, VMEM],
        mib=24,
    )(f, t, from_partner, from_partner2, q, rec, b0, b1)
    got_early = lax.ppermute(to_early, "focus", swap)
    tops = lax.all_to_all(top, ("focus", "gx", "gy"), 0, 0)
    got_near = lax.ppermute(to_near, "focus", swap)
    vx, to_far, velocity = call(
        velocity_rows,
        [(slabs, ext, LANES), (far, cols), (rows, cols)],
        [SMEM, HBM, VMEM],
        [vmem(r, 8, wide), vmem(slabs, ext, LANES), DMA((2 * slabs + 2,))],
        "velocity_rows",
        us=60,
        out_specs=[HBM, HBM, HBM],
    )(f, vs, got_early)
    got_far = lax.ppermute(to_far, "focus", swap)

    def work(n):
        r = (n + 2 * EDGE) // 8
        return [vmem(r + 2, 8, wide)] * 2 + [vmem(r, 8, wide)] * 2

    staged = own + 2 * HALO
    (mine,) = call(
        outer_part,
        [(own, cols)],
        [SMEM, VMEM, HBM, VMEM, VMEM, VMEM, HBM],
        [vmem(slabs - 1, own + 2 * STAGED, LANES), vmem(slabs, staged, LANES), vmem(slabs, staged, LANES)]
        + [vmem(-(-(own + HALO) // LANES) * LANES, LANES)]
        + work(own)
        + [DMA((slabs,))],
        "outer_part",
        us=8,
    )(f, tops, level_set, from_right, from_left, got1, vx)
    theirs = lax.ppermute(mine, "focus", swap)
    mid = rows - 2 * own
    staged = mid + 2 * STAGED
    level, velocity = call(
        middle_part,
        [(rows, cols), (rows, cols)],
        [SMEM, VMEM, HBM, VMEM, VMEM, HBM, VMEM, VMEM, VMEM, HBM],
        [vmem(slabs - 1, staged, LANES), vmem(slabs, staged, LANES), vmem(slabs, staged, LANES)]
        + work(mid)
        + [DMA((2 * slabs + 1,))],
        "middle_part",
        us=20,
        out_specs=[HBM, HBM],
        aliases={9: 1},
        mib=20,
    )(f, tops, vx, got_early, got_near, level_set, from_right, from_left, mine, velocity)
    level, velocity = call(
        insert,
        [(rows, cols), (rows, cols)],
        [SMEM, VMEM, VMEM, HBM, HBM],
        [DMA((2,))],
        "insert",
        out_specs=[HBM, HBM],
        aliases={3: 0, 4: 1},
    )(f, theirs, got_far, level, velocity)
    return level, velocity


def solution(mesh):
    in_specs = (P("gx", "gy"), P("focus", "gx", "gy"), P("focus"))
    out_specs = (P("gx", "gy"), P("gx", "gy"))
    return jax.shard_map(
        per_device, mesh=mesh, in_specs=in_specs, out_specs=out_specs, check_vma=False
    )
```

```python
import jax
import jax.numpy as jnp
from jax import lax
from jax.experimental import pallas as pl
from jax.experimental.pallas import tpu as pltpu
from jax.sharding import PartitionSpec as P

EXT_SWEEPS = 8
REINIT_ITERS = 10
band_cells = 3.0
cfl_number = 0.5
pseudo_step = 0.5

HALO = 24
SIDE = 20
EDGE = 12
STAGED = 16
OWN_PARTS = (1, 4)
FIRST_PARTS = (27, 35)
EARLY = 208
LANES = 128
TINY = 1e-18

VMEM = pl.BlockSpec(memory_space=pltpu.VMEM)
SMEM = pl.BlockSpec(memory_space=pltpu.SMEM)
HBM = pl.BlockSpec(memory_space=pl.ANY)
DMA = pltpu.SemaphoreType.DMA


def vmem(*shape):
    return pltpu.VMEM(shape, jnp.float32)


def call(body, out_shapes, in_specs, scratch=(), name=None, out_specs=None, aliases=None, mib=16, us=1):
    out_specs = out_specs or [VMEM] * len(out_shapes)
    outs = [
        pltpu.HBM(s, jnp.float32) if spec is HBM else jax.ShapeDtypeStruct(s, jnp.float32)
        for s, spec in zip(out_shapes, out_specs)
    ]
    kernel = pl.pallas_call(
        body,
        out_shape=outs,
        in_specs=in_specs,
        out_specs=out_specs,
        scratch_shapes=list(scratch),
        name=name,
        input_output_aliases=aliases or {},
        compiler_params=pltpu.CompilerParams(vmem_limit_bytes=mib << 20),
        cost_estimate=pl.CostEstimate(flops=int(us * 1e9), bytes_accessed=0, transcendentals=0),
    )

    def run(*args):
        return kernel(
            *(pltpu.with_memory_space_constraint(x, pltpu.HBM) if spec is HBM else x for x, spec in zip(args, in_specs))
        )

    return run


def aligned(x, n=8):
    return pl.multiple_of(x, n)


def lanes_of(c):
    return slice(c * LANES, (c + 1) * LANES)


def blank(nat, f, main):
    for c in range(nat.shape[0]):
        nat[c, pl.ds(aligned(f * main), HALO), :] = jnp.zeros((HALO, LANES), jnp.float32)


def send_part(f_ref, w_hbm, g_ref, send_ref, buf, nat, w_ref, sems):
    n, main, cols = send_ref.shape[0], buf.shape[1], buf.shape[2]
    f = f_ref[0]
    start = (1 - f) * (g_ref.shape[1] - main)
    chunks = sems.shape[0] - 1
    weights = pltpu.make_async_copy(w_hbm, w_ref, sems.at[chunks])
    weights.start()
    step = main // 8 // chunks * 8
    spans = [(i * step, step if i < chunks - 1 else main - i * step) for i in range(chunks)]
    copies = [
        pltpu.make_async_copy(
            g_ref.at[:, pl.ds(aligned(start + at), n), :], buf.at[:, pl.ds(at, n), :], sems.at[i]
        )
        for i, (at, n) in enumerate(spans)
    ]
    for copy in copies:
        copy.start()
    blank(nat, 1 - f, main)
    weights.wait()
    for copy, (at, rows) in zip(copies, spans):
        copy.wait()
        part = w_ref[0] * buf[0, at : at + rows, :] + w_ref[1] * buf[1, at : at + rows, :]
        put(nat, pl.ds(aligned(f * HALO + at), rows), part)
    for k in range(n):
        send_ref[k] = spread(nat, nat.shape[1] // 8, k, cols)


def send_rest(main, f_ref, p_ref, _, send_ref, nat):
    rows, cols = p_ref.shape
    f = f_ref[0]
    r = nat.shape[1] // 8
    blank(nat, 1 - f, main)
    put(nat, pl.ds(aligned(f * HALO), main), p_ref[pl.ds(aligned((1 - f) * (rows - main)), main), :])
    for k in range(send_ref.shape[0]):
        send_ref[k] = spread(nat, r, r - send_ref.shape[0] + k, cols)


def strips(w_hbm, g_ref, ls_ref, p_ref, left_ref, right_ref, buf, w_ref, sems):
    rows, cols = ls_ref.shape
    chunks = sems.shape[0] - 1
    n = rows // chunks
    weights = pltpu.make_async_copy(w_hbm, w_ref, sems.at[chunks])
    weights.start()
    copies = [
        pltpu.make_async_copy(g_ref.at[:, pl.ds(i * n, n), :], buf.at[:, pl.ds(i * n, n), :], sems.at[i])
        for i in range(chunks)
    ]
    for copy in copies:
        copy.start()
    weights.wait()
    lane = lax.broadcasted_iota(jnp.int32, (LANES, LANES), 1)
    for i in range(rows // LANES):
        at = lanes_of(i)
        if i * LANES % n == 0:
            copies[i * LANES // n].wait()
        p_ref[at, :] = w_ref[0] * buf[0, at, :] + w_ref[1] * buf[1, at, :]
        first, last = slice(0, LANES), slice(cols - LANES, cols)
        packed = p_ref[at, first]
        for j, (ref, of) in enumerate(((ls_ref, first), (p_ref, last), (ls_ref, last)), 1):
            held = 0 if of.start == 0 else LANES - SIDE
            moved = pltpu.roll(ref[at, of], (j * SIDE - held) % LANES, 1)
            packed = jnp.where(lane < j * SIDE, packed, moved)
        turned_ = packed.T
        left_ref[:, at] = turned_[0 : 2 * SIDE, :]
        right_ref[:, at] = turned_[2 * SIDE : 4 * SIDE, :]


def turned(right, left):
    gap = jnp.zeros((LANES - 2 * SIDE, right.shape[1]), jnp.float32)
    return jnp.concatenate([right, gap, left], axis=0).T


def row_messages(f_ref, right_ref, left_ref, p_ref, ls_ref, fs_ref, m1_ref, m2_ref):
    rows, cols = ls_ref.shape
    f = f_ref[0]
    width = fs_ref.shape[1]
    theirs = pl.ds(aligned((1 - f) * (rows - width), LANES), width)
    fs_ref[0:SIDE, :] = right_ref[0:SIDE, theirs]
    fs_ref[SIDE:, :] = left_ref[0:SIDE, theirs]

    def corner(of, bottom):
        at = pl.ds(aligned(bottom * (rows - LANES), LANES), LANES)
        return turned(right_ref[of, at], left_ref[of, at])

    def ends(block, bottom):
        return jnp.where(bottom == 1, block[LANES - HALO :, :], block[0:HALO, :])

    outer, inner = 1 - f, f
    p_cols, ls_cols = slice(0, SIDE), slice(SIDE, 2 * SIDE)
    p_part, ls_part = slice(0, HALO), slice(HALO, 2 * HALO)
    at_outer = pl.ds(aligned(outer * (rows - HALO)), HALO)
    at_inner = pl.ds(aligned(inner * (rows - HALO)), HALO)
    m1_ref[p_part, 0:cols] = p_ref[at_outer, :]
    m1_ref[p_part, cols:] = ends(corner(p_cols, outer), outer)
    m1_ref[ls_part, 0:cols] = ls_ref[at_outer, :]
    m1_ref[ls_part, cols:] = ends(corner(ls_cols, outer), outer)
    m2_ref[:, 0:cols] = p_ref[at_inner, :]
    m2_ref[:, cols:] = ends(corner(p_cols, inner), inner)


def spread(nat, r, lo, width):
    return jnp.concatenate(
        [nat[c, pl.ds(lo, 8, stride=r), :] for c in range(width // LANES)], axis=1
    )


def unspread(nat, r, lo, value):
    for c in range(value.shape[1] // LANES):
        nat[c, pl.ds(lo, 8, stride=r), :] = value[:, lanes_of(c)]


def put(nat, rows, value, first=0):
    for c in range(value.shape[1] // LANES):
        nat[first + c, rows, :] = value[:, lanes_of(c)]


def half_setup(
    f_ref, p_ref, ls_ref, right_ref, left_ref, m1_ref, m2_ref, fs_ref,
    t_ref, q_ref, rec_ref, nat, lsx, pcol, lscol,
):
    rows, cols = ls_ref.shape
    f = f_ref[0]
    ext = lsx.shape[1]
    main = ext - HALO
    first = aligned((1 - f) * HALO)
    beside = pl.ds(aligned(f * main), HALO)
    put(nat, beside, m1_ref[0:HALO, :] + m2_ref[...])
    put(lsx, beside, m1_ref[HALO:, :])
    width = fs_ref.shape[1]
    skip = f * (width - main)
    lane0 = f * (rows - width)
    for i in range(width // LANES):
        at = pl.ds(aligned(lane0 + i * LANES, LANES), LANES)
        to = lanes_of(i)
        pcol[to, :] = turned(
            right_ref[0:SIDE, at] + fs_ref[0:SIDE, to], left_ref[0:SIDE, at] + fs_ref[SIDE:, to]
        )
        lscol[to, :] = turned(right_ref[SIDE:, at], left_ref[SIDE:, at])
    start = f * (rows - main)
    last = cols // LANES
    for i in range(main // 8):
        to = pl.ds(aligned(first + i * 8), 8)
        of = pl.ds(aligned(start + i * 8), 8)
        side = pl.ds(aligned(skip + i * 8), 8)
        put(nat, to, p_ref[of, :])
        put(lsx, to, ls_ref[of, :])
        nat[last, to, :] = pcol[side, :]
        lsx[last, to, :] = lscol[side, :]

    r = ext // 8
    for k in range(r):
        x = spread(lsx, r, k, cols + LANES) * (1.0 / band_cells)
        u = x * x
        q = 1.0 / (5.0 + 4.0 * u)
        q_ref[k] = q
        rec_ref[k] = (1.0 + u) * q
        t_ref[k] = spread(nat, r, k, cols + LANES)


def wrap(ref, r):
    ref[0] = pltpu.roll(ref[r], 1, 0)
    ref[r + 1] = pltpu.roll(ref[1], 7, 0)


def sweep(src, r, body, first=0):
    up, centre = src[first], src[first + 1]
    for k in range(first, r):
        down = src[k + 2]
        body(k, up, centre, down)
        up, centre = centre, down


def relaxed(a_ref, rec_ref, width):
    def relax(k, up, centre, down):
        beside = (up + down) + (pltpu.roll(centre, 1, 1) + pltpu.roll(centre, width - 1, 1))
        return a_ref[k] + rec_ref[k] * beside

    return relax


def add_part(t, part):
    cols = part.shape[1]
    return jnp.concatenate([t[:, 0:cols] + part, t[:, cols:]], axis=1)


def velocity_begun(t_ref, rp1_ref, q_ref, rec_ref, v0, v1, a_ref):
    n = rp1_ref.shape[0]
    for k in range(n):
        source = add_part(t_ref[k], rp1_ref[k])
        v0[k + 1] = source
        a_ref[k] = source * q_ref[k]
    relax = relaxed(a_ref, rec_ref, t_ref.shape[2])
    for level in range(1, EXT_SWEEPS + 1):
        src, dst = (v0, v1) if level % 2 else (v1, v0)

        def body(k, *cells):
            dst[k + 1] = relax(k, *cells)

        sweep(src, n - level, body, level)


def velocity_ended(
    f_ref, t_ref, rp1_ref, rp2_ref, q_ref, rec_ref, b0_ref, b1_ref, vs_hbm, early_ref, near_ref, top_ref,
    nat, a_ref, v0, v1, vs_ref, sems,
):
    n, _, cols = rp1_ref.shape
    r, _, width = t_ref.shape
    ext = 8 * r
    f = f_ref[0]
    group = r // sems.shape[0]
    copies = [
        pltpu.make_async_copy(vs_ref.at[pl.ds(i * group, group)], vs_hbm.at[pl.ds(i * group, group)], sems.at[i])
        for i in range(sems.shape[0])
    ]
    sub = lax.broadcasted_iota(jnp.int32, (8, cols), 0)
    tops = [jnp.zeros((8, cols), jnp.float32)] * 2
    done = set()

    def final(k, value):
        vs_ref[k] = value
        unspread(nat, r, k, value)
        done.add(k)
        i = k // group
        if all(i * group + j in done for j in range(group)):
            copies[i].start()
        size = jnp.abs(value[:, 0:cols])
        row = sub * r + k
        if k < HALO or 7 * r + k >= ext - HALO:
            size = jnp.where((row >= HALO) & (row < ext - HALO), size, 0.0)
        tops[k % 2] = jnp.maximum(tops[k % 2], size)

    edge = EXT_SWEEPS + 1
    for k in (*range(edge), *range(n - edge, n)):
        v0[k + 1] = b0_ref[k + 1]
        v1[k + 1] = b1_ref[k + 1]
    for k in (*range(EXT_SWEEPS), *range(n - EXT_SWEEPS, r)):
        source = add_part(t_ref[k], rp1_ref[k] if k < n else rp2_ref[k - n])
        a_ref[k] = source * q_ref[k]
        if k >= n:
            v0[k + 1] = source
    assert EXT_SWEEPS % 2 == 0
    for k in range(EXT_SWEEPS, n - EXT_SWEEPS):
        final(k, b0_ref[k + 1])
    wrap(v0, r)
    relax = relaxed(a_ref, rec_ref, width)
    for level in range(1, EXT_SWEEPS + 1):
        src, dst = (v0, v1) if level % 2 else (v1, v0)

        def body(k, *cells):
            value = relax(k, *cells)
            if level == EXT_SWEEPS:
                final(k, value)
            else:
                dst[k + 1] = value

        sweep(src, r, body, n - level)
        sweep(src, level, body)
        if level < EXT_SWEEPS:
            wrap(dst, r)
    near = near_ref.shape[0] - 2 * SIDE
    half = ext - 2 * HALO
    early = early_ref.shape[0]
    at_early = pl.ds(aligned(HALO + (1 - f) * (half - early)), early)
    at_near = pl.ds(aligned(HALO + (1 - f) * (half - early - near) + f * early), near)
    for c in range(cols // LANES):
        early_ref[:, lanes_of(c)] = nat[c, at_early, :]
        near_ref[0:near, lanes_of(c)] = nat[c, at_near, :]
    for i in range(half // LANES):
        side = nat[cols // LANES, HALO + i * LANES : HALO + (i + 1) * LANES, :].T
        near_ref[near : near + SIDE, lanes_of(i)] = side[0:SIDE, :]
        near_ref[near + SIDE :, lanes_of(i)] = side[LANES - SIDE :, :]
    top_ref[...] = jnp.full(top_ref.shape, jnp.max(jnp.maximum(*tops)), jnp.float32)
    for copy in copies:
        copy.wait()


def velocity_rows(f_ref, vs_hbm, early_ref, vx_hbm, far_hbm, vel_hbm, vs_ref, nat, sems):
    slabs, ext, _ = nat.shape
    last = slabs - 1
    r = ext // 8
    parts = 2
    group = r // parts
    used = iter(range(sems.shape[0]))

    def begin(src, dst):
        copy = pltpu.make_async_copy(src, dst, sems.at[next(used)])
        copy.start()
        return copy

    loads = [
        begin(vs_hbm.at[pl.ds(i * group, group)], vs_ref.at[pl.ds(i * group, group)]) for i in range(parts)
    ]
    for k in range(r):
        if k % group == 0:
            loads[k // group].wait()
        unspread(nat, r, k, vs_ref[k])
    far = far_hbm.shape[0]
    half = ext - 2 * HALO
    f = f_ref[0]
    at_far = pl.ds(aligned(HALO + f * (half - far)), far)
    lanes = [pl.ds(c * LANES, LANES) for c in range(last)]
    copies = [begin(nat.at[c, at_far, :], far_hbm.at[:, lanes[c]]) for c in range(last)]
    copies.append(begin(nat, vx_hbm))
    early = early_ref.shape[0]
    theirs = vel_hbm.at[pl.ds(aligned((1 - f) * half + f * (half - early)), early), :]
    copies.append(begin(early_ref, theirs))
    for c in range(last):
        mine = vel_hbm.at[pl.ds(aligned(f * half), half), lanes[c]]
        copies.append(begin(nat.at[c, pl.ds(HALO, half), :], mine))
    for copy in copies:
        copy.wait()


def speeds(sigma, above, below, before, after):
    a = jnp.maximum(sigma * above, TINY)
    b = jnp.minimum(sigma * below, 0.0)
    c = jnp.maximum(sigma * before, 0.0)
    d = jnp.minimum(sigma * after, 0.0)
    return (a * a + b * b) + (c * c + d * d)


def differences(src, r, width, body):
    centre = src[1]
    above = centre - src[0]
    for k in range(r):
        down = src[k + 2]
        below = down - centre
        before = centre - pltpu.roll(centre, 1, 1)
        after = pltpu.roll(centre, width - 1, 1) - centre
        body(k, centre, above, below, before, after)
        centre, above = down, below


def reinit(top_ref, ls_nat, v_nat, base, r, out_nat, shift, p0, p1, h_ref, s_ref, width, coming=(), later=()):
    step = cfl_number / (jnp.max(top_ref[...]) + 1e-06)
    for k in range(r):
        p0[k + 1] = spread(ls_nat, r, base + k, width)
    wrap(p0, r)
    for copy in coming:
        copy.wait()
    for copy in later:
        copy.start()

    def advance(k, centre, *steps):
        speed = spread(v_nat, r, base + k, width)
        sigma = jnp.where(speed >= 0.0, 1.0, -1.0)
        total = speeds(sigma, *steps)
        advanced = centre - step * (speed * (total * lax.rsqrt(total)))
        p1[k + 1] = advanced
        h_ref[k] = pseudo_step * (advanced * lax.rsqrt(advanced * advanced + 1.0))
        s_ref[k] = jnp.where(advanced >= 0.0, 1.0, -1.0)

    differences(p0, r, width, advance)
    wrap(p1, r)

    def one(src, dst):
        def body(k, centre, *steps):
            total = speeds(s_ref[k], *steps)
            h = h_ref[k]
            dst[k + 1] = (centre + h) - h * (total * lax.rsqrt(total))

        differences(src, r, width, body)
        wrap(dst, r)

    def pair(i, _):
        one(p1, p0)
        one(p0, p1)
        return 0

    assert REINIT_ITERS % 2 == 0
    lax.fori_loop(0, REINIT_ITERS // 2 - 1, pair, 0)
    one(p1, p0)
    cols = width - LANES

    def final(k, centre, *steps):
        total = speeds(s_ref[k][:, 0:cols], *(x[:, 0:cols] for x in steps))
        h = h_ref[k][:, 0:cols]
        unspread(out_nat, r, k + shift, (centre[:, 0:cols] + h) - h * (total * lax.rsqrt(total)))

    differences(p0, r, width, final)


def outer_part(
    f_ref, top_ref, ls_hbm, right_ref, left_ref, m1_ref, vx_hbm, out_ref, lsm_ref, vm_ref,
    nat, lsn, vn, lscol, p0, p1, h_ref, s_ref, sems,
):
    n, cols = out_ref.shape
    rows = ls_hbm.shape[0]
    f = f_ref[0]
    staged = lsn.shape[1]
    last = cols // LANES
    inside = n + HALO
    first = aligned((1 - f) * HALO)
    start = aligned(f * (rows - inside))
    copies = [
        pltpu.make_async_copy(
            ls_hbm.at[pl.ds(start, inside), pl.ds(c * LANES, LANES)], lsn.at[c, pl.ds(first, inside), :], sems.at[c]
        )
        for c in range(last)
    ]
    from_ext = aligned(f * (vx_hbm.shape[1] - staged))
    copies.append(pltpu.make_async_copy(vx_hbm.at[:, pl.ds(from_ext, staged), :], vn, sems.at[last]))
    for copy in copies:
        copy.start()
    middle, cut = lsm_ref.shape[1], vm_ref.shape[1]
    low = (rows - middle) // 2
    later = [
        pltpu.make_async_copy(
            ls_hbm.at[pl.ds(low, middle), pl.ds(c * LANES, LANES)], lsm_ref.at[c], sems.at[last + 1 + c]
        )
        for c in range(last)
    ]
    later.append(
        pltpu.make_async_copy(
            vx_hbm.at[:, pl.ds(aligned(HALO + (1 - f) * low), cut), :], vm_ref, sems.at[2 * last + 1]
        )
    )
    put(lsn, pl.ds(aligned(f * inside), HALO), m1_ref[HALO:, :])
    width = lscol.shape[0]
    for i in range(width // LANES):
        at = pl.ds(aligned(f * (rows - width) + i * LANES, LANES), LANES)
        lscol[lanes_of(i), :] = turned(right_ref[SIDE:, at], left_ref[SIDE:, at])
    lsn[last, pl.ds(first, inside), :] = lscol[pl.ds(aligned(f * (width - inside)), inside), :]
    for copy in copies[:last]:
        copy.wait()
    r = (n + 2 * EDGE) // 8
    reinit(
        top_ref, lsn, vn, HALO - EDGE, r, nat, STAGED - EDGE, p0, p1, h_ref, s_ref, cols + LANES,
        copies[last:], later,
    )
    for c in range(last):
        out_ref[:, lanes_of(c)] = nat[c, STAGED : STAGED + n, :]
    for i in range(rows // LANES):
        at = i * LANES
        first, end = max(at, low), min(at + LANES, low + middle)
        if first < end:
            block = turned(right_ref[SIDE:, at : at + LANES], left_ref[SIDE:, at : at + LANES])
            lsm_ref[last, first - low : end - low, :] = block[first - at : end - at, :]
    for copy in later:
        copy.wait()


def middle_part(
    f_ref, top_ref, vm_ref, early_ref, near_ref, lsn, mine_ref, _, level_ref, vel_ref,
    nat, vn, p0, p1, h_ref, s_ref, sems,
):
    rows, cols = level_ref.shape
    f = f_ref[0]
    staged = lsn.shape[1]
    n = staged - 2 * STAGED
    r = (n + 2 * EDGE) // 8
    low = (rows - staged) // 2
    last = cols // LANES
    half = rows // 2
    cut = half - low
    near = near_ref.shape[0] - 2 * SIDE
    early = early_ref.shape[0]
    own = mine_ref.shape[0]
    used = iter(range(sems.shape[0]))

    def begin(src, dst):
        copy = pltpu.make_async_copy(src, dst, sems.at[next(used)])
        copy.start()
        return copy

    ready = [
        begin(near_ref.at[pl.ds(0, near), :], vel_ref.at[pl.ds(aligned((1 - f) * (half + early) + f * low), near), :]),
        begin(mine_ref, level_ref.at[pl.ds(aligned(f * (rows - own)), own), :]),
    ]
    for c in range(last + 1):
        vn[c, pl.ds(aligned(f * cut), cut), :] = vm_ref[c]
    put(vn, pl.ds(aligned((1 - f) * cut + f * near), early), early_ref[...])
    put(vn, pl.ds(aligned((1 - f) * (cut + early)), near), near_ref[0:near, :])
    for i in range(half // LANES):
        at = i * LANES
        block = turned(near_ref[near : near + SIDE, at : at + LANES], near_ref[near + SIDE :, at : at + LANES])

        @pl.when(f == 0)
        def _():
            end = min(at + LANES, staged - cut)
            if at < end:
                vn[last, cut + at : cut + end, :] = block[0 : end - at, :]

        @pl.when(f == 1)
        def _():
            first = max(at, low)
            if first < at + LANES:
                vn[last, first - low : at + LANES - low, :] = block[first - at :, :]

    reinit(top_ref, lsn, vn, STAGED - EDGE, r, nat, STAGED - EDGE, p0, p1, h_ref, s_ref, cols + LANES)
    for c in range(last):
        ready.append(
            begin(nat.at[c, pl.ds(STAGED, n), :], level_ref.at[pl.ds(low + STAGED, n), pl.ds(c * LANES, LANES)])
        )
    for copy in ready:
        copy.wait()


def insert(f_ref, theirs_ref, far_ref, _, __, level_ref, vel_ref, sems):
    rows = level_ref.shape[0]
    n, far = theirs_ref.shape[0], far_ref.shape[0]
    f = f_ref[0]
    copies = [
        pltpu.make_async_copy(
            theirs_ref, level_ref.at[pl.ds(aligned((1 - f) * (rows - n)), n), :], sems.at[0]
        ),
        pltpu.make_async_copy(
            far_ref, vel_ref.at[pl.ds(aligned((1 - f) * (rows - far)), far), :], sems.at[1]
        ),
    ]
    for copy in copies:
        copy.start()
    for copy in copies:
        copy.wait()


def shifted(n, by):
    return [(i, (i + by) % n) for i in range(n)]


def per_device(level_set, focus_grads, focus_weight):
    rows, cols = level_set.shape
    half = rows // 2
    gx, gy = lax.axis_size("gx"), lax.axis_size("gy")
    f = lax.axis_index("focus").reshape(1).astype(jnp.int32)
    planes = focus_grads.shape[0]
    assert planes == 2 and lax.axis_size("focus") == 2
    swap = [(0, 1), (1, 0)]
    main, ext, wide = half + HALO, half + 2 * HALO, cols + LANES
    slabs = wide // LANES
    r = ext // 8
    part = r * FIRST_PARTS[0] // FIRST_PARTS[1]
    weights = pltpu.SMEM(focus_weight.shape, jnp.float32)

    (to_partner,) = call(
        send_part,
        [(part, 8, cols)],
        [SMEM, HBM, HBM],
        [vmem(planes, main, cols), vmem(slabs - 1, ext, LANES), weights, DMA((9,))],
        "send_part",
    )(f, focus_weight, focus_grads)
    from_partner = lax.ppermute(to_partner, "focus", swap)

    p, left, right = call(
        strips,
        [(rows, cols), (2 * SIDE, rows), (2 * SIDE, rows)],
        [HBM, HBM, VMEM],
        [vmem(planes, rows, cols), weights, DMA((5,))],
        "strips",
        mib=16,
        us=2,
    )(focus_weight, focus_grads, level_set)
    from_right = lax.ppermute(left, "gy", shifted(gy, -1))
    from_left = lax.ppermute(right, "gy", shifted(gy, 1))
    side = -(-main // LANES) * LANES
    fs, m1, m2 = call(
        row_messages,
        [(2 * SIDE, side), (2 * HALO, wide), (HALO, wide)],
        [SMEM, VMEM, VMEM, VMEM, VMEM],
        (),
        "row_messages",
    )(f, from_right, from_left, p, level_set)

    def place(f, x):
        return f * gx + x % gx

    same = [(place(0, x), place(0, x + 1)) for x in range(gx)] + [(place(1, x), place(1, x - 1)) for x in range(gx)]
    cross = [(place(0, x), place(1, x - 1)) for x in range(gx)] + [(place(1, x), place(0, x + 1)) for x in range(gx)]
    got1 = lax.ppermute(m1, ("focus", "gx"), same)
    got2 = lax.ppermute(m2, ("focus", "gx"), cross)
    got_fs = lax.ppermute(fs, "focus", swap)
    (to_partner2,) = call(
        lambda *refs: send_rest(main, *refs),
        [(r - part, 8, cols)],
        [SMEM, VMEM, VMEM],
        [vmem(slabs - 1, ext, LANES)],
        "send_rest",
    )(f, p, got2)
    from_partner2 = lax.ppermute(to_partner2, "focus", swap)
    t, q, rec = call(
        half_setup,
        [(r, 8, wide)] * 3,
        [SMEM] + [VMEM] * 7,
        [vmem(slabs, ext, LANES), vmem(slabs, ext, LANES), vmem(side, LANES), vmem(side, LANES)],
        "half_setup",
        us=2,
        mib=20,
    )(f, p, level_set, from_right, from_left, got1, got2, got_fs)
    devices = 2 * gx * gy
    own = rows * OWN_PARTS[0] // OWN_PARTS[1]
    far = own - STAGED
    near = half - far - EARLY
    b0, b1 = call(
        velocity_begun,
        [(r + 2, 8, wide)] * 2,
        [VMEM] * 4,
        [vmem(part, 8, wide)],
        "velocity_begun",
        us=4,
    )(t, from_partner, q, rec)
    vs, to_early, to_near, top = call(
        velocity_ended,
        [(r, 8, wide), (EARLY, cols), (near + 2 * SIDE, cols), (devices, LANES)],
        [SMEM] + [VMEM] * 7,
        [
            vmem(slabs, ext, LANES), vmem(r, 8, wide), vmem(r + 2, 8, wide), vmem(r + 2, 8, wide),
            vmem(r, 8, wide), DMA((7,)),
        ],
        "velocity_ended",
        us=5,
        out_specs=[HBM, VMEM, VMEM, VMEM],
        mib=24,
    )(f, t, from_partner, from_partner2, q, rec, b0, b1)
    got_early = lax.ppermute(to_early, "focus", swap)
    tops = lax.all_to_all(top, ("focus", "gx", "gy"), 0, 0)
    got_near = lax.ppermute(to_near, "focus", swap)
    vx, to_far, velocity = call(
        velocity_rows,
        [(slabs, ext, LANES), (far, cols), (rows, cols)],
        [SMEM, HBM, VMEM],
        [vmem(r, 8, wide), vmem(slabs, ext, LANES), DMA((2 * slabs + 2,))],
        "velocity_rows",
        us=60,
        out_specs=[HBM, HBM, HBM],
    )(f, vs, got_early)
    got_far = lax.ppermute(to_far, "focus", swap)

    def work(n):
        r = (n + 2 * EDGE) // 8
        return [vmem(r + 2, 8, wide)] * 2 + [vmem(r, 8, wide)] * 2

    staged = own + 2 * HALO
    mid = rows - 2 * own
    middle = mid + 2 * STAGED
    mine, ls_mid, v_mid = call(
        outer_part,
        [(own, cols), (slabs, middle, LANES), (slabs, middle // 2, LANES)],
        [SMEM, VMEM, HBM, VMEM, VMEM, VMEM, HBM],
        [vmem(slabs - 1, own + 2 * STAGED, LANES), vmem(slabs, staged, LANES), vmem(slabs, staged, LANES)]
        + [vmem(-(-(own + HALO) // LANES) * LANES, LANES)]
        + work(own)
        + [DMA((2 * slabs,))],
        "outer_part",
        us=8,
    )(f, tops, level_set, from_right, from_left, got1, vx)
    theirs = lax.ppermute(mine, "focus", swap)
    level, velocity = call(
        middle_part,
        [(rows, cols), (rows, cols)],
        [SMEM] + [VMEM] * 6 + [HBM],
        [vmem(slabs - 1, middle, LANES), vmem(slabs, middle, LANES)]
        + work(mid)
        + [DMA((slabs + 1,))],
        "middle_part",
        us=20,
        out_specs=[HBM, HBM],
        aliases={7: 1},
        mib=20,
    )(f, tops, v_mid, got_early, got_near, ls_mid, mine, velocity)
    level, velocity = call(
        insert,
        [(rows, cols), (rows, cols)],
        [SMEM, VMEM, VMEM, HBM, HBM],
        [DMA((2,))],
        "insert",
        out_specs=[HBM, HBM],
        aliases={3: 0, 4: 1},
    )(f, theirs, got_far, level, velocity)
    return level, velocity


def solution(mesh):
    in_specs = (P("gx", "gy"), P("focus", "gx", "gy"), P("focus"))
    out_specs = (P("gx", "gy"), P("gx", "gy"))
    return jax.shard_map(
        per_device, mesh=mesh, in_specs=in_specs, out_specs=out_specs, check_vma=False
    )
```

```python
import jax
import jax.numpy as jnp
from jax import lax
from jax.experimental import pallas as pl
from jax.experimental.pallas import tpu as pltpu
from jax.sharding import PartitionSpec as P

EXT_SWEEPS = 8
REINIT_ITERS = 10
band_cells = 3.0
cfl_number = 0.5
pseudo_step = 0.5

HALO = 24
SIDE = 20
SPARE = 4
EDGE = 12
STAGED = 16
OWN_PARTS = (33, 128)
FIRST_PARTS = (27, 35)
EARLY = 208
LANES = 128
TINY = 1e-18

VMEM = pl.BlockSpec(memory_space=pltpu.VMEM)
SMEM = pl.BlockSpec(memory_space=pltpu.SMEM)
HBM = pl.BlockSpec(memory_space=pl.ANY)
DMA = pltpu.SemaphoreType.DMA


def vmem(*shape):
    return pltpu.VMEM(shape, jnp.float32)


def call(body, out_shapes, in_specs, scratch=(), name=None, out_specs=None, aliases=None, mib=16, us=1):
    out_specs = out_specs or [VMEM] * len(out_shapes)
    outs = [
        pltpu.HBM(s, jnp.float32) if spec is HBM else jax.ShapeDtypeStruct(s, jnp.float32)
        for s, spec in zip(out_shapes, out_specs)
    ]
    kernel = pl.pallas_call(
        body,
        out_shape=outs,
        in_specs=in_specs,
        out_specs=out_specs,
        scratch_shapes=list(scratch),
        name=name,
        input_output_aliases=aliases or {},
        compiler_params=pltpu.CompilerParams(vmem_limit_bytes=mib << 20),
        cost_estimate=pl.CostEstimate(flops=int(us * 1e9), bytes_accessed=0, transcendentals=0),
    )

    def run(*args):
        return kernel(
            *(pltpu.with_memory_space_constraint(x, pltpu.HBM) if spec is HBM else x for x, spec in zip(args, in_specs))
        )

    return run


def aligned(x, n=8):
    return pl.multiple_of(x, n)


def lanes_of(c):
    return slice(c * LANES, (c + 1) * LANES)


def shares(count, parts):
    ends = [count * i // parts for i in range(parts + 1)]
    return [(a, b - a) for a, b in zip(ends, ends[1:])]


def swept(ext):
    return (ext - 2 * SPARE) // 8


def blank(nat, f, main):
    for c in range(nat.shape[0]):
        nat[c, pl.ds(aligned(f * main), HALO), :] = jnp.zeros((HALO, LANES), jnp.float32)


def send_part(f_ref, w_hbm, g_ref, send_ref, buf, nat, w_ref, sems):
    n, main, cols = send_ref.shape[0], buf.shape[1], buf.shape[2]
    f = f_ref[0]
    start = (1 - f) * (g_ref.shape[1] - main)
    chunks = sems.shape[0] - 1
    weights = pltpu.make_async_copy(w_hbm, w_ref, sems.at[chunks])
    weights.start()
    step = main // 8 // chunks * 8
    spans = [(i * step, step if i < chunks - 1 else main - i * step) for i in range(chunks)]
    copies = [
        pltpu.make_async_copy(
            g_ref.at[:, pl.ds(aligned(start + at), n), :], buf.at[:, pl.ds(at, n), :], sems.at[i]
        )
        for i, (at, n) in enumerate(spans)
    ]
    for copy in copies:
        copy.start()
    blank(nat, 1 - f, main)
    weights.wait()
    for copy, (at, rows) in zip(copies, spans):
        copy.wait()
        part = w_ref[0] * buf[0, at : at + rows, :] + w_ref[1] * buf[1, at : at + rows, :]
        put(nat, pl.ds(aligned(f * HALO + at), rows), part)
    for k in range(n):
        send_ref[k] = spread(nat, swept(nat.shape[1]), SPARE + k, cols)


def send_rest(main, f_ref, p_ref, _, send_ref, nat):
    rows, cols = p_ref.shape
    f = f_ref[0]
    r = swept(nat.shape[1])
    blank(nat, 1 - f, main)
    put(nat, pl.ds(aligned(f * HALO), main), p_ref[pl.ds(aligned((1 - f) * (rows - main)), main), :])
    for k in range(send_ref.shape[0]):
        send_ref[k] = spread(nat, r, SPARE + r - send_ref.shape[0] + k, cols)


def strips(w_hbm, g_ref, ls_ref, p_ref, left_ref, right_ref, buf, w_ref, sems):
    rows, cols = ls_ref.shape
    chunks = sems.shape[0] - 1
    n = rows // chunks
    weights = pltpu.make_async_copy(w_hbm, w_ref, sems.at[chunks])
    weights.start()
    copies = [
        pltpu.make_async_copy(g_ref.at[:, pl.ds(i * n, n), :], buf.at[:, pl.ds(i * n, n), :], sems.at[i])
        for i in range(chunks)
    ]
    for copy in copies:
        copy.start()
    weights.wait()
    lane = lax.broadcasted_iota(jnp.int32, (LANES, LANES), 1)
    for i in range(rows // LANES):
        at = lanes_of(i)
        if i * LANES % n == 0:
            copies[i * LANES // n].wait()
        p_ref[at, :] = w_ref[0] * buf[0, at, :] + w_ref[1] * buf[1, at, :]
        first, last = slice(0, LANES), slice(cols - LANES, cols)
        packed = p_ref[at, first]
        for j, (ref, of) in enumerate(((ls_ref, first), (p_ref, last), (ls_ref, last)), 1):
            held = 0 if of.start == 0 else LANES - SIDE
            moved = pltpu.roll(ref[at, of], (j * SIDE - held) % LANES, 1)
            packed = jnp.where(lane < j * SIDE, packed, moved)
        turned_ = packed.T
        left_ref[:, at] = turned_[0 : 2 * SIDE, :]
        right_ref[:, at] = turned_[2 * SIDE : 4 * SIDE, :]


def turned(right, left):
    gap = jnp.zeros((LANES - 2 * SIDE, right.shape[1]), jnp.float32)
    return jnp.concatenate([right, gap, left], axis=0).T


def row_messages(f_ref, right_ref, left_ref, p_ref, ls_ref, fs_ref, m1_ref, m2_ref):
    rows, cols = ls_ref.shape
    f = f_ref[0]
    width = fs_ref.shape[1]
    theirs = pl.ds(aligned((1 - f) * (rows - width), LANES), width)
    fs_ref[0:SIDE, :] = right_ref[0:SIDE, theirs]
    fs_ref[SIDE:, :] = left_ref[0:SIDE, theirs]

    def corner(of, bottom):
        at = pl.ds(aligned(bottom * (rows - LANES), LANES), LANES)
        return turned(right_ref[of, at], left_ref[of, at])

    def ends(block, bottom):
        return jnp.where(bottom == 1, block[LANES - HALO :, :], block[0:HALO, :])

    outer, inner = 1 - f, f
    p_cols, ls_cols = slice(0, SIDE), slice(SIDE, 2 * SIDE)
    p_part, ls_part = slice(0, HALO), slice(HALO, 2 * HALO)
    at_outer = pl.ds(aligned(outer * (rows - HALO)), HALO)
    at_inner = pl.ds(aligned(inner * (rows - HALO)), HALO)
    m1_ref[p_part, 0:cols] = p_ref[at_outer, :]
    m1_ref[p_part, cols:] = ends(corner(p_cols, outer), outer)
    m1_ref[ls_part, 0:cols] = ls_ref[at_outer, :]
    m1_ref[ls_part, cols:] = ends(corner(ls_cols, outer), outer)
    m2_ref[:, 0:cols] = p_ref[at_inner, :]
    m2_ref[:, cols:] = ends(corner(p_cols, inner), inner)


def spread(nat, r, lo, width):
    return jnp.concatenate(
        [nat[c, pl.ds(lo, 8, stride=r), :] for c in range(width // LANES)], axis=1
    )


def unspread(nat, r, lo, value):
    for c in range(value.shape[1] // LANES):
        nat[c, pl.ds(lo, 8, stride=r), :] = value[:, lanes_of(c)]


def put(nat, rows, value, first=0):
    for c in range(value.shape[1] // LANES):
        nat[first + c, rows, :] = value[:, lanes_of(c)]


def half_setup(
    f_ref, p_ref, ls_ref, right_ref, left_ref, m1_ref, m2_ref, fs_ref,
    t_ref, q_ref, rec_ref, nat, lsx, pcol, lscol,
):
    rows, cols = ls_ref.shape
    f = f_ref[0]
    ext = lsx.shape[1]
    main = ext - HALO
    first = aligned((1 - f) * HALO)
    beside = pl.ds(aligned(f * main), HALO)
    put(nat, beside, m1_ref[0:HALO, :] + m2_ref[...])
    put(lsx, beside, m1_ref[HALO:, :])
    width = fs_ref.shape[1]
    skip = f * (width - main)
    lane0 = f * (rows - width)
    for i in range(width // LANES):
        at = pl.ds(aligned(lane0 + i * LANES, LANES), LANES)
        to = lanes_of(i)
        pcol[to, :] = turned(
            right_ref[0:SIDE, at] + fs_ref[0:SIDE, to], left_ref[0:SIDE, at] + fs_ref[SIDE:, to]
        )
        lscol[to, :] = turned(right_ref[SIDE:, at], left_ref[SIDE:, at])
    start = f * (rows - main)
    last = cols // LANES
    for i in range(main // 8):
        to = pl.ds(aligned(first + i * 8), 8)
        of = pl.ds(aligned(start + i * 8), 8)
        side = pl.ds(aligned(skip + i * 8), 8)
        put(nat, to, p_ref[of, :])
        put(lsx, to, ls_ref[of, :])
        nat[last, to, :] = pcol[side, :]
        lsx[last, to, :] = lscol[side, :]

    r = swept(ext)
    for k in range(r):
        x = spread(lsx, r, SPARE + k, cols + LANES) * (1.0 / band_cells)
        u = x * x
        q = 1.0 / (5.0 + 4.0 * u)
        q_ref[k] = q
        rec_ref[k] = (1.0 + u) * q
        t_ref[k] = spread(nat, r, SPARE + k, cols + LANES)


def wrap(ref, r):
    ref[0] = pltpu.roll(ref[r], 1, 0)
    ref[r + 1] = pltpu.roll(ref[1], 7, 0)


def sweep(src, r, body, first=0):
    up, centre = src[first], src[first + 1]
    for k in range(first, r):
        down = src[k + 2]
        body(k, up, centre, down)
        up, centre = centre, down


def relaxed(a_ref, rec_ref, width):
    def relax(k, up, centre, down):
        beside = (up + down) + (pltpu.roll(centre, 1, 1) + pltpu.roll(centre, width - 1, 1))
        return a_ref[k] + rec_ref[k] * beside

    return relax


def add_part(t, part):
    cols = part.shape[1]
    return jnp.concatenate([t[:, 0:cols] + part, t[:, cols:]], axis=1)


def velocity_begun(t_ref, rp1_ref, q_ref, rec_ref, v0, v1, a_ref):
    n = rp1_ref.shape[0]
    for k in range(n):
        source = add_part(t_ref[k], rp1_ref[k])
        v0[k + 1] = source
        a_ref[k] = source * q_ref[k]
    relax = relaxed(a_ref, rec_ref, t_ref.shape[2])
    for level in range(1, EXT_SWEEPS + 1):
        src, dst = (v0, v1) if level % 2 else (v1, v0)

        def body(k, *cells):
            dst[k + 1] = relax(k, *cells)

        sweep(src, n - level, body, level)


def velocity_ended(
    f_ref, t_ref, rp1_ref, rp2_ref, q_ref, rec_ref, b0_ref, b1_ref, vs_hbm, early_ref, near_ref, top_ref,
    nat, a_ref, v0, v1, vs_ref, sems,
):
    begun, _, cols = rp1_ref.shape
    r, _, width = t_ref.shape
    ext = nat.shape[1]
    f = f_ref[0]
    groups = shares(r, sems.shape[0])
    copies = [
        pltpu.make_async_copy(vs_ref.at[pl.ds(at, n)], vs_hbm.at[pl.ds(at, n)], sems.at[i])
        for i, (at, n) in enumerate(groups)
    ]
    sub = lax.broadcasted_iota(jnp.int32, (8, cols), 0)
    tops = [jnp.zeros((8, cols), jnp.float32)] * 2
    done = set()

    def final(k, value):
        vs_ref[k] = value
        unspread(nat, r, SPARE + k, value)
        done.add(k)
        for i, (at, n) in enumerate(groups):
            if at <= k < at + n and all(j in done for j in range(at, at + n)):
                copies[i].start()
        size = jnp.abs(value[:, 0:cols])
        row = sub * r + (SPARE + k)
        if SPARE + k < HALO or SPARE + 7 * r + k >= ext - HALO:
            size = jnp.where((row >= HALO) & (row < ext - HALO), size, 0.0)
        tops[k % 2] = jnp.maximum(tops[k % 2], size)

    edge = EXT_SWEEPS + 1
    for k in (*range(edge), *range(begun - edge, begun)):
        v0[k + 1] = b0_ref[k + 1]
        v1[k + 1] = b1_ref[k + 1]
    for k in (*range(EXT_SWEEPS), *range(begun - EXT_SWEEPS, r)):
        source = add_part(t_ref[k], rp1_ref[k] if k < begun else rp2_ref[k - begun])
        a_ref[k] = source * q_ref[k]
        if k >= begun:
            v0[k + 1] = source
    assert EXT_SWEEPS % 2 == 0
    for k in range(EXT_SWEEPS, begun - EXT_SWEEPS):
        final(k, b0_ref[k + 1])
    wrap(v0, r)
    relax = relaxed(a_ref, rec_ref, width)
    for level in range(1, EXT_SWEEPS + 1):
        src, dst = (v0, v1) if level % 2 else (v1, v0)

        def body(k, *cells):
            value = relax(k, *cells)
            if level == EXT_SWEEPS:
                final(k, value)
            else:
                dst[k + 1] = value

        sweep(src, r, body, begun - level)
        sweep(src, level, body)
        if level < EXT_SWEEPS:
            wrap(dst, r)
    near = near_ref.shape[0] - 2 * SIDE
    half = ext - 2 * HALO
    early = early_ref.shape[0]
    at_early = pl.ds(aligned(HALO + (1 - f) * (half - early)), early)
    at_near = pl.ds(aligned(HALO + (1 - f) * (half - early - near) + f * early), near)
    for c in range(cols // LANES):
        early_ref[:, lanes_of(c)] = nat[c, at_early, :]
        near_ref[0:near, lanes_of(c)] = nat[c, at_near, :]
    for i in range(half // LANES):
        side = nat[cols // LANES, HALO + i * LANES : HALO + (i + 1) * LANES, :].T
        near_ref[near : near + SIDE, lanes_of(i)] = side[0:SIDE, :]
        near_ref[near + SIDE :, lanes_of(i)] = side[LANES - SIDE :, :]
    top_ref[...] = jnp.full(top_ref.shape, jnp.max(jnp.maximum(*tops)), jnp.float32)
    for copy in copies:
        copy.wait()


def velocity_rows(f_ref, vs_hbm, early_ref, vx_hbm, far_hbm, vel_hbm, vs_ref, nat, sems):
    slabs, ext, _ = nat.shape
    last = slabs - 1
    r = vs_ref.shape[0]
    used = iter(range(sems.shape[0]))

    def begin(src, dst):
        copy = pltpu.make_async_copy(src, dst, sems.at[next(used)])
        copy.start()
        return copy

    groups = shares(r, 3)
    loads = [begin(vs_hbm.at[pl.ds(at, n)], vs_ref.at[pl.ds(at, n)]) for at, n in groups]
    for load, (at, n) in zip(loads, groups):
        load.wait()
        for k in range(at, at + n):
            unspread(nat, r, SPARE + k, vs_ref[k])
    far = far_hbm.shape[0]
    half = ext - 2 * HALO
    f = f_ref[0]
    at_far = pl.ds(aligned(HALO + f * (half - far)), far)
    lanes = [pl.ds(c * LANES, LANES) for c in range(last)]
    copies = [begin(nat.at[c, at_far, :], far_hbm.at[:, lanes[c]]) for c in range(last)]
    copies.append(begin(nat, vx_hbm))
    early = early_ref.shape[0]
    theirs = vel_hbm.at[pl.ds(aligned((1 - f) * half + f * (half - early)), early), :]
    copies.append(begin(early_ref, theirs))
    for c in range(last):
        mine = vel_hbm.at[pl.ds(aligned(f * half), half), lanes[c]]
        copies.append(begin(nat.at[c, pl.ds(HALO, half), :], mine))
    for copy in copies:
        copy.wait()


def speeds(sigma, above, below, before, after):
    a = jnp.maximum(sigma * above, TINY)
    b = jnp.minimum(sigma * below, 0.0)
    c = jnp.maximum(sigma * before, 0.0)
    d = jnp.minimum(sigma * after, 0.0)
    return (a * a + b * b) + (c * c + d * d)


def differences(src, r, width, body):
    centre = src[1]
    above = centre - src[0]
    for k in range(r):
        down = src[k + 2]
        below = down - centre
        before = centre - pltpu.roll(centre, 1, 1)
        after = pltpu.roll(centre, width - 1, 1) - centre
        body(k, centre, above, below, before, after)
        centre, above = down, below


def reinit(top_ref, ls_nat, v_nat, base, r, out_nat, shift, p0, p1, h_ref, s_ref, width, coming=(), later=()):
    step = cfl_number / (jnp.max(top_ref[...]) + 1e-06)
    for k in range(r):
        p0[k + 1] = spread(ls_nat, r, base + k, width)
    wrap(p0, r)
    for copy in coming:
        copy.wait()
    for copy in later:
        copy.start()

    def advance(k, centre, *steps):
        speed = spread(v_nat, r, base + k, width)
        sigma = jnp.where(speed >= 0.0, 1.0, -1.0)
        total = speeds(sigma, *steps)
        advanced = centre - step * (speed * (total * lax.rsqrt(total)))
        p1[k + 1] = advanced
        h_ref[k] = pseudo_step * (advanced * lax.rsqrt(advanced * advanced + 1.0))
        s_ref[k] = jnp.where(advanced >= 0.0, 1.0, -1.0)

    differences(p0, r, width, advance)
    wrap(p1, r)

    def one(src, dst):
        def body(k, centre, *steps):
            total = speeds(s_ref[k], *steps)
            h = h_ref[k]
            dst[k + 1] = (centre + h) - h * (total * lax.rsqrt(total))

        differences(src, r, width, body)
        wrap(dst, r)

    def pair(i, _):
        one(p1, p0)
        one(p0, p1)
        return 0

    assert REINIT_ITERS % 2 == 0
    lax.fori_loop(0, REINIT_ITERS // 2 - 1, pair, 0)
    one(p1, p0)
    cols = width - LANES

    def final(k, centre, *steps):
        total = speeds(s_ref[k][:, 0:cols], *(x[:, 0:cols] for x in steps))
        h = h_ref[k][:, 0:cols]
        unspread(out_nat, r, k + shift, (centre[:, 0:cols] + h) - h * (total * lax.rsqrt(total)))

    differences(p0, r, width, final)


def outer_part(
    f_ref, top_ref, ls_hbm, right_ref, left_ref, m1_ref, vx_hbm, out_ref, lsm_ref, vm_ref,
    nat, lsn, vn, lscol, p0, p1, h_ref, s_ref, sems,
):
    n, cols = out_ref.shape
    rows = ls_hbm.shape[0]
    f = f_ref[0]
    staged = lsn.shape[1]
    last = cols // LANES
    inside = n + HALO
    first = aligned((1 - f) * HALO)
    start = aligned(f * (rows - inside))
    copies = [
        pltpu.make_async_copy(
            ls_hbm.at[pl.ds(start, inside), pl.ds(c * LANES, LANES)], lsn.at[c, pl.ds(first, inside), :], sems.at[c]
        )
        for c in range(last)
    ]
    from_ext = aligned(f * (vx_hbm.shape[1] - staged))
    copies.append(pltpu.make_async_copy(vx_hbm.at[:, pl.ds(from_ext, staged), :], vn, sems.at[last]))
    for copy in copies:
        copy.start()
    middle, cut = lsm_ref.shape[1], vm_ref.shape[1]
    low = (rows - middle) // 2
    later = [
        pltpu.make_async_copy(
            ls_hbm.at[pl.ds(low, middle), pl.ds(c * LANES, LANES)], lsm_ref.at[c], sems.at[last + 1 + c]
        )
        for c in range(last)
    ]
    later.append(
        pltpu.make_async_copy(
            vx_hbm.at[:, pl.ds(aligned(HALO + (1 - f) * low), cut), :], vm_ref, sems.at[2 * last + 1]
        )
    )
    put(lsn, pl.ds(aligned(f * inside), HALO), m1_ref[HALO:, :])
    width = lscol.shape[0]
    for i in range(width // LANES):
        at = pl.ds(aligned(f * (rows - width) + i * LANES, LANES), LANES)
        lscol[lanes_of(i), :] = turned(right_ref[SIDE:, at], left_ref[SIDE:, at])
    lsn[last, pl.ds(first, inside), :] = lscol[pl.ds(aligned(f * (width - inside)), inside), :]
    for copy in copies[:last]:
        copy.wait()
    r = (n + 2 * EDGE) // 8
    reinit(
        top_ref, lsn, vn, HALO - EDGE, r, nat, STAGED - EDGE, p0, p1, h_ref, s_ref, cols + LANES,
        copies[last:], later,
    )
    for c in range(last):
        out_ref[:, lanes_of(c)] = nat[c, STAGED : STAGED + n, :]
    for i in range(rows // LANES):
        at = i * LANES
        first, end = max(at, low), min(at + LANES, low + middle)
        if first < end:
            block = turned(right_ref[SIDE:, at : at + LANES], left_ref[SIDE:, at : at + LANES])
            lsm_ref[last, first - low : end - low, :] = block[first - at : end - at, :]
    for copy in later:
        copy.wait()


def middle_part(
    f_ref, top_ref, vm_ref, early_ref, near_ref, lsn, mine_ref, _, level_ref, nat, vel_ref,
    vn, p0, p1, h_ref, s_ref, sems,
):
    rows, cols = level_ref.shape
    f = f_ref[0]
    staged = lsn.shape[1]
    n = staged - 2 * STAGED
    r = (n + 2 * EDGE) // 8
    low = (rows - staged) // 2
    last = cols // LANES
    half = rows // 2
    cut = half - low
    near = near_ref.shape[0] - 2 * SIDE
    early = early_ref.shape[0]
    own = mine_ref.shape[0]
    used = iter(range(sems.shape[0]))

    def begin(src, dst):
        copy = pltpu.make_async_copy(src, dst, sems.at[next(used)])
        copy.start()
        return copy

    ready = [
        begin(near_ref.at[pl.ds(0, near), :], vel_ref.at[pl.ds(aligned((1 - f) * (half + early) + f * low), near), :]),
        begin(mine_ref, level_ref.at[pl.ds(aligned(f * (rows - own)), own), :]),
    ]
    for c in range(last + 1):
        vn[c, pl.ds(aligned(f * cut), cut), :] = vm_ref[c]
    put(vn, pl.ds(aligned((1 - f) * cut + f * near), early), early_ref[...])
    put(vn, pl.ds(aligned((1 - f) * (cut + early)), near), near_ref[0:near, :])
    for i in range(half // LANES):
        at = i * LANES
        block = turned(near_ref[near : near + SIDE, at : at + LANES], near_ref[near + SIDE :, at : at + LANES])

        @pl.when(f == 0)
        def _():
            end = min(at + LANES, staged - cut)
            if at < end:
                vn[last, cut + at : cut + end, :] = block[0 : end - at, :]

        @pl.when(f == 1)
        def _():
            first = max(at, low)
            if first < at + LANES:
                vn[last, first - low : at + LANES - low, :] = block[first - at :, :]

    reinit(top_ref, lsn, vn, STAGED - EDGE, r, nat, STAGED - EDGE, p0, p1, h_ref, s_ref, cols + LANES)
    for copy in ready:
        copy.wait()


def insert(f_ref, theirs_ref, far_ref, middle_ref, _, __, level_ref, vel_ref, sems):
    rows = level_ref.shape[0]
    n, far = theirs_ref.shape[0], far_ref.shape[0]
    slabs = middle_ref.shape[0]
    f = f_ref[0]
    mid = rows - 2 * n
    copies = [
        pltpu.make_async_copy(
            middle_ref.at[c, pl.ds(STAGED, mid), :],
            level_ref.at[pl.ds(n, mid), pl.ds(c * LANES, LANES)],
            sems.at[c],
        )
        for c in range(slabs)
    ]
    copies += [
        pltpu.make_async_copy(
            theirs_ref, level_ref.at[pl.ds(aligned((1 - f) * (rows - n)), n), :], sems.at[slabs]
        ),
        pltpu.make_async_copy(
            far_ref, vel_ref.at[pl.ds(aligned((1 - f) * (rows - far)), far), :], sems.at[slabs + 1]
        ),
    ]
    for copy in copies:
        copy.start()
    for copy in copies:
        copy.wait()


def shifted(n, by):
    return [(i, (i + by) % n) for i in range(n)]


def per_device(level_set, focus_grads, focus_weight):
    rows, cols = level_set.shape
    half = rows // 2
    gx, gy = lax.axis_size("gx"), lax.axis_size("gy")
    f = lax.axis_index("focus").reshape(1).astype(jnp.int32)
    planes = focus_grads.shape[0]
    assert planes == 2 and lax.axis_size("focus") == 2
    swap = [(0, 1), (1, 0)]
    main, ext, wide = half + HALO, half + 2 * HALO, cols + LANES
    slabs = wide // LANES
    r = swept(ext)
    part = r * FIRST_PARTS[0] // FIRST_PARTS[1]
    weights = pltpu.SMEM(focus_weight.shape, jnp.float32)

    (to_partner,) = call(
        send_part,
        [(part, 8, cols)],
        [SMEM, HBM, HBM],
        [vmem(planes, main, cols), vmem(slabs - 1, ext, LANES), weights, DMA((9,))],
        "send_part",
    )(f, focus_weight, focus_grads)
    from_partner = lax.ppermute(to_partner, "focus", swap)

    p, left, right = call(
        strips,
        [(rows, cols), (2 * SIDE, rows), (2 * SIDE, rows)],
        [HBM, HBM, VMEM],
        [vmem(planes, rows, cols), weights, DMA((5,))],
        "strips",
        mib=16,
        us=2,
    )(focus_weight, focus_grads, level_set)
    from_right = lax.ppermute(left, "gy", shifted(gy, -1))
    from_left = lax.ppermute(right, "gy", shifted(gy, 1))
    side = -(-main // LANES) * LANES
    fs, m1, m2 = call(
        row_messages,
        [(2 * SIDE, side), (2 * HALO, wide), (HALO, wide)],
        [SMEM, VMEM, VMEM, VMEM, VMEM],
        (),
        "row_messages",
    )(f, from_right, from_left, p, level_set)

    def place(f, x):
        return f * gx + x % gx

    same = [(place(0, x), place(0, x + 1)) for x in range(gx)] + [(place(1, x), place(1, x - 1)) for x in range(gx)]
    cross = [(place(0, x), place(1, x - 1)) for x in range(gx)] + [(place(1, x), place(0, x + 1)) for x in range(gx)]
    got1 = lax.ppermute(m1, ("focus", "gx"), same)
    got2 = lax.ppermute(m2, ("focus", "gx"), cross)
    got_fs = lax.ppermute(fs, "focus", swap)
    (to_partner2,) = call(
        lambda *refs: send_rest(main, *refs),
        [(r - part, 8, cols)],
        [SMEM, VMEM, VMEM],
        [vmem(slabs - 1, ext, LANES)],
        "send_rest",
    )(f, p, got2)
    from_partner2 = lax.ppermute(to_partner2, "focus", swap)
    t, q, rec = call(
        half_setup,
        [(r, 8, wide)] * 3,
        [SMEM] + [VMEM] * 7,
        [vmem(slabs, ext, LANES), vmem(slabs, ext, LANES), vmem(side, LANES), vmem(side, LANES)],
        "half_setup",
        us=2,
        mib=20,
    )(f, p, level_set, from_right, from_left, got1, got2, got_fs)
    devices = 2 * gx * gy
    own = rows * OWN_PARTS[0] // OWN_PARTS[1]
    far = own - STAGED
    near = half - far - EARLY
    b0, b1 = call(
        velocity_begun,
        [(r + 2, 8, wide)] * 2,
        [VMEM] * 4,
        [vmem(part, 8, wide)],
        "velocity_begun",
        us=4,
    )(t, from_partner, q, rec)
    vs, to_early, to_near, top = call(
        velocity_ended,
        [(r, 8, wide), (EARLY, cols), (near + 2 * SIDE, cols), (devices, LANES)],
        [SMEM] + [VMEM] * 7,
        [
            vmem(slabs, ext, LANES), vmem(r, 8, wide), vmem(r + 2, 8, wide), vmem(r + 2, 8, wide),
            vmem(r, 8, wide), DMA((8,)),
        ],
        "velocity_ended",
        us=5,
        out_specs=[HBM, VMEM, VMEM, VMEM],
        mib=24,
    )(f, t, from_partner, from_partner2, q, rec, b0, b1)
    got_early = lax.ppermute(to_early, "focus", swap)
    tops = lax.all_to_all(top, ("focus", "gx", "gy"), 0, 0)
    got_near = lax.ppermute(to_near, "focus", swap)
    vx, to_far, velocity = call(
        velocity_rows,
        [(slabs, ext, LANES), (far, cols), (rows, cols)],
        [SMEM, HBM, VMEM],
        [vmem(r, 8, wide), vmem(slabs, ext, LANES), DMA((2 * slabs + 3,))],
        "velocity_rows",
        us=60,
        out_specs=[HBM, HBM, HBM],
    )(f, vs, got_early)
    got_far = lax.ppermute(to_far, "focus", swap)

    def work(n):
        r = (n + 2 * EDGE) // 8
        return [vmem(r + 2, 8, wide)] * 2 + [vmem(r, 8, wide)] * 2

    staged = own + 2 * HALO
    mid = rows - 2 * own
    middle = mid + 2 * STAGED
    mine, ls_mid, v_mid = call(
        outer_part,
        [(own, cols), (slabs, middle, LANES), (slabs, middle // 2, LANES)],
        [SMEM, VMEM, HBM, VMEM, VMEM, VMEM, HBM],
        [vmem(slabs - 1, own + 2 * STAGED, LANES), vmem(slabs, staged, LANES), vmem(slabs, staged, LANES)]
        + [vmem(-(-(own + HALO) // LANES) * LANES, LANES)]
        + work(own)
        + [DMA((2 * slabs,))],
        "outer_part",
        us=8,
    )(f, tops, level_set, from_right, from_left, got1, vx)
    theirs = lax.ppermute(mine, "focus", swap)
    level, middle_rows, velocity = call(
        middle_part,
        [(rows, cols), (slabs - 1, middle, LANES), (rows, cols)],
        [SMEM] + [VMEM] * 6 + [HBM],
        [vmem(slabs, middle, LANES)] + work(mid) + [DMA((2,))],
        "middle_part",
        us=20,
        out_specs=[HBM, VMEM, HBM],
        aliases={7: 2},
        mib=20,
    )(f, tops, v_mid, got_early, got_near, ls_mid, mine, velocity)
    level, velocity = call(
        insert,
        [(rows, cols), (rows, cols)],
        [SMEM, VMEM, VMEM, VMEM, HBM, HBM],
        [DMA((slabs + 1,))],
        "insert",
        out_specs=[HBM, HBM],
        aliases={4: 0, 5: 1},
    )(f, theirs, got_far, middle_rows, level, velocity)
    return level, velocity


def solution(mesh):
    in_specs = (P("gx", "gy"), P("focus", "gx", "gy"), P("focus"))
    out_specs = (P("gx", "gy"), P("gx", "gy"))
    return jax.shard_map(
        per_device, mesh=mesh, in_specs=in_specs, out_specs=out_specs, check_vma=False
    )
```

```python
import jax
import jax.numpy as jnp
from jax import lax
from jax.experimental import pallas as pl
from jax.experimental.pallas import tpu as pltpu
from jax.sharding import PartitionSpec as P

EXT_SWEEPS = 8
REINIT_ITERS = 10
band_cells = 3.0
cfl_number = 0.5
pseudo_step = 0.5

HALO = 24
SIDE = 20
SPARE = 4
EDGE = 12
STAGED = 16
OWN_PARTS = (1, 4)
FIRST_PARTS = (28, 35)
EARLY = 208
LANES = 128
TINY = 1e-18

VMEM = pl.BlockSpec(memory_space=pltpu.VMEM)
SMEM = pl.BlockSpec(memory_space=pltpu.SMEM)
HBM = pl.BlockSpec(memory_space=pl.ANY)
DMA = pltpu.SemaphoreType.DMA


def vmem(*shape):
    return pltpu.VMEM(shape, jnp.float32)


def call(body, out_shapes, in_specs, scratch=(), name=None, out_specs=None, aliases=None, mib=16, us=1):
    out_specs = out_specs or [VMEM] * len(out_shapes)
    outs = [
        pltpu.HBM(s, jnp.float32) if spec is HBM else jax.ShapeDtypeStruct(s, jnp.float32)
        for s, spec in zip(out_shapes, out_specs)
    ]
    kernel = pl.pallas_call(
        body,
        out_shape=outs,
        in_specs=in_specs,
        out_specs=out_specs,
        scratch_shapes=list(scratch),
        name=name,
        input_output_aliases=aliases or {},
        compiler_params=pltpu.CompilerParams(vmem_limit_bytes=mib << 20),
        cost_estimate=pl.CostEstimate(flops=int(us * 1e9), bytes_accessed=0, transcendentals=0),
    )

    def run(*args):
        return kernel(
            *(pltpu.with_memory_space_constraint(x, pltpu.HBM) if spec is HBM else x for x, spec in zip(args, in_specs))
        )

    return run


def aligned(x, n=8):
    return pl.multiple_of(x, n)


def lanes_of(c):
    return slice(c * LANES, (c + 1) * LANES)


def shares(count, parts):
    ends = [count * i // parts for i in range(parts + 1)]
    return [(a, b - a) for a, b in zip(ends, ends[1:])]


def swept(ext):
    return (ext - 2 * SPARE) // 8


def blank(nat, f, main):
    for c in range(nat.shape[0]):
        nat[c, pl.ds(aligned(f * main), HALO), :] = jnp.zeros((HALO, LANES), jnp.float32)


def send_part(f_ref, w_hbm, g_ref, send_ref, buf, nat, w_ref, sems):
    n, main, cols = send_ref.shape[0], buf.shape[1], buf.shape[2]
    f = f_ref[0]
    start = (1 - f) * (g_ref.shape[1] - main)
    chunks = sems.shape[0] - 1
    weights = pltpu.make_async_copy(w_hbm, w_ref, sems.at[chunks])
    weights.start()
    step = main // 8 // chunks * 8
    spans = [(i * step, step if i < chunks - 1 else main - i * step) for i in range(chunks)]
    copies = [
        pltpu.make_async_copy(
            g_ref.at[:, pl.ds(aligned(start + at), n), :], buf.at[:, pl.ds(at, n), :], sems.at[i]
        )
        for i, (at, n) in enumerate(spans)
    ]
    for copy in copies:
        copy.start()
    blank(nat, 1 - f, main)
    weights.wait()
    for copy, (at, rows) in zip(copies, spans):
        copy.wait()
        part = w_ref[0] * buf[0, at : at + rows, :] + w_ref[1] * buf[1, at : at + rows, :]
        put(nat, pl.ds(aligned(f * HALO + at), rows), part)
    for k in range(n):
        send_ref[k] = spread(nat, swept(nat.shape[1]), SPARE + k, cols)


def send_rest(main, f_ref, p_ref, _, send_ref, nat):
    rows, cols = p_ref.shape
    f = f_ref[0]
    r = swept(nat.shape[1])
    blank(nat, 1 - f, main)
    put(nat, pl.ds(aligned(f * HALO), main), p_ref[pl.ds(aligned((1 - f) * (rows - main)), main), :])
    for k in range(send_ref.shape[0]):
        send_ref[k] = spread(nat, r, SPARE + r - send_ref.shape[0] + k, cols)


def strips(w_hbm, g_ref, ls_ref, p_ref, left_ref, right_ref, buf, w_ref, sems):
    rows, cols = ls_ref.shape
    chunks = sems.shape[0] - 1
    n = rows // chunks
    weights = pltpu.make_async_copy(w_hbm, w_ref, sems.at[chunks])
    weights.start()
    copies = [
        pltpu.make_async_copy(g_ref.at[:, pl.ds(i * n, n), :], buf.at[:, pl.ds(i * n, n), :], sems.at[i])
        for i in range(chunks)
    ]
    for copy in copies:
        copy.start()
    weights.wait()
    lane = lax.broadcasted_iota(jnp.int32, (LANES, LANES), 1)
    for i in range(rows // LANES):
        at = lanes_of(i)
        if i * LANES % n == 0:
            copies[i * LANES // n].wait()
        p_ref[at, :] = w_ref[0] * buf[0, at, :] + w_ref[1] * buf[1, at, :]
        first, last = slice(0, LANES), slice(cols - LANES, cols)
        packed = p_ref[at, first]
        for j, (ref, of) in enumerate(((ls_ref, first), (p_ref, last), (ls_ref, last)), 1):
            held = 0 if of.start == 0 else LANES - SIDE
            moved = pltpu.roll(ref[at, of], (j * SIDE - held) % LANES, 1)
            packed = jnp.where(lane < j * SIDE, packed, moved)
        turned_ = packed.T
        left_ref[:, at] = turned_[0 : 2 * SIDE, :]
        right_ref[:, at] = turned_[2 * SIDE : 4 * SIDE, :]


def turned(right, left):
    gap = jnp.zeros((LANES - 2 * SIDE, right.shape[1]), jnp.float32)
    return jnp.concatenate([right, gap, left], axis=0).T


def row_messages(f_ref, right_ref, left_ref, p_ref, ls_ref, fs_ref, m1_ref, m2_ref):
    rows, cols = ls_ref.shape
    f = f_ref[0]
    width = fs_ref.shape[1]
    theirs = pl.ds(aligned((1 - f) * (rows - width), LANES), width)
    fs_ref[0:SIDE, :] = right_ref[0:SIDE, theirs]
    fs_ref[SIDE:, :] = left_ref[0:SIDE, theirs]

    def corner(of, bottom):
        at = pl.ds(aligned(bottom * (rows - LANES), LANES), LANES)
        return turned(right_ref[of, at], left_ref[of, at])

    def ends(block, bottom):
        return jnp.where(bottom == 1, block[LANES - HALO :, :], block[0:HALO, :])

    outer, inner = 1 - f, f
    p_cols, ls_cols = slice(0, SIDE), slice(SIDE, 2 * SIDE)
    p_part, ls_part = slice(0, HALO), slice(HALO, 2 * HALO)
    at_outer = pl.ds(aligned(outer * (rows - HALO)), HALO)
    at_inner = pl.ds(aligned(inner * (rows - HALO)), HALO)
    m1_ref[p_part, 0:cols] = p_ref[at_outer, :]
    m1_ref[p_part, cols:] = ends(corner(p_cols, outer), outer)
    m1_ref[ls_part, 0:cols] = ls_ref[at_outer, :]
    m1_ref[ls_part, cols:] = ends(corner(ls_cols, outer), outer)
    m2_ref[:, 0:cols] = p_ref[at_inner, :]
    m2_ref[:, cols:] = ends(corner(p_cols, inner), inner)


def spread(nat, r, lo, width):
    return jnp.concatenate(
        [nat[c, pl.ds(lo, 8, stride=r), :] for c in range(width // LANES)], axis=1
    )


def unspread(nat, r, lo, value):
    for c in range(value.shape[1] // LANES):
        nat[c, pl.ds(lo, 8, stride=r), :] = value[:, lanes_of(c)]


def put(nat, rows, value, first=0):
    for c in range(value.shape[1] // LANES):
        nat[first + c, rows, :] = value[:, lanes_of(c)]


def half_setup(
    f_ref, p_ref, ls_ref, right_ref, left_ref, m1_ref, m2_ref, fs_ref,
    t_ref, q_ref, rec_ref, nat, lsx, pcol, lscol,
):
    rows, cols = ls_ref.shape
    f = f_ref[0]
    ext = lsx.shape[1]
    main = ext - HALO
    first = aligned((1 - f) * HALO)
    beside = pl.ds(aligned(f * main), HALO)
    put(nat, beside, m1_ref[0:HALO, :] + m2_ref[...])
    put(lsx, beside, m1_ref[HALO:, :])
    width = fs_ref.shape[1]
    skip = f * (width - main)
    lane0 = f * (rows - width)
    for i in range(width // LANES):
        at = pl.ds(aligned(lane0 + i * LANES, LANES), LANES)
        to = lanes_of(i)
        pcol[to, :] = turned(
            right_ref[0:SIDE, at] + fs_ref[0:SIDE, to], left_ref[0:SIDE, at] + fs_ref[SIDE:, to]
        )
        lscol[to, :] = turned(right_ref[SIDE:, at], left_ref[SIDE:, at])
    start = f * (rows - main)
    last = cols // LANES
    for i in range(main // 8):
        to = pl.ds(aligned(first + i * 8), 8)
        of = pl.ds(aligned(start + i * 8), 8)
        side = pl.ds(aligned(skip + i * 8), 8)
        put(nat, to, p_ref[of, :])
        put(lsx, to, ls_ref[of, :])
        nat[last, to, :] = pcol[side, :]
        lsx[last, to, :] = lscol[side, :]

    r = swept(ext)
    for k in range(r):
        x = spread(lsx, r, SPARE + k, cols + LANES) * (1.0 / band_cells)
        u = x * x
        q = 1.0 / (5.0 + 4.0 * u)
        q_ref[k] = q
        rec_ref[k] = (1.0 + u) * q
        t_ref[k] = spread(nat, r, SPARE + k, cols + LANES)


def wrap(ref, r):
    ref[0] = pltpu.roll(ref[r], 1, 0)
    ref[r + 1] = pltpu.roll(ref[1], 7, 0)


def sweep(src, r, body, first=0):
    up, centre = src[first], src[first + 1]
    for k in range(first, r):
        down = src[k + 2]
        body(k, up, centre, down)
        up, centre = centre, down


def relaxed(a_ref, rec_ref, width):
    def relax(k, up, centre, down):
        beside = (up + down) + (pltpu.roll(centre, 1, 1) + pltpu.roll(centre, width - 1, 1))
        return a_ref[k] + rec_ref[k] * beside

    return relax


def add_part(t, part):
    cols = part.shape[1]
    return jnp.concatenate([t[:, 0:cols] + part, t[:, cols:]], axis=1)


def velocity_begun(t_ref, rp1_ref, q_ref, rec_ref, v0, v1, a_ref):
    n = rp1_ref.shape[0]
    for k in range(n):
        source = add_part(t_ref[k], rp1_ref[k])
        v0[k + 1] = source
        a_ref[k] = source * q_ref[k]
    relax = relaxed(a_ref, rec_ref, t_ref.shape[2])
    for level in range(1, EXT_SWEEPS + 1):
        src, dst = (v0, v1) if level % 2 else (v1, v0)

        def body(k, *cells):
            dst[k + 1] = relax(k, *cells)

        sweep(src, n - level, body, level)


def velocity_ended(
    f_ref, t_ref, rp1_ref, rp2_ref, q_ref, rec_ref, b0_ref, b1_ref, vs_hbm, early_ref, near_ref, top_ref,
    nat, a_ref, v0, v1, vs_ref, sems,
):
    begun, _, cols = rp1_ref.shape
    r, _, width = t_ref.shape
    ext = nat.shape[1]
    f = f_ref[0]
    groups = shares(r, sems.shape[0])
    copies = [
        pltpu.make_async_copy(vs_ref.at[pl.ds(at, n)], vs_hbm.at[pl.ds(at, n)], sems.at[i])
        for i, (at, n) in enumerate(groups)
    ]
    sub = lax.broadcasted_iota(jnp.int32, (8, cols), 0)
    tops = [jnp.zeros((8, cols), jnp.float32)] * 2
    done = set()

    def final(k, value):
        vs_ref[k] = value
        unspread(nat, r, SPARE + k, value)
        done.add(k)
        for i, (at, n) in enumerate(groups):
            if at <= k < at + n and all(j in done for j in range(at, at + n)):
                copies[i].start()
        size = jnp.abs(value[:, 0:cols])
        row = sub * r + (SPARE + k)
        if SPARE + k < HALO or SPARE + 7 * r + k >= ext - HALO:
            size = jnp.where((row >= HALO) & (row < ext - HALO), size, 0.0)
        tops[k % 2] = jnp.maximum(tops[k % 2], size)

    edge = EXT_SWEEPS + 1
    for k in (*range(edge), *range(begun - edge, begun)):
        v0[k + 1] = b0_ref[k + 1]
        v1[k + 1] = b1_ref[k + 1]
    for k in (*range(EXT_SWEEPS), *range(begun - EXT_SWEEPS, r)):
        source = add_part(t_ref[k], rp1_ref[k] if k < begun else rp2_ref[k - begun])
        a_ref[k] = source * q_ref[k]
        if k >= begun:
            v0[k + 1] = source
    assert EXT_SWEEPS % 2 == 0
    for k in range(EXT_SWEEPS, begun - EXT_SWEEPS):
        final(k, b0_ref[k + 1])
    wrap(v0, r)
    relax = relaxed(a_ref, rec_ref, width)
    for level in range(1, EXT_SWEEPS + 1):
        src, dst = (v0, v1) if level % 2 else (v1, v0)

        def body(k, *cells):
            value = relax(k, *cells)
            if level == EXT_SWEEPS:
                final(k, value)
            else:
                dst[k + 1] = value

        sweep(src, r, body, begun - level)
        sweep(src, level, body)
        if level < EXT_SWEEPS:
            wrap(dst, r)
    near = near_ref.shape[0] - 2 * SIDE
    half = ext - 2 * HALO
    early = early_ref.shape[0]
    at_early = pl.ds(aligned(HALO + (1 - f) * (half - early)), early)
    at_near = pl.ds(aligned(HALO + (1 - f) * (half - early - near) + f * early), near)
    for c in range(cols // LANES):
        early_ref[:, lanes_of(c)] = nat[c, at_early, :]
        near_ref[0:near, lanes_of(c)] = nat[c, at_near, :]
    for i in range(half // LANES):
        side = nat[cols // LANES, HALO + i * LANES : HALO + (i + 1) * LANES, :].T
        near_ref[near : near + SIDE, lanes_of(i)] = side[0:SIDE, :]
        near_ref[near + SIDE :, lanes_of(i)] = side[LANES - SIDE :, :]
    top_ref[...] = jnp.full(top_ref.shape, jnp.max(jnp.maximum(*tops)), jnp.float32)
    for copy in copies:
        copy.wait()


def velocity_rows(f_ref, vs_hbm, early_ref, vx_hbm, far_hbm, vel_hbm, vs_ref, nat, sems):
    slabs, ext, _ = nat.shape
    last = slabs - 1
    r = vs_ref.shape[0]
    used = iter(range(sems.shape[0]))

    def begin(src, dst):
        copy = pltpu.make_async_copy(src, dst, sems.at[next(used)])
        copy.start()
        return copy

    groups = shares(r, 3)
    loads = [begin(vs_hbm.at[pl.ds(at, n)], vs_ref.at[pl.ds(at, n)]) for at, n in groups]
    for load, (at, n) in zip(loads, groups):
        load.wait()
        for k in range(at, at + n):
            unspread(nat, r, SPARE + k, vs_ref[k])
    far = far_hbm.shape[0]
    half = ext - 2 * HALO
    f = f_ref[0]
    at_far = pl.ds(aligned(HALO + f * (half - far)), far)
    lanes = [pl.ds(c * LANES, LANES) for c in range(last)]
    copies = [begin(nat.at[c, at_far, :], far_hbm.at[:, lanes[c]]) for c in range(last)]
    copies += [begin(nat.at[c], vx_hbm.at[c]) for c in range(slabs)]
    early = early_ref.shape[0]
    theirs = vel_hbm.at[pl.ds(aligned((1 - f) * half + f * (half - early)), early), :]
    copies.append(begin(early_ref, theirs))
    for c in range(last):
        mine = vel_hbm.at[pl.ds(aligned(f * half), half), lanes[c]]
        copies.append(begin(nat.at[c, pl.ds(HALO, half), :], mine))
    for copy in copies:
        copy.wait()


def speeds(sigma, above, below, before, after):
    a = jnp.maximum(sigma * above, TINY)
    b = jnp.minimum(sigma * below, 0.0)
    c = jnp.maximum(sigma * before, 0.0)
    d = jnp.minimum(sigma * after, 0.0)
    return (a * a + b * b) + (c * c + d * d)


def differences(src, r, width, body):
    centre = src[1]
    above = centre - src[0]
    for k in range(r):
        down = src[k + 2]
        below = down - centre
        before = centre - pltpu.roll(centre, 1, 1)
        after = pltpu.roll(centre, width - 1, 1) - centre
        body(k, centre, above, below, before, after)
        centre, above = down, below


def reinit(top_ref, ls_nat, v_nat, base, r, out_nat, shift, p0, p1, h_ref, s_ref, width, coming=(), later=()):
    step = cfl_number / (jnp.max(top_ref[...]) + 1e-06)
    for k in range(r):
        p0[k + 1] = spread(ls_nat, r, base + k, width)
    wrap(p0, r)
    for copy in coming:
        copy.wait()
    for copy in later:
        copy.start()

    def advance(k, centre, *steps):
        speed = spread(v_nat, r, base + k, width)
        sigma = jnp.where(speed >= 0.0, 1.0, -1.0)
        total = speeds(sigma, *steps)
        advanced = centre - step * (speed * (total * lax.rsqrt(total)))
        p1[k + 1] = advanced
        h_ref[k] = pseudo_step * (advanced * lax.rsqrt(advanced * advanced + 1.0))
        s_ref[k] = jnp.where(advanced >= 0.0, 1.0, -1.0)

    differences(p0, r, width, advance)
    wrap(p1, r)

    def one(src, dst):
        def body(k, centre, *steps):
            total = speeds(s_ref[k], *steps)
            h = h_ref[k]
            dst[k + 1] = (centre + h) - h * (total * lax.rsqrt(total))

        differences(src, r, width, body)
        wrap(dst, r)

    def pair(i, _):
        one(p1, p0)
        one(p0, p1)
        return 0

    assert REINIT_ITERS % 2 == 0
    lax.fori_loop(0, REINIT_ITERS // 2 - 1, pair, 0)
    one(p1, p0)
    cols = width - LANES

    def final(k, centre, *steps):
        total = speeds(s_ref[k][:, 0:cols], *(x[:, 0:cols] for x in steps))
        h = h_ref[k][:, 0:cols]
        unspread(out_nat, r, k + shift, (centre[:, 0:cols] + h) - h * (total * lax.rsqrt(total)))

    differences(p0, r, width, final)


def outer_part(
    f_ref, top_ref, ls_hbm, right_ref, left_ref, m1_ref, vx_hbm, out_ref, lsm_ref, vm_ref,
    nat, lsn, vn, lscol, p0, p1, h_ref, s_ref, sems,
):
    n, cols = out_ref.shape
    rows = ls_hbm.shape[0]
    f = f_ref[0]
    staged = lsn.shape[1]
    last = cols // LANES
    inside = n + HALO
    first = aligned((1 - f) * HALO)
    start = aligned(f * (rows - inside))
    copies = [
        pltpu.make_async_copy(
            ls_hbm.at[pl.ds(start, inside), pl.ds(c * LANES, LANES)], lsn.at[c, pl.ds(first, inside), :], sems.at[c]
        )
        for c in range(last)
    ]
    from_ext = aligned(f * (vx_hbm.shape[1] - staged))
    copies += [
        pltpu.make_async_copy(vx_hbm.at[c, pl.ds(from_ext, staged), :], vn.at[c], sems.at[last + c])
        for c in range(last + 1)
    ]
    for copy in copies:
        copy.start()
    middle, cut = lsm_ref.shape[1], vm_ref.shape[1]
    low = (rows - middle) // 2
    later = [
        pltpu.make_async_copy(
            ls_hbm.at[pl.ds(low, middle), pl.ds(c * LANES, LANES)], lsm_ref.at[c], sems.at[2 * last + 1 + c]
        )
        for c in range(last)
    ]
    later.append(
        pltpu.make_async_copy(
            vx_hbm.at[:, pl.ds(aligned(HALO + (1 - f) * low), cut), :], vm_ref, sems.at[3 * last + 1]
        )
    )
    put(lsn, pl.ds(aligned(f * inside), HALO), m1_ref[HALO:, :])
    width = lscol.shape[0]
    for i in range(width // LANES):
        at = pl.ds(aligned(f * (rows - width) + i * LANES, LANES), LANES)
        lscol[lanes_of(i), :] = turned(right_ref[SIDE:, at], left_ref[SIDE:, at])
    lsn[last, pl.ds(first, inside), :] = lscol[pl.ds(aligned(f * (width - inside)), inside), :]
    for copy in copies[:last]:
        copy.wait()
    r = (n + 2 * EDGE) // 8
    reinit(
        top_ref, lsn, vn, HALO - EDGE, r, nat, STAGED - EDGE, p0, p1, h_ref, s_ref, cols + LANES,
        copies[last:], later,
    )
    for c in range(last):
        out_ref[:, lanes_of(c)] = nat[c, STAGED : STAGED + n, :]
    for i in range(rows // LANES):
        at = i * LANES
        first, end = max(at, low), min(at + LANES, low + middle)
        if first < end:
            block = turned(right_ref[SIDE:, at : at + LANES], left_ref[SIDE:, at : at + LANES])
            lsm_ref[last, first - low : end - low, :] = block[first - at : end - at, :]
    for copy in later:
        copy.wait()


def middle_part(
    f_ref, top_ref, vm_ref, early_ref, near_ref, lsn, mine_ref, _, level_ref, nat, vel_ref,
    vn, p0, p1, h_ref, s_ref, sems,
):
    rows, cols = level_ref.shape
    f = f_ref[0]
    staged = lsn.shape[1]
    n = staged - 2 * STAGED
    r = (n + 2 * EDGE) // 8
    low = (rows - staged) // 2
    last = cols // LANES
    half = rows // 2
    cut = half - low
    near = near_ref.shape[0] - 2 * SIDE
    early = early_ref.shape[0]
    own = mine_ref.shape[0]
    used = iter(range(sems.shape[0]))

    def begin(src, dst):
        copy = pltpu.make_async_copy(src, dst, sems.at[next(used)])
        copy.start()
        return copy

    ready = [
        begin(near_ref.at[pl.ds(0, near), :], vel_ref.at[pl.ds(aligned((1 - f) * (half + early) + f * low), near), :]),
        begin(mine_ref, level_ref.at[pl.ds(aligned(f * (rows - own)), own), :]),
    ]
    for c in range(last + 1):
        vn[c, pl.ds(aligned(f * cut), cut), :] = vm_ref[c]
    put(vn, pl.ds(aligned((1 - f) * cut + f * near), early), early_ref[...])
    put(vn, pl.ds(aligned((1 - f) * (cut + early)), near), near_ref[0:near, :])
    def block(at):
        return turned(near_ref[near : near + SIDE, at : at + LANES], near_ref[near + SIDE :, at : at + LANES])

    @pl.when(f == 0)
    def _():
        for at in range(0, staged - cut, LANES):
            end = min(at + LANES, staged - cut)
            vn[last, cut + at : cut + end, :] = block(at)[0 : end - at, :]

    @pl.when(f == 1)
    def _():
        for at in range(low // LANES * LANES, half, LANES):
            first = max(at, low)
            vn[last, first - low : at + LANES - low, :] = block(at)[first - at :, :]

    reinit(top_ref, lsn, vn, STAGED - EDGE, r, nat, STAGED - EDGE, p0, p1, h_ref, s_ref, cols + LANES)
    for copy in ready:
        copy.wait()


def insert(f_ref, theirs_ref, far_ref, middle_ref, _, __, level_ref, vel_ref, sems):
    rows = level_ref.shape[0]
    n, far = theirs_ref.shape[0], far_ref.shape[0]
    slabs = middle_ref.shape[0]
    f = f_ref[0]
    mid = rows - 2 * n
    copies = [
        pltpu.make_async_copy(
            middle_ref.at[c, pl.ds(STAGED, mid), :],
            level_ref.at[pl.ds(n, mid), pl.ds(c * LANES, LANES)],
            sems.at[c],
        )
        for c in range(slabs)
    ]
    pieces = [(theirs_ref, level_ref, at, count) for at, count in shares(n // 8, slabs)]
    pieces += [(far_ref, vel_ref, at, count) for at, count in shares(far // 8, slabs)]
    for i, (src, dst, at, count) in enumerate(pieces):
        first = aligned((1 - f) * (rows - src.shape[0]) + at * 8)
        copies.append(
            pltpu.make_async_copy(
                src.at[pl.ds(at * 8, count * 8), :], dst.at[pl.ds(first, count * 8), :], sems.at[slabs + i]
            )
        )
    for copy in copies:
        copy.start()
    for copy in copies:
        copy.wait()


def shifted(n, by):
    return [(i, (i + by) % n) for i in range(n)]


def per_device(level_set, focus_grads, focus_weight):
    rows, cols = level_set.shape
    half = rows // 2
    gx, gy = lax.axis_size("gx"), lax.axis_size("gy")
    f = lax.axis_index("focus").reshape(1).astype(jnp.int32)
    planes = focus_grads.shape[0]
    assert planes == 2 and lax.axis_size("focus") == 2
    swap = [(0, 1), (1, 0)]
    main, ext, wide = half + HALO, half + 2 * HALO, cols + LANES
    slabs = wide // LANES
    r = swept(ext)
    part = r * FIRST_PARTS[0] // FIRST_PARTS[1]
    weights = pltpu.SMEM(focus_weight.shape, jnp.float32)

    (to_partner,) = call(
        send_part,
        [(part, 8, cols)],
        [SMEM, HBM, HBM],
        [vmem(planes, main, cols), vmem(slabs - 1, ext, LANES), weights, DMA((9,))],
        "send_part",
    )(f, focus_weight, focus_grads)
    from_partner = lax.ppermute(to_partner, "focus", swap)

    p, left, right = call(
        strips,
        [(rows, cols), (2 * SIDE, rows), (2 * SIDE, rows)],
        [HBM, HBM, VMEM],
        [vmem(planes, rows, cols), weights, DMA((5,))],
        "strips",
        mib=16,
        us=2,
    )(focus_weight, focus_grads, level_set)
    from_right = lax.ppermute(left, "gy", shifted(gy, -1))
    from_left = lax.ppermute(right, "gy", shifted(gy, 1))
    side = -(-main // LANES) * LANES
    fs, m1, m2 = call(
        row_messages,
        [(2 * SIDE, side), (2 * HALO, wide), (HALO, wide)],
        [SMEM, VMEM, VMEM, VMEM, VMEM],
        (),
        "row_messages",
    )(f, from_right, from_left, p, level_set)

    def place(f, x):
        return f * gx + x % gx

    same = [(place(0, x), place(0, x + 1)) for x in range(gx)] + [(place(1, x), place(1, x - 1)) for x in range(gx)]
    cross = [(place(0, x), place(1, x - 1)) for x in range(gx)] + [(place(1, x), place(0, x + 1)) for x in range(gx)]
    got1 = lax.ppermute(m1, ("focus", "gx"), same)
    got2 = lax.ppermute(m2, ("focus", "gx"), cross)
    got_fs = lax.ppermute(fs, "focus", swap)
    (to_partner2,) = call(
        lambda *refs: send_rest(main, *refs),
        [(r - part, 8, cols)],
        [SMEM, VMEM, VMEM],
        [vmem(slabs - 1, ext, LANES)],
        "send_rest",
    )(f, p, got2)
    from_partner2 = lax.ppermute(to_partner2, "focus", swap)
    t, q, rec = call(
        half_setup,
        [(r, 8, wide)] * 3,
        [SMEM] + [VMEM] * 7,
        [vmem(slabs, ext, LANES), vmem(slabs, ext, LANES), vmem(side, LANES), vmem(side, LANES)],
        "half_setup",
        us=2,
        mib=20,
    )(f, p, level_set, from_right, from_left, got1, got2, got_fs)
    devices = 2 * gx * gy
    own = rows * OWN_PARTS[0] // OWN_PARTS[1]
    far = own - STAGED
    near = half - far - EARLY
    b0, b1 = call(
        velocity_begun,
        [(r + 2, 8, wide)] * 2,
        [VMEM] * 4,
        [vmem(part, 8, wide)],
        "velocity_begun",
        us=4,
    )(t, from_partner, q, rec)
    vs, to_early, to_near, top = call(
        velocity_ended,
        [(r, 8, wide), (EARLY, cols), (near + 2 * SIDE, cols), (devices, LANES)],
        [SMEM] + [VMEM] * 7,
        [
            vmem(slabs, ext, LANES), vmem(r, 8, wide), vmem(r + 2, 8, wide), vmem(r + 2, 8, wide),
            vmem(r, 8, wide), DMA((8,)),
        ],
        "velocity_ended",
        us=5,
        out_specs=[HBM, VMEM, VMEM, VMEM],
        mib=24,
    )(f, t, from_partner, from_partner2, q, rec, b0, b1)
    got_early = lax.ppermute(to_early, "focus", swap)
    tops = lax.all_to_all(top, ("focus", "gx", "gy"), 0, 0)
    got_near = lax.ppermute(to_near, "focus", swap)
    vx, to_far, velocity = call(
        velocity_rows,
        [(slabs, ext, LANES), (far, cols), (rows, cols)],
        [SMEM, HBM, VMEM],
        [vmem(r, 8, wide), vmem(slabs, ext, LANES), DMA((3 * slabs + 3,))],
        "velocity_rows",
        us=60,
        out_specs=[HBM, HBM, HBM],
    )(f, vs, got_early)
    got_far = lax.ppermute(to_far, "focus", swap)

    def work(n):
        r = (n + 2 * EDGE) // 8
        return [vmem(r + 2, 8, wide)] * 2 + [vmem(r, 8, wide)] * 2

    staged = own + 2 * HALO
    mid = rows - 2 * own
    middle = mid + 2 * STAGED
    mine, ls_mid, v_mid = call(
        outer_part,
        [(own, cols), (slabs, middle, LANES), (slabs, middle // 2, LANES)],
        [SMEM, VMEM, HBM, VMEM, VMEM, VMEM, HBM],
        [vmem(slabs - 1, own + 2 * STAGED, LANES), vmem(slabs, staged, LANES), vmem(slabs, staged, LANES)]
        + [vmem(-(-(own + HALO) // LANES) * LANES, LANES)]
        + work(own)
        + [DMA((3 * slabs,))],
        "outer_part",
        us=8,
    )(f, tops, level_set, from_right, from_left, got1, vx)
    theirs = lax.ppermute(mine, "focus", swap)
    level, middle_rows, velocity = call(
        middle_part,
        [(rows, cols), (slabs - 1, middle, LANES), (rows, cols)],
        [SMEM] + [VMEM] * 6 + [HBM],
        [vmem(slabs, middle, LANES)] + work(mid) + [DMA((2,))],
        "middle_part",
        us=20,
        out_specs=[HBM, VMEM, HBM],
        aliases={7: 2},
        mib=20,
    )(f, tops, v_mid, got_early, got_near, ls_mid, mine, velocity)
    level, velocity = call(
        insert,
        [(rows, cols), (rows, cols)],
        [SMEM, VMEM, VMEM, VMEM, HBM, HBM],
        [DMA((3 * (slabs - 1),))],
        "insert",
        out_specs=[HBM, HBM],
        aliases={4: 0, 5: 1},
    )(f, theirs, got_far, middle_rows, level, velocity)
    return level, velocity


def solution(mesh):
    in_specs = (P("gx", "gy"), P("focus", "gx", "gy"), P("focus"))
    out_specs = (P("gx", "gy"), P("gx", "gy"))
    return jax.shard_map(
        per_device, mesh=mesh, in_specs=in_specs, out_specs=out_specs, check_vma=False
    )
```

```python
import jax
import jax.numpy as jnp
from jax import lax
from jax.experimental import pallas as pl
from jax.experimental.pallas import tpu as pltpu
from jax.sharding import PartitionSpec as P

EXT_SWEEPS = 8
REINIT_ITERS = 10
band_cells = 3.0
cfl_number = 0.5
pseudo_step = 0.5

HALO = 24
SIDE = 20
SPARE = 4
EDGE = 12
STAGED = 16
OWN_PARTS = (1, 4)
FIRST_PARTS = (28, 35)
EARLY = 208
LANES = 128
TINY = 1e-18

VMEM = pl.BlockSpec(memory_space=pltpu.VMEM)
SMEM = pl.BlockSpec(memory_space=pltpu.SMEM)
HBM = pl.BlockSpec(memory_space=pl.ANY)
DMA = pltpu.SemaphoreType.DMA


def vmem(*shape):
    return pltpu.VMEM(shape, jnp.float32)


def call(body, out_shapes, in_specs, scratch=(), name=None, out_specs=None, aliases=None, mib=16, us=1):
    out_specs = out_specs or [VMEM] * len(out_shapes)
    outs = [
        pltpu.HBM(s, jnp.float32) if spec is HBM else jax.ShapeDtypeStruct(s, jnp.float32)
        for s, spec in zip(out_shapes, out_specs)
    ]
    kernel = pl.pallas_call(
        body,
        out_shape=outs,
        in_specs=in_specs,
        out_specs=out_specs,
        scratch_shapes=list(scratch),
        name=name,
        input_output_aliases=aliases or {},
        compiler_params=pltpu.CompilerParams(vmem_limit_bytes=mib << 20),
        cost_estimate=pl.CostEstimate(flops=int(us * 1e9), bytes_accessed=0, transcendentals=0),
    )

    def run(*args):
        return kernel(
            *(pltpu.with_memory_space_constraint(x, pltpu.HBM) if spec is HBM else x for x, spec in zip(args, in_specs))
        )

    return run


def aligned(x, n=8):
    return pl.multiple_of(x, n)


def lanes_of(c):
    return slice(c * LANES, (c + 1) * LANES)


def shares(count, parts):
    ends = [count * i // parts for i in range(parts + 1)]
    return [(a, b - a) for a, b in zip(ends, ends[1:])]


def swept(ext):
    return (ext - 2 * SPARE) // 8


def blank(nat, f, main):
    for c in range(nat.shape[0]):
        nat[c, pl.ds(aligned(f * main), HALO), :] = jnp.zeros((HALO, LANES), jnp.float32)


def send_part(f_ref, w_hbm, g_ref, send_ref, buf, nat, w_ref, sems):
    n, main, cols = send_ref.shape[0], buf.shape[1], buf.shape[2]
    f = f_ref[0]
    start = (1 - f) * (g_ref.shape[1] - main)
    chunks = sems.shape[0] - 1
    weights = pltpu.make_async_copy(w_hbm, w_ref, sems.at[chunks])
    weights.start()
    step = main // 8 // chunks * 8
    spans = [(i * step, step if i < chunks - 1 else main - i * step) for i in range(chunks)]
    copies = [
        pltpu.make_async_copy(
            g_ref.at[:, pl.ds(aligned(start + at), n), :], buf.at[:, pl.ds(at, n), :], sems.at[i]
        )
        for i, (at, n) in enumerate(spans)
    ]
    for copy in copies:
        copy.start()
    blank(nat, 1 - f, main)
    weights.wait()
    for copy, (at, rows) in zip(copies, spans):
        copy.wait()
        part = w_ref[0] * buf[0, at : at + rows, :] + w_ref[1] * buf[1, at : at + rows, :]
        put(nat, pl.ds(aligned(f * HALO + at), rows), part)
    for k in range(n):
        send_ref[k] = spread(nat, swept(nat.shape[1]), SPARE + k, cols)


def send_rest(main, f_ref, p_ref, _, send_ref, nat):
    rows, cols = p_ref.shape
    f = f_ref[0]
    r = swept(nat.shape[1])
    blank(nat, 1 - f, main)
    put(nat, pl.ds(aligned(f * HALO), main), p_ref[pl.ds(aligned((1 - f) * (rows - main)), main), :])
    for k in range(send_ref.shape[0]):
        send_ref[k] = spread(nat, r, SPARE + r - send_ref.shape[0] + k, cols)


def strips(w_hbm, g_ref, ls_ref, p_ref, left_ref, right_ref, buf, w_ref, sems):
    rows, cols = ls_ref.shape
    chunks = sems.shape[0] - 1
    n = rows // chunks
    weights = pltpu.make_async_copy(w_hbm, w_ref, sems.at[chunks])
    weights.start()
    copies = [
        pltpu.make_async_copy(g_ref.at[:, pl.ds(i * n, n), :], buf.at[:, pl.ds(i * n, n), :], sems.at[i])
        for i in range(chunks)
    ]
    for copy in copies:
        copy.start()
    weights.wait()
    lane = lax.broadcasted_iota(jnp.int32, (LANES, LANES), 1)
    for i in range(rows // LANES):
        at = lanes_of(i)
        if i * LANES % n == 0:
            copies[i * LANES // n].wait()
        p_ref[at, :] = w_ref[0] * buf[0, at, :] + w_ref[1] * buf[1, at, :]
        first, last = slice(0, LANES), slice(cols - LANES, cols)
        packed = p_ref[at, first]
        for j, (ref, of) in enumerate(((ls_ref, first), (p_ref, last), (ls_ref, last)), 1):
            held = 0 if of.start == 0 else LANES - SIDE
            moved = pltpu.roll(ref[at, of], (j * SIDE - held) % LANES, 1)
            packed = jnp.where(lane < j * SIDE, packed, moved)
        turned_ = packed.T
        left_ref[:, at] = turned_[0 : 2 * SIDE, :]
        right_ref[:, at] = turned_[2 * SIDE : 4 * SIDE, :]


def turned(right, left):
    gap = jnp.zeros((LANES - 2 * SIDE, right.shape[1]), jnp.float32)
    return jnp.concatenate([right, gap, left], axis=0).T


def row_messages(f_ref, right_ref, left_ref, p_ref, ls_ref, fs_ref, m1_ref, m2_ref):
    rows, cols = ls_ref.shape
    f = f_ref[0]
    width = fs_ref.shape[1]
    theirs = pl.ds(aligned((1 - f) * (rows - width), LANES), width)
    fs_ref[0:SIDE, :] = right_ref[0:SIDE, theirs]
    fs_ref[SIDE:, :] = left_ref[0:SIDE, theirs]

    def corner(of, bottom):
        at = pl.ds(aligned(bottom * (rows - LANES), LANES), LANES)
        return turned(right_ref[of, at], left_ref[of, at])

    def ends(block, bottom):
        return jnp.where(bottom == 1, block[LANES - HALO :, :], block[0:HALO, :])

    outer, inner = 1 - f, f
    p_cols, ls_cols = slice(0, SIDE), slice(SIDE, 2 * SIDE)
    p_part, ls_part = slice(0, HALO), slice(HALO, 2 * HALO)
    at_outer = pl.ds(aligned(outer * (rows - HALO)), HALO)
    at_inner = pl.ds(aligned(inner * (rows - HALO)), HALO)
    m1_ref[p_part, 0:cols] = p_ref[at_outer, :]
    m1_ref[p_part, cols:] = ends(corner(p_cols, outer), outer)
    m1_ref[ls_part, 0:cols] = ls_ref[at_outer, :]
    m1_ref[ls_part, cols:] = ends(corner(ls_cols, outer), outer)
    m2_ref[:, 0:cols] = p_ref[at_inner, :]
    m2_ref[:, cols:] = ends(corner(p_cols, inner), inner)


def spread(nat, r, lo, width):
    return jnp.concatenate(
        [nat[c, pl.ds(lo, 8, stride=r), :] for c in range(width // LANES)], axis=1
    )


def unspread(nat, r, lo, value):
    for c in range(value.shape[1] // LANES):
        nat[c, pl.ds(lo, 8, stride=r), :] = value[:, lanes_of(c)]


def put(nat, rows, value, first=0):
    for c in range(value.shape[1] // LANES):
        nat[first + c, rows, :] = value[:, lanes_of(c)]


def half_setup(
    f_ref, p_ref, ls_ref, right_ref, left_ref, m1_ref, m2_ref, fs_ref,
    t_ref, q_ref, rec_ref, nat, lsx, pcol, lscol,
):
    rows, cols = ls_ref.shape
    f = f_ref[0]
    ext = lsx.shape[1]
    main = ext - HALO
    first = aligned((1 - f) * HALO)
    beside = pl.ds(aligned(f * main), HALO)
    put(nat, beside, m1_ref[0:HALO, :] + m2_ref[...])
    put(lsx, beside, m1_ref[HALO:, :])
    width = fs_ref.shape[1]
    skip = f * (width - main)
    lane0 = f * (rows - width)
    for i in range(width // LANES):
        at = pl.ds(aligned(lane0 + i * LANES, LANES), LANES)
        to = lanes_of(i)
        pcol[to, :] = turned(
            right_ref[0:SIDE, at] + fs_ref[0:SIDE, to], left_ref[0:SIDE, at] + fs_ref[SIDE:, to]
        )
        lscol[to, :] = turned(right_ref[SIDE:, at], left_ref[SIDE:, at])
    start = f * (rows - main)
    last = cols // LANES
    for i in range(main // 8):
        to = pl.ds(aligned(first + i * 8), 8)
        of = pl.ds(aligned(start + i * 8), 8)
        side = pl.ds(aligned(skip + i * 8), 8)
        put(nat, to, p_ref[of, :])
        put(lsx, to, ls_ref[of, :])
        nat[last, to, :] = pcol[side, :]
        lsx[last, to, :] = lscol[side, :]

    r = swept(ext)
    for k in range(r):
        x = spread(lsx, r, SPARE + k, cols + LANES) * (1.0 / band_cells)
        u = x * x
        q = 1.0 / (5.0 + 4.0 * u)
        q_ref[k] = q
        rec_ref[k] = (1.0 + u) * q
        t_ref[k] = spread(nat, r, SPARE + k, cols + LANES)


def wrap(ref, r):
    ref[0] = pltpu.roll(ref[r], 1, 0)
    ref[r + 1] = pltpu.roll(ref[1], 7, 0)


def sweep(src, r, body, first=0):
    up, centre = src[first], src[first + 1]
    for k in range(first, r):
        down = src[k + 2]
        body(k, up, centre, down)
        up, centre = centre, down


def relaxed(a_ref, rec_ref, width):
    def relax(k, up, centre, down):
        beside = (up + down) + (pltpu.roll(centre, 1, 1) + pltpu.roll(centre, width - 1, 1))
        return a_ref[k] + rec_ref[k] * beside

    return relax


def add_part(t, part):
    cols = part.shape[1]
    return jnp.concatenate([t[:, 0:cols] + part, t[:, cols:]], axis=1)


def velocity_begun(t_ref, rp1_ref, q_ref, rec_ref, v0, v1, a_ref):
    n = rp1_ref.shape[0]
    for k in range(n):
        source = add_part(t_ref[k], rp1_ref[k])
        v0[k + 1] = source
        a_ref[k] = source * q_ref[k]
    relax = relaxed(a_ref, rec_ref, t_ref.shape[2])
    for level in range(1, EXT_SWEEPS + 1):
        src, dst = (v0, v1) if level % 2 else (v1, v0)

        def body(k, *cells):
            dst[k + 1] = relax(k, *cells)

        sweep(src, n - level, body, level)


def velocity_ended(
    f_ref, t_ref, rp1_ref, rp2_ref, q_ref, rec_ref, b0_ref, b1_ref, vs_hbm, early_ref, near_ref, top_ref,
    nat, a_ref, v0, v1, vs_ref, sems,
):
    begun, _, cols = rp1_ref.shape
    r, _, width = t_ref.shape
    ext = nat.shape[1]
    f = f_ref[0]
    groups = shares(r, sems.shape[0])
    copies = [
        pltpu.make_async_copy(vs_ref.at[pl.ds(at, n)], vs_hbm.at[pl.ds(at, n)], sems.at[i])
        for i, (at, n) in enumerate(groups)
    ]
    sub = lax.broadcasted_iota(jnp.int32, (8, cols), 0)
    tops = [jnp.zeros((8, cols), jnp.float32)] * 2
    done = set()

    def final(k, value):
        vs_ref[k] = value
        unspread(nat, r, SPARE + k, value)
        done.add(k)
        for i, (at, n) in enumerate(groups):
            if at <= k < at + n and all(j in done for j in range(at, at + n)):
                copies[i].start()
        size = jnp.abs(value[:, 0:cols])
        row = sub * r + (SPARE + k)
        if SPARE + k < HALO or SPARE + 7 * r + k >= ext - HALO:
            size = jnp.where((row >= HALO) & (row < ext - HALO), size, 0.0)
        tops[k % 2] = jnp.maximum(tops[k % 2], size)

    edge = EXT_SWEEPS + 1
    for k in (*range(edge), *range(begun - edge, begun)):
        v0[k + 1] = b0_ref[k + 1]
        v1[k + 1] = b1_ref[k + 1]
    for k in (*range(EXT_SWEEPS), *range(begun - EXT_SWEEPS, r)):
        source = add_part(t_ref[k], rp1_ref[k] if k < begun else rp2_ref[k - begun])
        a_ref[k] = source * q_ref[k]
        if k >= begun:
            v0[k + 1] = source
    assert EXT_SWEEPS % 2 == 0
    for k in range(EXT_SWEEPS, begun - EXT_SWEEPS):
        final(k, b0_ref[k + 1])
    wrap(v0, r)
    relax = relaxed(a_ref, rec_ref, width)
    for level in range(1, EXT_SWEEPS + 1):
        src, dst = (v0, v1) if level % 2 else (v1, v0)

        def body(k, *cells):
            value = relax(k, *cells)
            if level == EXT_SWEEPS:
                final(k, value)
            else:
                dst[k + 1] = value

        sweep(src, r, body, begun - level)
        sweep(src, level, body)
        if level < EXT_SWEEPS:
            wrap(dst, r)
    near = near_ref.shape[0] - 2 * SIDE
    half = ext - 2 * HALO
    early = early_ref.shape[0]
    at_early = pl.ds(aligned(HALO + (1 - f) * (half - early)), early)
    at_near = pl.ds(aligned(HALO + (1 - f) * (half - early - near) + f * early), near)
    for c in range(cols // LANES):
        early_ref[:, lanes_of(c)] = nat[c, at_early, :]
        near_ref[0:near, lanes_of(c)] = nat[c, at_near, :]
    for i in range(half // LANES):
        side = nat[cols // LANES, HALO + i * LANES : HALO + (i + 1) * LANES, :].T
        near_ref[near : near + SIDE, lanes_of(i)] = side[0:SIDE, :]
        near_ref[near + SIDE :, lanes_of(i)] = side[LANES - SIDE :, :]
    top_ref[...] = jnp.full(top_ref.shape, jnp.max(jnp.maximum(*tops)), jnp.float32)
    for copy in copies:
        copy.wait()


def velocity_rows(f_ref, vs_hbm, early_ref, vx_hbm, far_hbm, vel_hbm, vs_ref, nat, sems):
    slabs, ext, _ = nat.shape
    last = slabs - 1
    r = vs_ref.shape[0]
    used = iter(range(sems.shape[0]))

    def begin(src, dst):
        copy = pltpu.make_async_copy(src, dst, sems.at[next(used)])
        copy.start()
        return copy

    groups = shares(r, 6)
    loads = [begin(vs_hbm.at[pl.ds(at, n)], vs_ref.at[pl.ds(at, n)]) for at, n in groups]
    for load, (at, n) in zip(loads, groups):
        load.wait()
        for k in range(at, at + n):
            unspread(nat, r, SPARE + k, vs_ref[k])
    far = far_hbm.shape[0]
    half = ext - 2 * HALO
    f = f_ref[0]
    at_far = pl.ds(aligned(HALO + f * (half - far)), far)
    lanes = [pl.ds(c * LANES, LANES) for c in range(last)]
    copies = [begin(nat.at[c, at_far, :], far_hbm.at[:, lanes[c]]) for c in range(last)]
    copies += [begin(nat.at[c], vx_hbm.at[c]) for c in range(slabs)]
    early = early_ref.shape[0]
    theirs = vel_hbm.at[pl.ds(aligned((1 - f) * half + f * (half - early)), early), :]
    copies.append(begin(early_ref, theirs))
    for c in range(last):
        mine = vel_hbm.at[pl.ds(aligned(f * half), half), lanes[c]]
        copies.append(begin(nat.at[c, pl.ds(HALO, half), :], mine))
    for copy in copies:
        copy.wait()


def speeds(sigma, above, below, before, after):
    a = jnp.maximum(sigma * above, TINY)
    b = jnp.minimum(sigma * below, 0.0)
    c = jnp.maximum(sigma * before, 0.0)
    d = jnp.minimum(sigma * after, 0.0)
    return (a * a + b * b) + (c * c + d * d)


def differences(src, r, width, body):
    centre = src[1]
    above = centre - src[0]
    for k in range(r):
        down = src[k + 2]
        below = down - centre
        before = centre - pltpu.roll(centre, 1, 1)
        after = pltpu.roll(centre, width - 1, 1) - centre
        body(k, centre, above, below, before, after)
        centre, above = down, below


def reinit(top_ref, ls_nat, v_nat, base, r, out_nat, shift, p0, p1, h_ref, s_ref, width, coming=(), later=()):
    step = cfl_number / (jnp.max(top_ref[...]) + 1e-06)
    for k in range(r):
        p0[k + 1] = spread(ls_nat, r, base + k, width)
    wrap(p0, r)
    for copy in coming:
        copy.wait()
    for copy in later:
        copy.start()

    def advance(k, centre, *steps):
        speed = spread(v_nat, r, base + k, width)
        sigma = jnp.where(speed >= 0.0, 1.0, -1.0)
        total = speeds(sigma, *steps)
        advanced = centre - step * (speed * (total * lax.rsqrt(total)))
        p1[k + 1] = advanced
        h_ref[k] = pseudo_step * (advanced * lax.rsqrt(advanced * advanced + 1.0))
        s_ref[k] = jnp.where(advanced >= 0.0, 1.0, -1.0)

    differences(p0, r, width, advance)
    wrap(p1, r)

    def one(src, dst):
        def body(k, centre, *steps):
            total = speeds(s_ref[k], *steps)
            h = h_ref[k]
            dst[k + 1] = (centre + h) - h * (total * lax.rsqrt(total))

        differences(src, r, width, body)
        wrap(dst, r)

    def pair(i, _):
        one(p1, p0)
        one(p0, p1)
        return 0

    assert REINIT_ITERS % 2 == 0
    lax.fori_loop(0, REINIT_ITERS // 2 - 1, pair, 0)
    one(p1, p0)
    cols = width - LANES

    def final(k, centre, *steps):
        total = speeds(s_ref[k][:, 0:cols], *(x[:, 0:cols] for x in steps))
        h = h_ref[k][:, 0:cols]
        unspread(out_nat, r, k + shift, (centre[:, 0:cols] + h) - h * (total * lax.rsqrt(total)))

    differences(p0, r, width, final)


def outer_part(
    f_ref, top_ref, ls_hbm, right_ref, left_ref, m1_ref, vx_hbm, out_ref, lsm_ref, vm_ref,
    nat, lsn, vn, lscol, p0, p1, h_ref, s_ref, sems,
):
    n, cols = out_ref.shape
    rows = ls_hbm.shape[0]
    f = f_ref[0]
    staged = lsn.shape[1]
    last = cols // LANES
    inside = n + HALO
    first = aligned((1 - f) * HALO)
    start = aligned(f * (rows - inside))
    copies = [
        pltpu.make_async_copy(
            ls_hbm.at[pl.ds(start, inside), pl.ds(c * LANES, LANES)], lsn.at[c, pl.ds(first, inside), :], sems.at[c]
        )
        for c in range(last)
    ]
    from_ext = aligned(f * (vx_hbm.shape[1] - staged))
    copies += [
        pltpu.make_async_copy(vx_hbm.at[c, pl.ds(from_ext, staged), :], vn.at[c], sems.at[last + c])
        for c in range(last + 1)
    ]
    for copy in copies:
        copy.start()
    middle, cut = lsm_ref.shape[1], vm_ref.shape[1]
    low = (rows - middle) // 2
    later = [
        pltpu.make_async_copy(
            ls_hbm.at[pl.ds(low, middle), pl.ds(c * LANES, LANES)], lsm_ref.at[c], sems.at[2 * last + 1 + c]
        )
        for c in range(last)
    ]
    later.append(
        pltpu.make_async_copy(
            vx_hbm.at[:, pl.ds(aligned(HALO + (1 - f) * low), cut), :], vm_ref, sems.at[3 * last + 1]
        )
    )
    put(lsn, pl.ds(aligned(f * inside), HALO), m1_ref[HALO:, :])
    width = lscol.shape[0]
    for i in range(width // LANES):
        at = pl.ds(aligned(f * (rows - width) + i * LANES, LANES), LANES)
        lscol[lanes_of(i), :] = turned(right_ref[SIDE:, at], left_ref[SIDE:, at])
    lsn[last, pl.ds(first, inside), :] = lscol[pl.ds(aligned(f * (width - inside)), inside), :]
    for copy in copies[:last]:
        copy.wait()
    r = (n + 2 * EDGE) // 8
    reinit(
        top_ref, lsn, vn, HALO - EDGE, r, nat, STAGED - EDGE, p0, p1, h_ref, s_ref, cols + LANES,
        copies[last:], later,
    )
    for c in range(last):
        out_ref[:, lanes_of(c)] = nat[c, STAGED : STAGED + n, :]
    for i in range(rows // LANES):
        at = i * LANES
        first, end = max(at, low), min(at + LANES, low + middle)
        if first < end:
            block = turned(right_ref[SIDE:, at : at + LANES], left_ref[SIDE:, at : at + LANES])
            lsm_ref[last, first - low : end - low, :] = block[first - at : end - at, :]
    for copy in later:
        copy.wait()


def middle_part(
    f_ref, top_ref, vm_ref, early_ref, near_ref, lsn, mine_ref, _, level_ref, nat, vel_ref,
    vn, p0, p1, h_ref, s_ref, sems,
):
    rows, cols = level_ref.shape
    f = f_ref[0]
    staged = lsn.shape[1]
    n = staged - 2 * STAGED
    r = (n + 2 * EDGE) // 8
    low = (rows - staged) // 2
    last = cols // LANES
    half = rows // 2
    cut = half - low
    near = near_ref.shape[0] - 2 * SIDE
    early = early_ref.shape[0]
    own = mine_ref.shape[0]
    used = iter(range(sems.shape[0]))

    def begin(src, dst):
        copy = pltpu.make_async_copy(src, dst, sems.at[next(used)])
        copy.start()
        return copy

    ready = [
        begin(near_ref.at[pl.ds(0, near), :], vel_ref.at[pl.ds(aligned((1 - f) * (half + early) + f * low), near), :]),
        begin(mine_ref, level_ref.at[pl.ds(aligned(f * (rows - own)), own), :]),
    ]
    for c in range(last + 1):
        vn[c, pl.ds(aligned(f * cut), cut), :] = vm_ref[c]
    put(vn, pl.ds(aligned((1 - f) * cut + f * near), early), early_ref[...])
    put(vn, pl.ds(aligned((1 - f) * (cut + early)), near), near_ref[0:near, :])
    def block(at):
        return turned(near_ref[near : near + SIDE, at : at + LANES], near_ref[near + SIDE :, at : at + LANES])

    @pl.when(f == 0)
    def _():
        for at in range(0, staged - cut, LANES):
            end = min(at + LANES, staged - cut)
            vn[last, cut + at : cut + end, :] = block(at)[0 : end - at, :]

    @pl.when(f == 1)
    def _():
        for at in range(low // LANES * LANES, half, LANES):
            first = max(at, low)
            vn[last, first - low : at + LANES - low, :] = block(at)[first - at :, :]

    reinit(top_ref, lsn, vn, STAGED - EDGE, r, nat, STAGED - EDGE, p0, p1, h_ref, s_ref, cols + LANES)
    for copy in ready:
        copy.wait()


def insert(f_ref, theirs_ref, far_ref, middle_ref, _, __, level_ref, vel_ref, sems):
    rows = level_ref.shape[0]
    n, far = theirs_ref.shape[0], far_ref.shape[0]
    slabs = middle_ref.shape[0]
    f = f_ref[0]
    mid = rows - 2 * n
    copies = [
        pltpu.make_async_copy(
            middle_ref.at[c, pl.ds(STAGED, mid), :],
            level_ref.at[pl.ds(n, mid), pl.ds(c * LANES, LANES)],
            sems.at[c],
        )
        for c in range(slabs)
    ]
    pieces = [(theirs_ref, level_ref, at, count) for at, count in shares(n // 8, slabs)]
    pieces += [(far_ref, vel_ref, at, count) for at, count in shares(far // 8, slabs)]
    for i, (src, dst, at, count) in enumerate(pieces):
        first = aligned((1 - f) * (rows - src.shape[0]) + at * 8)
        copies.append(
            pltpu.make_async_copy(
                src.at[pl.ds(at * 8, count * 8), :], dst.at[pl.ds(first, count * 8), :], sems.at[slabs + i]
            )
        )
    for copy in copies:
        copy.start()
    for copy in copies:
        copy.wait()


def shifted(n, by):
    return [(i, (i + by) % n) for i in range(n)]


def per_device(level_set, focus_grads, focus_weight):
    rows, cols = level_set.shape
    half = rows // 2
    gx, gy = lax.axis_size("gx"), lax.axis_size("gy")
    f = lax.axis_index("focus").reshape(1).astype(jnp.int32)
    planes = focus_grads.shape[0]
    assert planes == 2 and lax.axis_size("focus") == 2
    swap = [(0, 1), (1, 0)]
    main, ext, wide = half + HALO, half + 2 * HALO, cols + LANES
    slabs = wide // LANES
    r = swept(ext)
    part = r * FIRST_PARTS[0] // FIRST_PARTS[1]
    weights = pltpu.SMEM(focus_weight.shape, jnp.float32)

    (to_partner,) = call(
        send_part,
        [(part, 8, cols)],
        [SMEM, HBM, HBM],
        [vmem(planes, main, cols), vmem(slabs - 1, ext, LANES), weights, DMA((9,))],
        "send_part",
    )(f, focus_weight, focus_grads)
    from_partner = lax.ppermute(to_partner, "focus", swap)

    p, left, right = call(
        strips,
        [(rows, cols), (2 * SIDE, rows), (2 * SIDE, rows)],
        [HBM, HBM, VMEM],
        [vmem(planes, rows, cols), weights, DMA((5,))],
        "strips",
        mib=16,
        us=2,
    )(focus_weight, focus_grads, level_set)
    from_right = lax.ppermute(left, "gy", shifted(gy, -1))
    from_left = lax.ppermute(right, "gy", shifted(gy, 1))
    side = -(-main // LANES) * LANES
    fs, m1, m2 = call(
        row_messages,
        [(2 * SIDE, side), (2 * HALO, wide), (HALO, wide)],
        [SMEM, VMEM, VMEM, VMEM, VMEM],
        (),
        "row_messages",
    )(f, from_right, from_left, p, level_set)

    def place(f, x):
        return f * gx + x % gx

    same = [(place(0, x), place(0, x + 1)) for x in range(gx)] + [(place(1, x), place(1, x - 1)) for x in range(gx)]
    cross = [(place(0, x), place(1, x - 1)) for x in range(gx)] + [(place(1, x), place(0, x + 1)) for x in range(gx)]
    got1 = lax.ppermute(m1, ("focus", "gx"), same)
    got2 = lax.ppermute(m2, ("focus", "gx"), cross)
    got_fs = lax.ppermute(fs, "focus", swap)
    (to_partner2,) = call(
        lambda *refs: send_rest(main, *refs),
        [(r - part, 8, cols)],
        [SMEM, VMEM, VMEM],
        [vmem(slabs - 1, ext, LANES)],
        "send_rest",
    )(f, p, got2)
    from_partner2 = lax.ppermute(to_partner2, "focus", swap)
    t, q, rec = call(
        half_setup,
        [(r, 8, wide)] * 3,
        [SMEM] + [VMEM] * 7,
        [vmem(slabs, ext, LANES), vmem(slabs, ext, LANES), vmem(side, LANES), vmem(side, LANES)],
        "half_setup",
        us=2,
        mib=20,
    )(f, p, level_set, from_right, from_left, got1, got2, got_fs)
    devices = 2 * gx * gy
    own = rows * OWN_PARTS[0] // OWN_PARTS[1]
    far = own - STAGED
    near = half - far - EARLY
    b0, b1 = call(
        velocity_begun,
        [(r + 2, 8, wide)] * 2,
        [VMEM] * 4,
        [vmem(part, 8, wide)],
        "velocity_begun",
        us=4,
    )(t, from_partner, q, rec)
    vs, to_early, to_near, top = call(
        velocity_ended,
        [(r, 8, wide), (EARLY, cols), (near + 2 * SIDE, cols), (devices, LANES)],
        [SMEM] + [VMEM] * 7,
        [
            vmem(slabs, ext, LANES), vmem(r, 8, wide), vmem(r + 2, 8, wide), vmem(r + 2, 8, wide),
            vmem(r, 8, wide), DMA((8,)),
        ],
        "velocity_ended",
        us=5,
        out_specs=[HBM, VMEM, VMEM, VMEM],
        mib=24,
    )(f, t, from_partner, from_partner2, q, rec, b0, b1)
    got_early = lax.ppermute(to_early, "focus", swap)
    tops = lax.all_to_all(top, ("focus", "gx", "gy"), 0, 0)
    got_near = lax.ppermute(to_near, "focus", swap)
    vx, to_far, velocity = call(
        velocity_rows,
        [(slabs, ext, LANES), (far, cols), (rows, cols)],
        [SMEM, HBM, VMEM],
        [vmem(r, 8, wide), vmem(slabs, ext, LANES), DMA((3 * slabs + 6,))],
        "velocity_rows",
        us=60,
        out_specs=[HBM, HBM, HBM],
    )(f, vs, got_early)
    got_far = lax.ppermute(to_far, "focus", swap)

    def work(n):
        r = (n + 2 * EDGE) // 8
        return [vmem(r + 2, 8, wide)] * 2 + [vmem(r, 8, wide)] * 2

    staged = own + 2 * HALO
    mid = rows - 2 * own
    middle = mid + 2 * STAGED
    mine, ls_mid, v_mid = call(
        outer_part,
        [(own, cols), (slabs, middle, LANES), (slabs, middle // 2, LANES)],
        [SMEM, VMEM, HBM, VMEM, VMEM, VMEM, HBM],
        [vmem(slabs - 1, own + 2 * STAGED, LANES), vmem(slabs, staged, LANES), vmem(slabs, staged, LANES)]
        + [vmem(-(-(own + HALO) // LANES) * LANES, LANES)]
        + work(own)
        + [DMA((3 * slabs,))],
        "outer_part",
        us=8,
    )(f, tops, level_set, from_right, from_left, got1, vx)
    theirs = lax.ppermute(mine, "focus", swap)
    level, middle_rows, velocity = call(
        middle_part,
        [(rows, cols), (slabs - 1, middle, LANES), (rows, cols)],
        [SMEM] + [VMEM] * 6 + [HBM],
        [vmem(slabs, middle, LANES)] + work(mid) + [DMA((2,))],
        "middle_part",
        us=20,
        out_specs=[HBM, VMEM, HBM],
        aliases={7: 2},
        mib=20,
    )(f, tops, v_mid, got_early, got_near, ls_mid, mine, velocity)
    level, velocity = call(
        insert,
        [(rows, cols), (rows, cols)],
        [SMEM, VMEM, VMEM, VMEM, HBM, HBM],
        [DMA((3 * (slabs - 1),))],
        "insert",
        out_specs=[HBM, HBM],
        aliases={4: 0, 5: 1},
    )(f, theirs, got_far, middle_rows, level, velocity)
    return level, velocity


def solution(mesh):
    in_specs = (P("gx", "gy"), P("focus", "gx", "gy"), P("focus"))
    out_specs = (P("gx", "gy"), P("gx", "gy"))
    return jax.shard_map(
        per_device, mesh=mesh, in_specs=in_specs, out_specs=out_specs, check_vma=False
    )
```
